32 devices in a mesh: groups: 2 (over y), expert: 4 (over z), mp: 4 (over x, core).
Axes of the slice: x: 2, y: 2, z: 4, core: 2. Of those that a mesh axis runs over, the one named last changes fastest.
Arguments:
- tokens: bfloat16 [1024, 3584], P(('groups', 'expert'), 'mp'), parts along dimension 0, may hold values from -6 to 6
- route_ids: int32 [1024, 8], P(('groups', 'expert')), parts along dimension 0, may hold values from 0 to 255, all different within a row
- route_weights: float32 [1024, 8], P(('groups', 'expert')), parts along dimension 0, may hold values from 0.2 to 1
- gate_weight: bfloat16 [4, 3584, 1024], P('expert', None, 'mp'), may hold values from -0.09375 to 0.09375
- gate_scale: float32 [4, 28, 8], P('expert', None, 'mp'), may hold values from 0.5 to 2
- up_weight: bfloat16 [4, 3584, 1024], P('expert', None, 'mp'), may hold values from -0.09375 to 0.09375
- up_scale: float32 [4, 28, 8], P('expert', None, 'mp'), may hold values from 0.5 to 2
- down_weight: bfloat16 [4, 1024, 3584], P('expert', 'mp'), may hold values from -0.1875 to 0.1875
- down_scale: float32 [4, 8, 28], P('expert', 'mp'), may hold values from 0.5 to 2
Outputs:
- mixed: bfloat16 [1024, 3584], P(('groups', 'expert'), 'mp'), parts along dimension 0
- hessian: float32 [8, 1024, 1024], P(('groups', 'expert'), 'mp'), parts along dimension 0
The draws below stay inside these ranges and needn't reach their ends.
There are 2 independent parts, one for each index of `groups`. The reference program is written for one: setup_inputs(seed, part) draws one part's arguments, and reference() takes and returns one part's arrays. A program takes and returns all parts, laid end to end along the dimension named above; an argument that names none is the same for every part. Nothing has to cross between parts.
Inputs may be any that keep to these rules, and one draw needn't show every extreme that they name: `route_ids`: each row names 8 different experts of 256, and every expert is named by some row.
All inputs are finite; a program needn't handle non-finite values.
Results may differ from the reference program's by a relative error of at most 0.011.
Values may be sent and summed in bfloat16 or wider, within the bound.
No kernel may reach another device: no remote copies, remote signals or barrier semaphores. Data moves between devices by JAX's collectives and lax.ppermute only.
A program may use at most 64 MiB of HBM per device.

```python
import math
import jax
import jax.numpy as jnp
from jax import lax

D = 3584
FF = 1024
ROUTED_ALL = 256
TOP = 8
QBLK = 128
TOK_DEV = 128
TOKENS = 512
EXPERTS = 4
CAP = 8
N_EXPERT = 4
N_MP = 4


def levels(key, dims, shards, smallest, largest):
    factor_of, own = 1.0, jax.random.fold_in(key, 6)
    for dim, parts in shards:
        heights = jnp.exp(jax.random.uniform(jax.random.fold_in(own, dim), (parts,), jnp.float32, smallest / len(shards), largest / len(shards)))
        factor_of = factor_of * jnp.repeat(heights, dims[dim] // parts).reshape([-1 if axis == dim else 1 for axis in range(len(dims))])
    return factor_of


def distinct(stream_key, rows, amount, top, lift):
    order = jax.random.permutation(jax.random.fold_in(stream_key, 1), amount)
    favour = order
    for power in range(3):
        favour = favour * favour // amount
    favour = favour * lift // amount
    lots = jax.random.randint(jax.random.fold_in(stream_key, 2), (rows, amount), 0, 4096) + favour
    sure = jax.random.permutation(jax.random.fold_in(stream_key, 3), rows)[jnp.arange(amount) % rows]
    lots = jnp.where(jnp.arange(rows)[:, None] == sure[None, :], 1 << 14, lots)
    merit = lots * amount + jnp.arange(amount)
    return lax.top_k(merit.astype(jnp.int32), top)[1].astype(jnp.int32)


def normal_values(stream_key, extent, deviation, bound, cuts=(), kind=jnp.bfloat16):
    array = deviation * jax.random.normal(stream_key, extent, jnp.float32)
    if cuts:
        array = array * levels(stream_key, extent, cuts, -0.22, 0.18)
    return jnp.clip(array, -bound, bound).astype(kind)


def setup_inputs(seed: int = 0, part: int = 0) -> dict:
    key_list = jax.random.split(jax.random.key(seed), 10)
    part_keys = jax.random.split(jax.random.fold_in(key_list[9], part), 10)
    return {
        "tokens": normal_values(part_keys[0], (TOKENS, D), 1.0, 6.0, ((0, 4), (1, 4))),
        "route_ids": distinct(part_keys[1], TOKENS, ROUTED_ALL, TOP, 256),
        "route_weights": jnp.clip(0.2 + 0.8 * jax.random.uniform(part_keys[2], (TOKENS, TOP), jnp.float32) ** levels(part_keys[2], (TOKENS, TOP), ((0, 4),), -0.2, 0.2), 0.2, 1.0),
        "gate_weight": normal_values(key_list[3], (EXPERTS, D, FF), D ** -0.5, 0.09375, ((0, 4), (2, 4))),
        "gate_scale": jnp.clip(jnp.exp(math.log(2.0) - 1.3862944 * jax.random.uniform(key_list[4], (EXPERTS, D // QBLK, FF // QBLK), jnp.float32) ** levels(key_list[4], (EXPERTS, D // QBLK, FF // QBLK), ((0, 4), (2, 4)), -0.2, 0.2)), 0.5, 2.0),
        "up_weight": normal_values(key_list[5], (EXPERTS, D, FF), D ** -0.5, 0.09375, ((0, 4), (2, 4))),
        "up_scale": jnp.clip(jnp.exp(math.log(2.0) - 1.3862944 * jax.random.uniform(key_list[6], (EXPERTS, D // QBLK, FF // QBLK), jnp.float32) ** levels(key_list[6], (EXPERTS, D // QBLK, FF // QBLK), ((0, 4), (2, 4)), -0.2, 0.2)), 0.5, 2.0),
        "down_weight": normal_values(key_list[7], (EXPERTS, FF, D), FF ** -0.5, 0.1875, ((0, 4), (1, 4))),
        "down_scale": jnp.clip(jnp.exp(math.log(2.0) - 1.3862944 * jax.random.uniform(key_list[8], (EXPERTS, FF // QBLK, D // QBLK), jnp.float32) ** levels(key_list[8], (EXPERTS, FF // QBLK, D // QBLK), ((0, 4), (1, 4)), -0.2, 0.2)), 0.5, 2.0),
    }


def dequant(weight, scale):
    spread = jnp.repeat(jnp.repeat(scale, QBLK, axis=0), QBLK, axis=1)
    return (weight.astype(jnp.float32) * spread).astype(jnp.bfloat16)


def route_slots(route_ids, experts, capacity):
    flat = route_ids.reshape(-1)
    onehot = (flat[:, None] == jnp.arange(experts, dtype=jnp.int32)[None, :]).astype(jnp.int32)
    position = jnp.sum((jnp.cumsum(onehot, axis=0) - 1) * onehot, axis=1)
    kept = (flat < experts) & (position < capacity)
    counts = jnp.minimum(jnp.sum(onehot, axis=0), capacity)
    targets = jnp.where(kept, flat * capacity + position, experts * capacity)
    return targets.reshape(route_ids.shape).astype(jnp.int32), counts.astype(jnp.int32)


def reference(tokens, route_ids, route_weights, gate_weight, gate_scale, up_weight, up_scale, down_weight, down_scale):
    blocks = route_ids.reshape(N_EXPERT, TOK_DEV, TOP)
    targets, counts = jax.vmap(lambda block: route_slots(block, EXPERTS, CAP))(blocks)
    row_total = jnp.sum(counts, axis=0)
    block_index = jnp.arange(N_EXPERT, dtype=jnp.int32)[:, None, None]
    slot_total = EXPERTS * N_EXPERT * CAP
    expert_of = targets // CAP
    position = targets % CAP
    global_slot = jnp.where(targets < EXPERTS * CAP, expert_of * (N_EXPERT * CAP) + block_index * CAP + position, slot_total)
    global_slot = global_slot.reshape(TOKENS, TOP).astype(jnp.int32)
    buffer = jnp.zeros((slot_total + 1, D), jnp.bfloat16)
    for route in range(TOP):
        buffer = buffer.at[global_slot[:, route]].set(tokens)
    rows = buffer[:slot_total].reshape(EXPERTS, N_EXPERT * CAP, D)
    group = FF // N_MP

    def one_expert(operands):
        inputs, gate_w, gate_s, up_w, up_s, down_w, down_s, total = operands
        gate_proj = jnp.dot(inputs, dequant(gate_w, gate_s), preferred_element_type=jnp.float32)
        up_proj = jnp.dot(inputs, dequant(up_w, up_s), preferred_element_type=jnp.float32)
        hidden = (jax.nn.silu(gate_proj) * up_proj).astype(jnp.bfloat16)
        hessian_block = jnp.dot(hidden.T, hidden, preferred_element_type=jnp.float32) * (2.0 / total.astype(jnp.float32))
        down_eff = dequant(down_w, down_s)
        partials = jnp.einsum("sgf,gfd->gsd", hidden.reshape(N_EXPERT * CAP, N_MP, group).astype(jnp.float32),
                              down_eff.reshape(N_MP, group, D).astype(jnp.float32))
        partials = lax.optimization_barrier(partials.astype(jnp.bfloat16))
        result = jnp.sum(partials.astype(jnp.float32), axis=0).astype(jnp.bfloat16)
        return hessian_block, result

    hessian, outputs = lax.map(one_expert, (rows, gate_weight, gate_scale, up_weight, up_scale, down_weight, down_scale, row_total))
    flat_out = jnp.concatenate([outputs.reshape(slot_total, D), jnp.zeros((1, D), jnp.bfloat16)], axis=0)
    mixed = jnp.zeros((TOKENS, D), jnp.float32)
    for route in range(TOP):
        mixed = mixed + route_weights[:, route:route + 1] * flat_out[global_slot[:, route]].astype(jnp.float32)
    return mixed.astype(jnp.bfloat16), hessian
```

```python
import functools

import jax
import jax.numpy as jnp
from jax import lax
from jax.experimental import pallas as pl
from jax.experimental.pallas import tpu as pltpu
from jax.sharding import PartitionSpec as P

ROUTED_ALL = 256
TOP = 8
QBLK = 128


def dequant(weight, scale):
    row_blocks, col_blocks = scale.shape
    blocks = (
        weight.astype(jnp.float32).reshape(row_blocks, QBLK, col_blocks, QBLK)
        * scale[:, None, :, None]
    )
    return blocks.astype(jnp.bfloat16).reshape(weight.shape)


def route_slots(route_ids, experts, capacity):
    flat = route_ids.reshape(-1)
    onehot = (flat[:, None] == jnp.arange(experts, dtype=jnp.int32)[None, :]).astype(jnp.int32)
    position = jnp.sum((jnp.cumsum(onehot, axis=0) - 1) * onehot, axis=1)
    kept = (flat < experts) & (position < capacity)
    counts = jnp.minimum(jnp.sum(onehot, axis=0), capacity)
    targets = jnp.where(kept, flat * capacity + position, experts * capacity)
    return (targets.reshape(route_ids.shape), counts)


def on_device_any_mesh(
    tokens,
    route_ids,
    route_weights,
    gate_weight,
    gate_scale,
    up_weight,
    up_scale,
    down_weight,
    down_scale,
):
    experts = lax.axis_size("expert")
    capacity = 2 * route_ids.shape[0] * route_ids.shape[1] // ROUTED_ALL
    slot_total = experts * capacity
    targets, counts = route_slots(route_ids, experts, capacity)
    count_column = counts[:, None]
    gate_eff = dequant(gate_weight[0], gate_scale[0])
    up_eff = dequant(up_weight[0], up_scale[0])
    down_eff = dequant(down_weight[0], down_scale[0])
    token_count = route_ids.shape[0]
    source_index = jnp.full((slot_total + 1,), token_count, jnp.int32)
    source_index = source_index.at[targets.reshape(-1)].set(
        jnp.repeat(jnp.arange(token_count, dtype=jnp.int32), TOP)
    )
    source_index = source_index[:slot_total]
    features = lax.all_gather(tokens, "mp", axis=1, tiled=True)
    padded = jnp.concatenate([features, jnp.zeros((1, features.shape[1]), jnp.bfloat16)], axis=0)
    arrived = lax.all_to_all(
        padded[source_index].reshape(experts, capacity, features.shape[1]),
        "expert",
        split_axis=0,
        concat_axis=0,
        tiled=True,
    )
    arrived_counts = lax.all_to_all(count_column, "expert", split_axis=0, concat_axis=0, tiled=True)
    inputs = arrived.reshape(slot_total, features.shape[1])
    gate_proj = jnp.dot(inputs, gate_eff, preferred_element_type=jnp.float32)
    up_proj = jnp.dot(inputs, up_eff, preferred_element_type=jnp.float32)
    hidden = (jax.nn.silu(gate_proj) * up_proj).astype(jnp.bfloat16)
    row_total = jnp.sum(arrived_counts).astype(jnp.float32)
    hessian_rows = lax.dot_general(
        hidden,
        lax.all_gather(hidden, "mp", axis=1, tiled=True),
        (((0,), (0,)), ((), ())),
        preferred_element_type=jnp.float32,
    ) * (2.0 / row_total)
    partial_value = jnp.dot(hidden, down_eff, preferred_element_type=jnp.float32)
    summed = lax.psum_scatter(
        partial_value.astype(jnp.bfloat16), "mp", scatter_dimension=1, tiled=True
    )
    returned = lax.all_to_all(
        summed.reshape(experts, capacity, summed.shape[1]),
        "expert",
        split_axis=0,
        concat_axis=0,
        tiled=True,
    )
    width = returned.shape[2]
    flat_back = jnp.concatenate(
        [returned.reshape(slot_total, width), jnp.zeros((1, width), jnp.bfloat16)], axis=0
    )
    mixed = jnp.zeros((tokens.shape[0], width), jnp.float32)
    for route in range(TOP):
        mixed = mixed + route_weights[:, route : route + 1] * flat_back[targets[:, route]].astype(
            jnp.float32
        )
    return (mixed.astype(jnp.bfloat16), hessian_rows[None])


BOTH = ("expert", "mp")
VMEM = pl.BlockSpec(memory_space=pltpu.VMEM)
SMEM = pl.BlockSpec(memory_space=pltpu.SMEM)
F32 = jnp.float32
BF16 = jnp.bfloat16


def swap_cores(value):
    return lax.ppermute(value, "mp", [(m, m ^ 1) for m in range(4)])


def to_chips(value, k):
    pairs = [(4 * z + m, 4 * (z ^ k) + (m ^ 2 * (m & 1))) for z in range(4) for m in range(4)]
    if k == 0:
        pairs = [(a, b) for a, b in pairs if a != b]
    return lax.ppermute(value, BOTH, pairs)


def across(value):
    return lax.ppermute(value, "mp", [(m, m ^ 2) for m in range(4)])


def route_kernel(capacity, ids_ref, weights_ref, tokens_ref, rows_ref, count_ref, coef_ref):
    z = lax.axis_index("expert")
    ids, weights = ids_ref[...], weights_ref[...]
    rows = ids.shape[1]
    live, weight = [], []
    for k in range(4):
        hit = ids == (z ^ k)
        live.append(jnp.sum(jnp.where(hit, 1.0, 0.0), axis=0, keepdims=True))
        weight.append(jnp.sum(jnp.where(hit, weights, 0.0), axis=0, keepdims=True))
    earlier = lax.broadcasted_iota(jnp.int32, (rows, rows), 0) < lax.broadcasted_iota(jnp.int32, (rows, rows), 1)
    position = jnp.dot(
        jnp.concatenate(live, axis=0).astype(BF16),
        jnp.where(earlier, 1.0, 0.0).astype(BF16),
        preferred_element_type=F32,
    )
    slot = lax.broadcasted_iota(jnp.int32, (capacity, rows), 0).astype(F32)
    chosen = []
    for k in range(4):
        kept = (live[k] > 0.5) & (position[k : k + 1] == slot)
        one = jnp.where(kept, 1.0, 0.0)
        chosen.append(one)
        coef_ref[capacity * k : capacity * (k + 1), :] = one * weight[k]
        total = jnp.minimum(jnp.sum(live[k], axis=1, keepdims=True), float(capacity))
        count_ref[k] = jnp.broadcast_to(total, count_ref.shape[1:]).astype(BF16)
    picked = jnp.dot(
        jnp.concatenate(chosen, axis=0).astype(BF16), tokens_ref[...], preferred_element_type=F32
    ).astype(BF16)
    rows_ref[...] = picked.reshape(rows_ref.shape)


def expert_kernel(
    arrived_ref,
    swapped_ref,
    gate_ref,
    gate_scale_ref,
    up_ref,
    up_scale_ref,
    down_ref,
    down_scale_ref,
    keep_ref,
    send_ref,
    hidden_ref,
    scaled_ref,
):
    m = lax.axis_index("mp")
    core = m % 2
    first = m ^ (2 * core)
    slots, width = scaled_ref.shape[0] // 4, scaled_ref.shape[1]
    blocks = width // QBLK
    half = gate_ref.shape[1] // 2
    gate = jnp.zeros((2 * slots, 2 * half), F32)
    up = jnp.zeros((2 * slots, 2 * half), F32)
    order = (first, first ^ 1, first ^ 3, first ^ 2)
    for quarter, share in enumerate(order):
        source = arrived_ref if quarter < 2 else swapped_ref
        for block in range(blocks):
            lanes = slice((quarter % 2) * width + block * QBLK, (quarter % 2) * width + (block + 1) * QBLK)
            x = source[:, :, lanes].reshape(slots, QBLK).astype(F32)
            at = share * blocks + block
            into = slice(block * QBLK, (block + 1) * QBLK)
            scaled_ref[0 * slots : 1 * slots, into] = (x * gate_scale_ref[0, at]).astype(BF16)
            scaled_ref[1 * slots : 2 * slots, into] = (x * gate_scale_ref[1, at]).astype(BF16)
            scaled_ref[2 * slots : 3 * slots, into] = (x * up_scale_ref[0, at]).astype(BF16)
            scaled_ref[3 * slots : 4 * slots, into] = (x * up_scale_ref[1, at]).astype(BF16)
        depth = pl.ds(pl.multiple_of(share * width, width), width)
        gate += jnp.dot(scaled_ref[: 2 * slots, :], gate_ref[depth, :], preferred_element_type=F32)
        up += jnp.dot(scaled_ref[2 * slots :, :], up_ref[depth, :], preferred_element_type=F32)
    parts = []
    for i in range(2):
        g = gate[i * slots : (i + 1) * slots, i * half : (i + 1) * half]
        u = up[i * slots : (i + 1) * slots, i * half : (i + 1) * half]
        parts.append((g / (1.0 + jnp.exp(-g)) * u).astype(BF16))
    hidden_ref[...] = jnp.concatenate(parts, axis=1)
    send_ref[:, 2 * width :] = hidden_ref[...]
    none = jnp.zeros_like(parts[0])
    stacked = jnp.concatenate(
        [jnp.concatenate([parts[0], none], axis=1), jnp.concatenate([none, parts[1]], axis=1)], axis=0
    )
    for out_ref, shares in ((send_ref, (first ^ 3, first ^ 2)), (keep_ref, (first, first ^ 1))):
        for part, share in enumerate(shares):
            for block in range(0, blocks, 7):
                size = min(7, blocks - block)
                lanes = pl.ds(pl.multiple_of(share * width + block * QBLK, QBLK), size * QBLK)
                both = jnp.dot(stacked, down_ref[:, lanes], preferred_element_type=F32)
                for i in range(size):
                    at = share * blocks + block + i
                    cut = slice(i * QBLK, (i + 1) * QBLK)
                    value = both[:slots, cut] * down_scale_ref[0, at] + both[slots:, cut] * down_scale_ref[1, at]
                    into = part * width + (block + i) * QBLK
                    out_ref[:, into : into + QBLK] = value.astype(BF16)


def hessian_kernel(arrived_ref, near_ref, far_ref, out_ref):
    m = lax.axis_index("mp")
    width = out_ref.shape[0]
    counts = arrived_ref[:, :, arrived_ref.shape[2] - QBLK :].astype(F32)
    factor = 2.0 / jnp.sum(counts[:, 0, :1], axis=0, keepdims=True)
    own = near_ref[:, :width]
    for share, ref, at in ((m, near_ref, 0), (m ^ 1, near_ref, 1), (m ^ 2, far_ref, 0), (m ^ 3, far_ref, 1)):
        other = ref[:, at * width : (at + 1) * width]
        block = lax.dot_general(own, other, (((0,), (0,)), ((), ())), preferred_element_type=F32)
        out_ref[:, pl.ds(pl.multiple_of(share * width, width), width)] = block * factor


def combine_kernel(coef_ref, near_ref, far_ref, out_ref):
    slots, width = coef_ref.shape[0], out_ref.shape[1]
    result = (near_ref[:, :width].astype(F32) + far_ref[...].astype(F32)).astype(BF16)
    coef = coef_ref[...]
    terms = []
    for _ in range(3):
        terms.append(coef.astype(BF16))
        coef = coef - terms[-1].astype(F32)
    out = lax.dot_general(
        jnp.concatenate(terms, axis=0),
        jnp.concatenate([result] * 3, axis=0),
        (((0,), (0,)), ((), ())),
        preferred_element_type=F32,
    )
    out_ref[...] = out.astype(BF16)


def on_device(
    tokens,
    route_ids,
    route_weights,
    gate_weight,
    gate_scale,
    up_weight,
    up_scale,
    down_weight,
    down_scale,
):
    rows, width = tokens.shape
    capacity = 2 * rows * TOP // ROUTED_ALL
    slots = 4 * capacity
    hidden_width = gate_weight.shape[2]
    shape = jax.ShapeDtypeStruct
    params = pltpu.CompilerParams(vmem_limit_bytes=24 * 1024 * 1024)
    on_core_one = lax.axis_index("mp") % 2 == 1

    picked, counts, coef = pl.pallas_call(
        functools.partial(route_kernel, capacity),
        out_shape=(
            shape((4, capacity, width), BF16),
            shape((4, capacity, QBLK), BF16),
            shape((slots, rows), F32),
        ),
        in_specs=[VMEM] * 3,
        out_specs=(VMEM,) * 3,
        compiler_params=params,
        name="route",
    )(route_ids.T, route_weights.T, tokens)

    message = jnp.concatenate([picked, swap_cores(picked), counts], axis=2)
    got = [to_chips(message[k], k) for k in range(4)]
    got[0] = jnp.where(on_core_one, got[0], message[0])
    arrived = jnp.stack(got)
    swapped = swap_cores(arrived[:, :, : 2 * width])

    keep, send, hidden = pl.pallas_call(
        expert_kernel,
        out_shape=(
            shape((slots, 2 * width), BF16),
            shape((slots, 2 * width + hidden_width), BF16),
            shape((slots, hidden_width), BF16),
        ),
        in_specs=[VMEM, VMEM, VMEM, SMEM, VMEM, SMEM, VMEM, SMEM],
        out_specs=(VMEM,) * 3,
        scratch_shapes=[pltpu.VMEM((4 * slots, width), BF16)],
        compiler_params=params,
        name="expert",
    )(
        arrived,
        swapped,
        gate_weight[0],
        gate_scale[0].T,
        up_weight[0],
        up_scale[0].T,
        down_weight[0],
        down_scale[0],
    )

    sent = swap_cores(send)
    summed = (keep.astype(F32) + sent[:, : 2 * width].astype(F32)).astype(BF16).reshape(4, capacity, 2 * width)
    near = jnp.concatenate([hidden, sent[:, 2 * width :]], axis=1)
    near_blocks = near.reshape(4, capacity, 2 * hidden_width)
    message = jnp.concatenate([summed[0]] + [near_blocks[k] for k in range(4)], axis=1)
    crossed = across(message)
    far = crossed[:, 2 * width :].reshape(capacity, 4, 2 * hidden_width).swapaxes(0, 1).reshape(slots, 2 * hidden_width)
    back = [jnp.where(on_core_one, crossed[:, : 2 * width], summed[0])]
    back += [to_chips(summed[k], k) for k in range(1, 4)]
    back = jnp.concatenate(back, axis=0)

    hessian = pl.pallas_call(
        hessian_kernel,
        out_shape=shape((hidden_width, 4 * hidden_width), F32),
        in_specs=[VMEM] * 3,
        out_specs=VMEM,
        compiler_params=params,
        name="hessian",
    )(arrived, near, far)

    mixed = pl.pallas_call(
        combine_kernel,
        out_shape=shape((rows, width), BF16),
        in_specs=[VMEM] * 3,
        out_specs=VMEM,
        compiler_params=params,
        name="combine",
    )(coef, back, swap_cores(back[:, width:]))
    return mixed, hessian[None]


def solution(mesh):
    placed = (
        P(("groups", "expert"), "mp"),
        P(("groups", "expert"), None),
        P(("groups", "expert"), None),
        P("expert", None, "mp"),
        P("expert", None, "mp"),
        P("expert", None, "mp"),
        P("expert", None, "mp"),
        P("expert", "mp", None),
        P("expert", "mp", None),
    )
    two_level = mesh.shape["expert"] == 4 and mesh.shape["mp"] == 4
    return jax.shard_map(
        on_device if two_level else on_device_any_mesh,
        mesh=mesh,
        in_specs=placed,
        out_specs=(P(("groups", "expert"), "mp"), P(("groups", "expert"), "mp", None)),
        check_vma=False,
    )
```

```python
import functools

import jax
import jax.numpy as jnp
from jax import lax
from jax.experimental import pallas as pl
from jax.experimental.pallas import tpu as pltpu
from jax.sharding import PartitionSpec as P

ROUTED_ALL = 256
TOP = 8
QBLK = 128


def dequant(weight, scale):
    row_blocks, col_blocks = scale.shape
    blocks = (
        weight.astype(jnp.float32).reshape(row_blocks, QBLK, col_blocks, QBLK)
        * scale[:, None, :, None]
    )
    return blocks.astype(jnp.bfloat16).reshape(weight.shape)


def route_slots(route_ids, experts, capacity):
    flat = route_ids.reshape(-1)
    onehot = (flat[:, None] == jnp.arange(experts, dtype=jnp.int32)[None, :]).astype(jnp.int32)
    position = jnp.sum((jnp.cumsum(onehot, axis=0) - 1) * onehot, axis=1)
    kept = (flat < experts) & (position < capacity)
    counts = jnp.minimum(jnp.sum(onehot, axis=0), capacity)
    targets = jnp.where(kept, flat * capacity + position, experts * capacity)
    return (targets.reshape(route_ids.shape), counts)


def on_device_any_mesh(
    tokens,
    route_ids,
    route_weights,
    gate_weight,
    gate_scale,
    up_weight,
    up_scale,
    down_weight,
    down_scale,
):
    experts = lax.axis_size("expert")
    capacity = 2 * route_ids.shape[0] * route_ids.shape[1] // ROUTED_ALL
    slot_total = experts * capacity
    targets, counts = route_slots(route_ids, experts, capacity)
    count_column = counts[:, None]
    gate_eff = dequant(gate_weight[0], gate_scale[0])
    up_eff = dequant(up_weight[0], up_scale[0])
    down_eff = dequant(down_weight[0], down_scale[0])
    token_count = route_ids.shape[0]
    source_index = jnp.full((slot_total + 1,), token_count, jnp.int32)
    source_index = source_index.at[targets.reshape(-1)].set(
        jnp.repeat(jnp.arange(token_count, dtype=jnp.int32), TOP)
    )
    source_index = source_index[:slot_total]
    features = lax.all_gather(tokens, "mp", axis=1, tiled=True)
    padded = jnp.concatenate([features, jnp.zeros((1, features.shape[1]), jnp.bfloat16)], axis=0)
    arrived = lax.all_to_all(
        padded[source_index].reshape(experts, capacity, features.shape[1]),
        "expert",
        split_axis=0,
        concat_axis=0,
        tiled=True,
    )
    arrived_counts = lax.all_to_all(count_column, "expert", split_axis=0, concat_axis=0, tiled=True)
    inputs = arrived.reshape(slot_total, features.shape[1])
    gate_proj = jnp.dot(inputs, gate_eff, preferred_element_type=jnp.float32)
    up_proj = jnp.dot(inputs, up_eff, preferred_element_type=jnp.float32)
    hidden = (jax.nn.silu(gate_proj) * up_proj).astype(jnp.bfloat16)
    row_total = jnp.sum(arrived_counts).astype(jnp.float32)
    hessian_rows = lax.dot_general(
        hidden,
        lax.all_gather(hidden, "mp", axis=1, tiled=True),
        (((0,), (0,)), ((), ())),
        preferred_element_type=jnp.float32,
    ) * (2.0 / row_total)
    partial_value = jnp.dot(hidden, down_eff, preferred_element_type=jnp.float32)
    summed = lax.psum_scatter(
        partial_value.astype(jnp.bfloat16), "mp", scatter_dimension=1, tiled=True
    )
    returned = lax.all_to_all(
        summed.reshape(experts, capacity, summed.shape[1]),
        "expert",
        split_axis=0,
        concat_axis=0,
        tiled=True,
    )
    width = returned.shape[2]
    flat_back = jnp.concatenate(
        [returned.reshape(slot_total, width), jnp.zeros((1, width), jnp.bfloat16)], axis=0
    )
    mixed = jnp.zeros((tokens.shape[0], width), jnp.float32)
    for route in range(TOP):
        mixed = mixed + route_weights[:, route : route + 1] * flat_back[targets[:, route]].astype(
            jnp.float32
        )
    return (mixed.astype(jnp.bfloat16), hessian_rows[None])


BOTH = ("expert", "mp")
VMEM = pl.BlockSpec(memory_space=pltpu.VMEM)
SMEM = pl.BlockSpec(memory_space=pltpu.SMEM)
F32 = jnp.float32
BF16 = jnp.bfloat16


def swap_cores(value):
    return lax.ppermute(value, "mp", [(m, m ^ 1) for m in range(4)])


def to_chips(value, k):
    pairs = [(4 * z + m, 4 * (z ^ k) + (m ^ 2 * (m & 1))) for z in range(4) for m in range(4)]
    if k == 0:
        pairs = [(a, b) for a, b in pairs if a != b]
    return lax.ppermute(value, BOTH, pairs)


def across(value):
    return lax.ppermute(value, BOTH, [(4 * z + m, 4 * z + (m ^ 2)) for z in range(4) for m in range(4)])


def earlier_kernel(out_ref):
    row, column = (lax.broadcasted_iota(jnp.int32, out_ref.shape, i) for i in range(2))
    out_ref[...] = jnp.where(row < column, 1.0, 0.0).astype(BF16)


def route_kernel(capacity, earlier_ref, ids_ref, weights_ref, tokens_ref, rows_ref, count_ref, coef_ref):
    z = lax.axis_index("expert")
    ids, weights = ids_ref[...], weights_ref[...]
    rows = ids.shape[1]
    live, weight = [], []
    for k in range(4):
        hit = ids == (z ^ k)
        live.append(jnp.sum(jnp.where(hit, 1.0, 0.0), axis=0, keepdims=True))
        weight.append(jnp.sum(jnp.where(hit, weights, 0.0), axis=0, keepdims=True))
    position = jnp.dot(
        jnp.concatenate(live, axis=0).astype(BF16),
        earlier_ref[...],
        preferred_element_type=F32,
    )
    slot = lax.broadcasted_iota(jnp.int32, (capacity, rows), 0).astype(F32)
    chosen = []
    for k in range(4):
        kept = (live[k] > 0.5) & (position[k : k + 1] == slot)
        one = jnp.where(kept, 1.0, 0.0)
        chosen.append(one)
        coef_ref[capacity * k : capacity * (k + 1), :] = one * weight[k]
        total = jnp.minimum(jnp.sum(live[k], axis=1, keepdims=True), float(capacity))
        count_ref[k] = jnp.broadcast_to(total, count_ref.shape[1:]).astype(BF16)
    picked = jnp.dot(
        jnp.concatenate(chosen, axis=0).astype(BF16), tokens_ref[...], preferred_element_type=F32
    ).astype(BF16)
    rows_ref[...] = picked.reshape(rows_ref.shape)


def expert_kernel(
    arrived_ref,
    swapped_ref,
    gate_ref,
    gate_scale_ref,
    up_ref,
    up_scale_ref,
    down_ref,
    down_scale_ref,
    keep_ref,
    send_ref,
    hidden_ref,
    scaled_ref,
):
    m = lax.axis_index("mp")
    core = m % 2
    first = m ^ (2 * core)
    slots, width = scaled_ref.shape[0] // 4, scaled_ref.shape[1]
    blocks = width // QBLK
    half = gate_ref.shape[1] // 2
    gate = jnp.zeros((2 * slots, 2 * half), F32)
    up = jnp.zeros((2 * slots, 2 * half), F32)
    order = (first, first ^ 1, first ^ 3, first ^ 2)
    for quarter, share in enumerate(order):
        source = arrived_ref if quarter < 2 else swapped_ref
        for block in range(blocks):
            lanes = slice((quarter % 2) * width + block * QBLK, (quarter % 2) * width + (block + 1) * QBLK)
            x = source[:, :, lanes].reshape(slots, QBLK).astype(F32)
            at = share * blocks + block
            into = slice(block * QBLK, (block + 1) * QBLK)
            scaled_ref[0 * slots : 1 * slots, into] = (x * gate_scale_ref[0, at]).astype(BF16)
            scaled_ref[1 * slots : 2 * slots, into] = (x * gate_scale_ref[1, at]).astype(BF16)
            scaled_ref[2 * slots : 3 * slots, into] = (x * up_scale_ref[0, at]).astype(BF16)
            scaled_ref[3 * slots : 4 * slots, into] = (x * up_scale_ref[1, at]).astype(BF16)
        depth = pl.ds(pl.multiple_of(share * width, width), width)
        gate += jnp.dot(scaled_ref[: 2 * slots, :], gate_ref[depth, :], preferred_element_type=F32)
        up += jnp.dot(scaled_ref[2 * slots :, :], up_ref[depth, :], preferred_element_type=F32)
    parts = []
    for i in range(2):
        g = gate[i * slots : (i + 1) * slots, i * half : (i + 1) * half]
        u = up[i * slots : (i + 1) * slots, i * half : (i + 1) * half]
        parts.append((g / (1.0 + jnp.exp(-g)) * u).astype(BF16))
    hidden_ref[...] = jnp.concatenate(parts, axis=1)
    send_ref[:, 2 * width :] = hidden_ref[...]
    none = jnp.zeros_like(parts[0])
    stacked = jnp.concatenate(
        [jnp.concatenate([parts[0], none], axis=1), jnp.concatenate([none, parts[1]], axis=1)], axis=0
    )
    for out_ref, shares in ((send_ref, (first ^ 3, first ^ 2)), (keep_ref, (first, first ^ 1))):
        for part, share in enumerate(shares):
            lanes = pl.ds(pl.multiple_of(share * width, width), width)
            both = jnp.dot(stacked, down_ref[:, lanes], preferred_element_type=F32)
            for block in range(blocks):
                at = share * blocks + block
                cut = slice(block * QBLK, (block + 1) * QBLK)
                value = both[:slots, cut] * down_scale_ref[0, at] + both[slots:, cut] * down_scale_ref[1, at]
                out_ref[:, part * width + block * QBLK : part * width + (block + 1) * QBLK] = value.astype(BF16)


def chip_sum_kernel(keep_ref, sent_ref, hidden_ref, message_ref, one_ref, two_ref, three_ref, near_ref):
    width, hidden_width = keep_ref.shape[1], hidden_ref.shape[1]
    rows = one_ref.shape[0]
    for k, out_ref in enumerate((message_ref, one_ref, two_ref, three_ref)):
        at = slice(k * rows, (k + 1) * rows)
        both = keep_ref[at, :].astype(F32) + sent_ref[at, :width].astype(F32)
        out_ref[:, :width] = both.astype(BF16)
        near = jnp.concatenate([hidden_ref[at, :], sent_ref[at, width:]], axis=1)
        near_ref[at, :] = near
        into = width + 2 * k * hidden_width
        message_ref[:, into : into + 2 * hidden_width] = near


def hessian_kernel(arrived_ref, near_ref, crossed_ref, out_ref):
    m = lax.axis_index("mp")
    width = out_ref.shape[0]
    counts = arrived_ref[:, :, arrived_ref.shape[2] - QBLK :].astype(F32)
    factor = 2.0 / jnp.sum(counts[:, 0, :1], axis=0, keepdims=True)
    own = near_ref[:, :width]
    start = crossed_ref.shape[1] - 8 * width
    far = [crossed_ref[:, start + i * width : start + (i + 1) * width] for i in range(8)]
    others = (
        (m, own),
        (m ^ 1, near_ref[:, width:]),
        (m ^ 2, jnp.concatenate(far[0::2], axis=0)),
        (m ^ 3, jnp.concatenate(far[1::2], axis=0)),
    )
    for share, other in others:
        block = lax.dot_general(own, other, (((0,), (0,)), ((), ())), preferred_element_type=F32)
        out_ref[:, pl.ds(pl.multiple_of(share * width, width), width)] = block * factor


def combine_kernel(coef_ref, near_ref, far_ref, out_ref):
    slots, width = coef_ref.shape[0], out_ref.shape[1]
    result = (near_ref[:, :width].astype(F32) + far_ref[...].astype(F32)).astype(BF16)
    coef = coef_ref[...]
    terms = []
    for _ in range(3):
        terms.append(coef.astype(BF16))
        coef = coef - terms[-1].astype(F32)
    out = lax.dot_general(
        jnp.concatenate(terms, axis=0),
        jnp.concatenate([result] * 3, axis=0),
        (((0,), (0,)), ((), ())),
        preferred_element_type=F32,
    )
    out_ref[...] = out.astype(BF16)


def on_device(
    tokens,
    route_ids,
    route_weights,
    gate_weight,
    gate_scale,
    up_weight,
    up_scale,
    down_weight,
    down_scale,
):
    rows, width = tokens.shape
    capacity = 2 * rows * TOP // ROUTED_ALL
    slots = 4 * capacity
    hidden_width = gate_weight.shape[2]
    shape = jax.ShapeDtypeStruct
    params = pltpu.CompilerParams(vmem_limit_bytes=24 * 1024 * 1024)

    earlier = pl.pallas_call(
        earlier_kernel,
        out_shape=shape((rows, rows), BF16),
        out_specs=VMEM,
        compiler_params=params,
        cost_estimate=pl.CostEstimate(flops=4 * 10**9, bytes_accessed=0, transcendentals=0),
        name="earlier",
    )()
    on_core_one = lax.axis_index("mp") % 2 == 1

    picked, counts, coef = pl.pallas_call(
        functools.partial(route_kernel, capacity),
        out_shape=(
            shape((4, capacity, width), BF16),
            shape((4, capacity, QBLK), BF16),
            shape((slots, rows), F32),
        ),
        in_specs=[VMEM] * 4,
        out_specs=(VMEM,) * 3,
        compiler_params=params,
        cost_estimate=pl.CostEstimate(flops=8 * 10**9, bytes_accessed=0, transcendentals=0),
        name="route",
    )(earlier, route_ids.T, route_weights.T, tokens)

    message = jnp.concatenate([picked, swap_cores(picked), counts], axis=2)

    got = [to_chips(message[k], k) for k in range(4)]
    got[0] = jnp.where(on_core_one, got[0], message[0])
    arrived = jnp.stack(got)
    swapped = swap_cores(arrived[:, :, : 2 * width])

    keep, send, hidden = pl.pallas_call(
        expert_kernel,
        out_shape=(
            shape((slots, 2 * width), BF16),
            shape((slots, 2 * width + hidden_width), BF16),
            shape((slots, hidden_width), BF16),
        ),
        in_specs=[VMEM, VMEM, VMEM, SMEM, VMEM, SMEM, VMEM, SMEM],
        out_specs=(VMEM,) * 3,
        scratch_shapes=[pltpu.VMEM((4 * slots, width), BF16)],
        compiler_params=params,
        name="expert",
    )(
        arrived,
        swapped,
        gate_weight[0],
        gate_scale[0].T,
        up_weight[0],
        up_scale[0].T,
        down_weight[0],
        down_scale[0],
    )

    message, *summed, near = pl.pallas_call(
        chip_sum_kernel,
        out_shape=(
            shape((capacity, 2 * width + 8 * hidden_width), BF16),
            *[shape((capacity, 2 * width), BF16)] * 3,
            shape((slots, 2 * hidden_width), BF16),
        ),
        in_specs=[VMEM] * 3,
        out_specs=(VMEM,) * 5,
        compiler_params=params,
        name="chip_sum",
    )(keep, swap_cores(send), hidden)

    crossed = across(message)
    back = [jnp.where(on_core_one, crossed[:, : 2 * width], message[:, : 2 * width])]
    back += [to_chips(summed[k - 1], k) for k in range(1, 4)]
    back = jnp.concatenate(back, axis=0)

    hessian = pl.pallas_call(
        hessian_kernel,
        out_shape=shape((hidden_width, 4 * hidden_width), F32),
        in_specs=[VMEM] * 3,
        out_specs=VMEM,
        compiler_params=params,
        name="hessian",
    )(arrived, near, crossed)

    mixed = pl.pallas_call(
        combine_kernel,
        out_shape=shape((rows, width), BF16),
        in_specs=[VMEM] * 3,
        out_specs=VMEM,
        compiler_params=params,
        name="combine",
    )(coef, back, swap_cores(back[:, width:]))
    return mixed, hessian[None]


def solution(mesh):
    placed = (
        P(("groups", "expert"), "mp"),
        P(("groups", "expert"), None),
        P(("groups", "expert"), None),
        P("expert", None, "mp"),
        P("expert", None, "mp"),
        P("expert", None, "mp"),
        P("expert", None, "mp"),
        P("expert", "mp", None),
        P("expert", "mp", None),
    )
    two_level = mesh.shape["expert"] == 4 and mesh.shape["mp"] == 4
    return jax.shard_map(
        on_device if two_level else on_device_any_mesh,
        mesh=mesh,
        in_specs=placed,
        out_specs=(P(("groups", "expert"), "mp"), P(("groups", "expert"), "mp", None)),
        check_vma=False,
    )
```

```python
import functools

import jax
import jax.numpy as jnp
from jax import lax
from jax.experimental import pallas as pl
from jax.experimental.pallas import tpu as pltpu
from jax.sharding import PartitionSpec as P

ROUTED_ALL = 256
TOP = 8
QBLK = 128


def dequant(weight, scale):
    row_blocks, col_blocks = scale.shape
    blocks = (
        weight.astype(jnp.float32).reshape(row_blocks, QBLK, col_blocks, QBLK)
        * scale[:, None, :, None]
    )
    return blocks.astype(jnp.bfloat16).reshape(weight.shape)


def route_slots(route_ids, experts, capacity):
    flat = route_ids.reshape(-1)
    onehot = (flat[:, None] == jnp.arange(experts, dtype=jnp.int32)[None, :]).astype(jnp.int32)
    position = jnp.sum((jnp.cumsum(onehot, axis=0) - 1) * onehot, axis=1)
    kept = (flat < experts) & (position < capacity)
    counts = jnp.minimum(jnp.sum(onehot, axis=0), capacity)
    targets = jnp.where(kept, flat * capacity + position, experts * capacity)
    return (targets.reshape(route_ids.shape), counts)


def on_device_any_mesh(
    tokens,
    route_ids,
    route_weights,
    gate_weight,
    gate_scale,
    up_weight,
    up_scale,
    down_weight,
    down_scale,
):
    experts = lax.axis_size("expert")
    capacity = 2 * route_ids.shape[0] * route_ids.shape[1] // ROUTED_ALL
    slot_total = experts * capacity
    targets, counts = route_slots(route_ids, experts, capacity)
    count_column = counts[:, None]
    gate_eff = dequant(gate_weight[0], gate_scale[0])
    up_eff = dequant(up_weight[0], up_scale[0])
    down_eff = dequant(down_weight[0], down_scale[0])
    token_count = route_ids.shape[0]
    source_index = jnp.full((slot_total + 1,), token_count, jnp.int32)
    source_index = source_index.at[targets.reshape(-1)].set(
        jnp.repeat(jnp.arange(token_count, dtype=jnp.int32), TOP)
    )
    source_index = source_index[:slot_total]
    features = lax.all_gather(tokens, "mp", axis=1, tiled=True)
    padded = jnp.concatenate([features, jnp.zeros((1, features.shape[1]), jnp.bfloat16)], axis=0)
    arrived = lax.all_to_all(
        padded[source_index].reshape(experts, capacity, features.shape[1]),
        "expert",
        split_axis=0,
        concat_axis=0,
        tiled=True,
    )
    arrived_counts = lax.all_to_all(count_column, "expert", split_axis=0, concat_axis=0, tiled=True)
    inputs = arrived.reshape(slot_total, features.shape[1])
    gate_proj = jnp.dot(inputs, gate_eff, preferred_element_type=jnp.float32)
    up_proj = jnp.dot(inputs, up_eff, preferred_element_type=jnp.float32)
    hidden = (jax.nn.silu(gate_proj) * up_proj).astype(jnp.bfloat16)
    row_total = jnp.sum(arrived_counts).astype(jnp.float32)
    hessian_rows = lax.dot_general(
        hidden,
        lax.all_gather(hidden, "mp", axis=1, tiled=True),
        (((0,), (0,)), ((), ())),
        preferred_element_type=jnp.float32,
    ) * (2.0 / row_total)
    partial_value = jnp.dot(hidden, down_eff, preferred_element_type=jnp.float32)
    summed = lax.psum_scatter(
        partial_value.astype(jnp.bfloat16), "mp", scatter_dimension=1, tiled=True
    )
    returned = lax.all_to_all(
        summed.reshape(experts, capacity, summed.shape[1]),
        "expert",
        split_axis=0,
        concat_axis=0,
        tiled=True,
    )
    width = returned.shape[2]
    flat_back = jnp.concatenate(
        [returned.reshape(slot_total, width), jnp.zeros((1, width), jnp.bfloat16)], axis=0
    )
    mixed = jnp.zeros((tokens.shape[0], width), jnp.float32)
    for route in range(TOP):
        mixed = mixed + route_weights[:, route : route + 1] * flat_back[targets[:, route]].astype(
            jnp.float32
        )
    return (mixed.astype(jnp.bfloat16), hessian_rows[None])


BOTH = ("expert", "mp")
VMEM = pl.BlockSpec(memory_space=pltpu.VMEM)
SMEM = pl.BlockSpec(memory_space=pltpu.SMEM)
F32 = jnp.float32
BF16 = jnp.bfloat16


def swap_cores(value):
    return lax.ppermute(value, "mp", [(m, m ^ 1) for m in range(4)])


def to_chips(value, k):
    pairs = [(4 * z + m, 4 * (z ^ k) + (m ^ 2 * (m & 1))) for z in range(4) for m in range(4)]
    if k == 0:
        pairs = [(a, b) for a, b in pairs if a != b]
    return lax.ppermute(value, BOTH, pairs)


def across(value):
    return lax.ppermute(value, BOTH, [(4 * z + m, 4 * z + (m ^ 2)) for z in range(4) for m in range(4)])


def earlier_kernel(out_ref):
    row, column = (lax.broadcasted_iota(jnp.int32, out_ref.shape, i) for i in range(2))
    out_ref[...] = jnp.where(row < column, 1.0, 0.0).astype(BF16)


def route_kernel(capacity, earlier_ref, ids_ref, weights_ref, tokens_ref, rows_ref, count_ref, coef_ref):
    z = lax.axis_index("expert")
    ids, weights = ids_ref[...], weights_ref[...]
    rows = ids.shape[1]
    live, weight = [], []
    for k in range(4):
        hit = ids == (z ^ k)
        live.append(jnp.sum(jnp.where(hit, 1.0, 0.0), axis=0, keepdims=True))
        weight.append(jnp.sum(jnp.where(hit, weights, 0.0), axis=0, keepdims=True))
    position = jnp.dot(
        jnp.concatenate(live, axis=0).astype(BF16),
        earlier_ref[...],
        preferred_element_type=F32,
    )
    slot = lax.broadcasted_iota(jnp.int32, (capacity, rows), 0).astype(F32)
    chosen = []
    for k in range(4):
        kept = (live[k] > 0.5) & (position[k : k + 1] == slot)
        one = jnp.where(kept, 1.0, 0.0)
        chosen.append(one)
        coef_ref[capacity * k : capacity * (k + 1), :] = one * weight[k]
        total = jnp.minimum(jnp.sum(live[k], axis=1, keepdims=True), float(capacity))
        count_ref[k] = jnp.broadcast_to(total, count_ref.shape[1:]).astype(BF16)
    picked = jnp.dot(
        jnp.concatenate(chosen, axis=0).astype(BF16), tokens_ref[...], preferred_element_type=F32
    ).astype(BF16)
    rows_ref[...] = picked.reshape(rows_ref.shape)


def spread_kernel(*refs):
    for scale_ref, out_ref in zip(refs[:3], refs[3:]):
        for at in range(scale_ref.shape[1]):
            for i in range(2):
                out_ref[i : i + 1, at * QBLK : (at + 1) * QBLK] = jnp.full((1, QBLK), scale_ref[i, at], F32)


def line_up_kernel(own_ref, other_ref, count_ref, *out_refs):
    for k, out_ref in enumerate(out_refs):
        out_ref[...] = jnp.concatenate([own_ref[k], other_ref[k], count_ref[k]], axis=1)


def collect_kernel(own_ref, three_ref, two_ref, one_ref, zero_ref, _, out_ref, count_ref):
    rows, width = own_ref.shape[0], out_ref.shape[1]
    crossed = (lax.axis_index("mp") % 2 == 1).astype(F32)
    value = own_ref[...].astype(F32) * (1.0 - crossed) + zero_ref[...].astype(F32) * crossed
    for k, rows_in in enumerate((value.astype(BF16), one_ref[...], two_ref[...], three_ref[...])):
        out_ref[k * rows : (k + 1) * rows, :] = rows_in[:, :width]
        count_ref[k * rows : (k + 1) * rows, :] = rows_in[:, width:]


def shares_in_order():
    m = lax.axis_index("mp")
    first = m ^ (2 * (m % 2))
    return (first, first ^ 1, first ^ 3, first ^ 2)


def project(x_ref, shares, weight_ref, scale_ref):
    slots, width = x_ref.shape[0], x_ref.shape[1] // len(shares)
    total = None
    for part, share in enumerate(shares):
        depth = pl.ds(pl.multiple_of(share * width, width), width)
        x = x_ref[:, part * width : (part + 1) * width].astype(F32)
        scaled = jnp.concatenate([(x * scale_ref[i : i + 1, depth]).astype(BF16) for i in range(2)], axis=0)
        term = jnp.dot(scaled, weight_ref[depth, :], preferred_element_type=F32)
        total = term if total is None else total + term
    return total


def project_down(parts, shares, down_ref, scale_ref, out_ref):
    slots, width = parts[0].shape[0], down_ref.shape[1] // 4
    none = jnp.zeros_like(parts[0])
    stacked = jnp.concatenate(
        [jnp.concatenate([parts[0], none], axis=1), jnp.concatenate([none, parts[1]], axis=1)], axis=0
    )
    for part, share in enumerate(shares):
        lanes = pl.ds(pl.multiple_of(share * width, width), width)
        both = jnp.dot(stacked, down_ref[:, lanes], preferred_element_type=F32)
        value = both[:slots] * scale_ref[:1, lanes] + both[slots:] * scale_ref[1:, lanes]
        out_ref[:, part * width : (part + 1) * width] = value.astype(BF16)


def near_kernel(x_ref, gate_ref, up_ref, gate_scale_ref, up_scale_ref, gate_out_ref, up_out_ref):
    shares = shares_in_order()[:2]
    gate_out_ref[...] = project(x_ref, shares, gate_ref, gate_scale_ref)
    up_out_ref[...] = project(x_ref, shares, up_ref, up_scale_ref)


def hidden_kernel(
    x_ref,
    near_gate_ref,
    near_up_ref,
    gate_ref,
    up_ref,
    down_ref,
    gate_scale_ref,
    up_scale_ref,
    down_scale_ref,
    send_ref,
    hidden_ref,
):
    shares = shares_in_order()[2:]
    gate = near_gate_ref[...] + project(x_ref, shares, gate_ref, gate_scale_ref)
    up = near_up_ref[...] + project(x_ref, shares, up_ref, up_scale_ref)
    slots, half = x_ref.shape[0], gate_ref.shape[1] // 2
    parts = []
    for i in range(2):
        g = gate[i * slots : (i + 1) * slots, i * half : (i + 1) * half]
        u = up[i * slots : (i + 1) * slots, i * half : (i + 1) * half]
        parts.append((g / (1.0 + jnp.exp(-g)) * u).astype(BF16))
        hidden_ref[:, i * half : (i + 1) * half] = parts[i]
        send_ref[:, x_ref.shape[1] + i * half : x_ref.shape[1] + (i + 1) * half] = parts[i]
    project_down(parts, shares, down_ref, down_scale_ref, send_ref)


def keep_kernel(hidden_ref, down_ref, down_scale_ref, keep_ref):
    half = hidden_ref.shape[1] // 2
    parts = (hidden_ref[:, :half], hidden_ref[:, half:])
    project_down(parts, shares_in_order()[:2], down_ref, down_scale_ref, keep_ref)


def chip_sum_kernel(keep_ref, sent_ref, hidden_ref, message_ref, one_ref, two_ref, three_ref, near_ref):
    width, hidden_width = keep_ref.shape[1], hidden_ref.shape[1]
    rows = one_ref.shape[0]
    for k, out_ref in enumerate((message_ref, one_ref, two_ref, three_ref)):
        at = slice(k * rows, (k + 1) * rows)
        both = keep_ref[at, :].astype(F32) + sent_ref[at, :width].astype(F32)
        out_ref[:, :width] = both.astype(BF16)
        near = jnp.concatenate([hidden_ref[at, :], sent_ref[at, width:]], axis=1)
        near_ref[at, :] = near
        into = width + 2 * k * hidden_width
        message_ref[:, into : into + 2 * hidden_width] = near


def hessian_kernel(count_ref, near_ref, crossed_ref, out_ref):
    m = lax.axis_index("mp")
    width = out_ref.shape[0]
    rows = count_ref.shape[0] // 4
    counts = [count_ref[k * rows : k * rows + 1, :].astype(F32)[:, :1] for k in range(4)]
    factor = 2.0 / (counts[0] + counts[1] + counts[2] + counts[3])
    own = near_ref[:, :width]
    start = crossed_ref.shape[1] - 8 * width
    far = [crossed_ref[:, start + i * width : start + (i + 1) * width] for i in range(8)]
    others = (
        (m, own),
        (m ^ 1, near_ref[:, width:]),
        (m ^ 2, jnp.concatenate(far[0::2], axis=0)),
        (m ^ 3, jnp.concatenate(far[1::2], axis=0)),
    )
    for share, other in others:
        block = lax.dot_general(own, other, (((0,), (0,)), ((), ())), preferred_element_type=F32)
        out_ref[:, pl.ds(pl.multiple_of(share * width, width), width)] = block * factor


def collect_back_kernel(own_ref, three_ref, two_ref, one_ref, zero_ref, mine_ref, other_ref):
    rows, width = one_ref.shape[0], mine_ref.shape[1]
    crossed = (lax.axis_index("mp") % 2 == 1).astype(F32)
    here = slice(0, 2 * width)
    value = own_ref[:, here].astype(F32) * (1.0 - crossed) + zero_ref[:, here].astype(F32) * crossed
    for k, rows_in in enumerate((value.astype(BF16), one_ref[...], two_ref[...], three_ref[...])):
        mine_ref[k * rows : (k + 1) * rows, :] = rows_in[:, :width]
        other_ref[k * rows : (k + 1) * rows, :] = rows_in[:, width:]


def combine_kernel(coef_ref, near_ref, far_ref, out_ref):
    slots, width = coef_ref.shape[0], out_ref.shape[1]
    result = (near_ref[...].astype(F32) + far_ref[...].astype(F32)).astype(BF16)
    coef = coef_ref[...]
    terms = []
    for _ in range(3):
        terms.append(coef.astype(BF16))
        coef = coef - terms[-1].astype(F32)
    out = lax.dot_general(
        jnp.concatenate(terms, axis=0),
        jnp.concatenate([result] * 3, axis=0),
        (((0,), (0,)), ((), ())),
        preferred_element_type=F32,
    )
    out_ref[...] = out.astype(BF16)


def on_device(
    tokens,
    route_ids,
    route_weights,
    gate_weight,
    gate_scale,
    up_weight,
    up_scale,
    down_weight,
    down_scale,
):
    rows, width = tokens.shape
    capacity = 2 * rows * TOP // ROUTED_ALL
    slots = 4 * capacity
    hidden_width = gate_weight.shape[2]
    shape = jax.ShapeDtypeStruct

    def call(kernel, name, outs, args, scalars=0, flops=0):
        single = not isinstance(outs, tuple)
        return pl.pallas_call(
            kernel,
            out_shape=outs,
            in_specs=[SMEM] * scalars + [VMEM] * (len(args) - scalars),
            out_specs=VMEM if single else (VMEM,) * len(outs),
            compiler_params=pltpu.CompilerParams(vmem_limit_bytes=8 * 1024 * 1024),
            cost_estimate=pl.CostEstimate(flops=flops, bytes_accessed=0, transcendentals=0) if flops else None,
            name=name,
        )(*args)

    earlier = call(earlier_kernel, "earlier", shape((rows, rows), BF16), (), flops=4 * 10**9)
    picked, counts, coef = call(
        functools.partial(route_kernel, capacity),
        "route",
        (shape((4, capacity, width), BF16), shape((4, capacity, QBLK), BF16), shape((slots, rows), F32)),
        (earlier, route_ids.T, route_weights.T, tokens),
        flops=10**11,
    )
    messages = call(
        line_up_kernel,
        "line_up",
        (shape((capacity, 2 * width + QBLK), BF16),) * 4,
        (picked, swap_cores(picked), counts),
    )
    scales = call(
        spread_kernel,
        "spread",
        (shape((2, 4 * width), F32),) * 3,
        (gate_scale[0].T, up_scale[0].T, down_scale[0]),
        scalars=3,
    )
    gate, up, down = gate_weight[0], up_weight[0], down_weight[0]

    arrived, arrived_counts = call(
        collect_kernel,
        "collect",
        (shape((slots, 2 * width), BF16), shape((slots, QBLK), BF16)),
        (messages[0], *[to_chips(messages[k], k) for k in (3, 2, 1, 0)], scales[0]),
    )
    swapped = swap_cores(arrived)
    near = call(
        near_kernel,
        "near",
        (shape((2 * slots, hidden_width), F32),) * 2,
        (arrived, gate, up, *scales[:2]),
    )
    send, hidden = call(
        hidden_kernel,
        "hidden",
        (shape((slots, 2 * width + hidden_width), BF16), shape((slots, hidden_width), BF16)),
        (swapped, *near, gate, up, down, *scales),
    )
    sent = swap_cores(send)
    keep = call(keep_kernel, "keep", shape((slots, 2 * width), BF16), (hidden, down, scales[2]))

    message, *summed, chip_hidden = call(
        chip_sum_kernel,
        "chip_sum",
        (
            shape((capacity, 2 * width + 8 * hidden_width), BF16),
            *[shape((capacity, 2 * width), BF16)] * 3,
            shape((slots, 2 * hidden_width), BF16),
        ),
        (keep, sent, hidden),
    )
    crossed = across(message)
    back = {k: to_chips(summed[k - 1], k) for k in range(1, 4)}
    back[0] = crossed
    hessian = call(
        hessian_kernel,
        "hessian",
        shape((hidden_width, 4 * hidden_width), F32),
        (arrived_counts, chip_hidden, crossed),
    )
    mine, other = call(
        collect_back_kernel, "collect_back", (shape((slots, width), BF16),) * 2, (message, *[back[k] for k in (3, 2, 1, 0)])
    )
    mixed = call(
        combine_kernel, "combine", shape((rows, width), BF16), (coef, mine, swap_cores(other))
    )
    return mixed, hessian[None]


def solution(mesh):
    placed = (
        P(("groups", "expert"), "mp"),
        P(("groups", "expert"), None),
        P(("groups", "expert"), None),
        P("expert", None, "mp"),
        P("expert", None, "mp"),
        P("expert", None, "mp"),
        P("expert", None, "mp"),
        P("expert", "mp", None),
        P("expert", "mp", None),
    )
    two_level = mesh.shape["expert"] == 4 and mesh.shape["mp"] == 4
    return jax.shard_map(
        on_device if two_level else on_device_any_mesh,
        mesh=mesh,
        in_specs=placed,
        out_specs=(P(("groups", "expert"), "mp"), P(("groups", "expert"), "mp", None)),
        check_vma=False,
    )
```

```python
import functools

import jax
import jax.numpy as jnp
from jax import lax
from jax.experimental import pallas as pl
from jax.experimental.pallas import tpu as pltpu
from jax.sharding import PartitionSpec as P

ROUTED_ALL = 256
TOP = 8
QBLK = 128


def dequant(weight, scale):
    row_blocks, col_blocks = scale.shape
    blocks = (
        weight.astype(jnp.float32).reshape(row_blocks, QBLK, col_blocks, QBLK)
        * scale[:, None, :, None]
    )
    return blocks.astype(jnp.bfloat16).reshape(weight.shape)


def route_slots(route_ids, experts, capacity):
    flat = route_ids.reshape(-1)
    onehot = (flat[:, None] == jnp.arange(experts, dtype=jnp.int32)[None, :]).astype(jnp.int32)
    position = jnp.sum((jnp.cumsum(onehot, axis=0) - 1) * onehot, axis=1)
    kept = (flat < experts) & (position < capacity)
    counts = jnp.minimum(jnp.sum(onehot, axis=0), capacity)
    targets = jnp.where(kept, flat * capacity + position, experts * capacity)
    return (targets.reshape(route_ids.shape), counts)


def on_device_any_mesh(
    tokens,
    route_ids,
    route_weights,
    gate_weight,
    gate_scale,
    up_weight,
    up_scale,
    down_weight,
    down_scale,
):
    experts = lax.axis_size("expert")
    capacity = 2 * route_ids.shape[0] * route_ids.shape[1] // ROUTED_ALL
    slot_total = experts * capacity
    targets, counts = route_slots(route_ids, experts, capacity)
    count_column = counts[:, None]
    gate_eff = dequant(gate_weight[0], gate_scale[0])
    up_eff = dequant(up_weight[0], up_scale[0])
    down_eff = dequant(down_weight[0], down_scale[0])
    token_count = route_ids.shape[0]
    source_index = jnp.full((slot_total + 1,), token_count, jnp.int32)
    source_index = source_index.at[targets.reshape(-1)].set(
        jnp.repeat(jnp.arange(token_count, dtype=jnp.int32), TOP)
    )
    source_index = source_index[:slot_total]
    features = lax.all_gather(tokens, "mp", axis=1, tiled=True)
    padded = jnp.concatenate([features, jnp.zeros((1, features.shape[1]), jnp.bfloat16)], axis=0)
    arrived = lax.all_to_all(
        padded[source_index].reshape(experts, capacity, features.shape[1]),
        "expert",
        split_axis=0,
        concat_axis=0,
        tiled=True,
    )
    arrived_counts = lax.all_to_all(count_column, "expert", split_axis=0, concat_axis=0, tiled=True)
    inputs = arrived.reshape(slot_total, features.shape[1])
    gate_proj = jnp.dot(inputs, gate_eff, preferred_element_type=jnp.float32)
    up_proj = jnp.dot(inputs, up_eff, preferred_element_type=jnp.float32)
    hidden = (jax.nn.silu(gate_proj) * up_proj).astype(jnp.bfloat16)
    row_total = jnp.sum(arrived_counts).astype(jnp.float32)
    hessian_rows = lax.dot_general(
        hidden,
        lax.all_gather(hidden, "mp", axis=1, tiled=True),
        (((0,), (0,)), ((), ())),
        preferred_element_type=jnp.float32,
    ) * (2.0 / row_total)
    partial_value = jnp.dot(hidden, down_eff, preferred_element_type=jnp.float32)
    summed = lax.psum_scatter(
        partial_value.astype(jnp.bfloat16), "mp", scatter_dimension=1, tiled=True
    )
    returned = lax.all_to_all(
        summed.reshape(experts, capacity, summed.shape[1]),
        "expert",
        split_axis=0,
        concat_axis=0,
        tiled=True,
    )
    width = returned.shape[2]
    flat_back = jnp.concatenate(
        [returned.reshape(slot_total, width), jnp.zeros((1, width), jnp.bfloat16)], axis=0
    )
    mixed = jnp.zeros((tokens.shape[0], width), jnp.float32)
    for route in range(TOP):
        mixed = mixed + route_weights[:, route : route + 1] * flat_back[targets[:, route]].astype(
            jnp.float32
        )
    return (mixed.astype(jnp.bfloat16), hessian_rows[None])


BOTH = ("expert", "mp")
VMEM = pl.BlockSpec(memory_space=pltpu.VMEM)
SMEM = pl.BlockSpec(memory_space=pltpu.SMEM)
F32 = jnp.float32
BF16 = jnp.bfloat16


def swap_cores(value):
    return lax.ppermute(value, "mp", [(m, m ^ 1) for m in range(4)])


def to_chips(value, k):
    pairs = [(4 * z + m, 4 * (z ^ k) + (m ^ 2 * (m & 1))) for z in range(4) for m in range(4)]
    return lax.ppermute(value, BOTH, pairs)


def across(value):
    return lax.ppermute(value, BOTH, [(4 * z + m, 4 * z + (m ^ 2)) for z in range(4) for m in range(4)])


def earlier_kernel(out_ref):
    row, column = (lax.broadcasted_iota(jnp.int32, out_ref.shape, i) for i in range(2))
    out_ref[...] = jnp.where(row < column, 1.0, 0.0).astype(BF16)


def route_kernel(capacity, earlier_ref, ids_ref, weights_ref, tokens_ref, rows_ref, cross_ref, count_ref, coef_ref):
    z = lax.axis_index("expert")
    ids, weights = ids_ref[...], weights_ref[...]
    rows = ids.shape[1]
    live, weight = [], []
    for k in range(4):
        hit = ids == (z ^ k)
        live.append(jnp.sum(jnp.where(hit, 1.0, 0.0), axis=0, keepdims=True))
        weight.append(jnp.sum(jnp.where(hit, weights, 0.0), axis=0, keepdims=True))
    position = jnp.dot(
        jnp.concatenate(live, axis=0).astype(BF16),
        earlier_ref[...],
        preferred_element_type=F32,
    )
    slot = lax.broadcasted_iota(jnp.int32, (capacity, rows), 0).astype(F32)
    chosen = []
    for k in range(4):
        kept = (live[k] > 0.5) & (position[k : k + 1] == slot)
        one = jnp.where(kept, 1.0, 0.0)
        chosen.append(one)
        coef_ref[capacity * k : capacity * (k + 1), :] = one * weight[k]
        total = jnp.minimum(jnp.sum(live[k], axis=1, keepdims=True), float(capacity))
        count_ref[k] = jnp.broadcast_to(total, count_ref.shape[1:]).astype(BF16)
    picked = jnp.dot(
        jnp.concatenate(chosen, axis=0).astype(BF16), tokens_ref[...], preferred_element_type=F32
    ).astype(BF16)
    rows_ref[...] = picked.reshape(rows_ref.shape)
    cross_ref[...] = jnp.zeros_like(cross_ref)
    cross_ref[:, : picked.shape[1]] = picked[:capacity]


def spread_kernel(*refs):
    for scale_ref, out_ref in zip(refs[:3], refs[3:]):
        for at in range(scale_ref.shape[1]):
            for i in range(2):
                out_ref[i : i + 1, at * QBLK : (at + 1) * QBLK] = jnp.full((1, QBLK), scale_ref[i, at], F32)


def line_up_kernel(own_ref, other_ref, count_ref, *out_refs):
    for k, out_ref in enumerate(out_refs, 1):
        out_ref[...] = jnp.concatenate([own_ref[k], other_ref[k], count_ref[k]], axis=1)


def on_core(core):
    return (lax.axis_index("mp") % 2 == core).astype(F32)


def collect_kernel(own_ref, other_ref, count_ref, crossed_ref, three_ref, two_ref, one_ref, _, out_ref, counts_ref):
    rows, width = crossed_ref.shape[0], out_ref.shape[1] // 2
    crossed = crossed_ref[:, :width]
    zero = on_core(0)
    out_ref[:rows, :width] = (own_ref[0].astype(F32) * zero + crossed.astype(F32) * (1.0 - zero)).astype(BF16)
    out_ref[:rows, width:] = (other_ref[0].astype(F32) * zero).astype(BF16)
    counts_ref[:rows, :] = count_ref[0]
    for k, ref in enumerate((one_ref, two_ref, three_ref), 1):
        out_ref[k * rows : (k + 1) * rows, :] = ref[:, : 2 * width]
        counts_ref[k * rows : (k + 1) * rows, :] = ref[:, 2 * width :]
    out_ref[4 * rows :, :width] = crossed
    out_ref[4 * rows :, width:] = jnp.zeros_like(crossed)


def shares_in_order():
    m = lax.axis_index("mp")
    first = m ^ (2 * (m % 2))
    return (first, first ^ 1, first ^ 3, first ^ 2)


def project(x, share, weight_ref, scale_ref):
    width = x.shape[1]
    depth = pl.ds(pl.multiple_of(share * width, width), width)
    scaled = jnp.concatenate([(x * scale_ref[i : i + 1, depth]).astype(BF16) for i in range(2)], axis=0)
    return jnp.dot(scaled, weight_ref[depth, :], preferred_element_type=F32)


def near_kernel(x_ref, gate_ref, up_ref, gate_scale_ref, up_scale_ref, gate_out_ref, up_out_ref):
    share = shares_in_order()[0]
    slots, width = gate_out_ref.shape[0] // 2, x_ref.shape[1] // 2
    x = x_ref[:slots, :width].astype(F32)
    gate_out_ref[...] = project(x, share, gate_ref, gate_scale_ref)
    up_out_ref[...] = project(x, share, up_ref, up_scale_ref)


def hidden_kernel(
    arrived_ref,
    swapped_ref,
    near_gate_ref,
    near_up_ref,
    gate_ref,
    up_ref,
    down_ref,
    gate_scale_ref,
    up_scale_ref,
    down_scale_ref,
    send_ref,
    keep_ref,
    hidden_ref,
    cross_ref,
):
    shares = shares_in_order()
    slots, half = near_gate_ref.shape[0] // 2, gate_ref.shape[1] // 2
    rows, width = slots // 4, arrived_ref.shape[1] // 2
    zero = on_core(0)
    filled = []
    for ref, lacks, missing_ref in ((arrived_ref, 1.0 - zero, swapped_ref), (swapped_ref, zero, arrived_ref)):
        first = ref[:rows, width:].astype(F32) + missing_ref[slots:, :width].astype(F32) * lacks
        filled.append(jnp.concatenate([first, ref[rows:slots, width:].astype(F32)], axis=0))
    gate, up = near_gate_ref[...], near_up_ref[...]
    for x, share in ((filled[0], shares[1]), (swapped_ref[:slots, :width].astype(F32), shares[2]), (filled[1], shares[3])):
        gate += project(x, share, gate_ref, gate_scale_ref)
        up += project(x, share, up_ref, up_scale_ref)
    parts = []
    for i in range(2):
        g = gate[i * slots : (i + 1) * slots, i * half : (i + 1) * half]
        u = up[i * slots : (i + 1) * slots, i * half : (i + 1) * half]
        parts.append((g / (1.0 + jnp.exp(-g)) * u).astype(BF16))
        lanes = slice(i * half, (i + 1) * half)
        hidden_ref[:, lanes] = parts[i]
        send_ref[:, 2 * width + i * half : 2 * width + (i + 1) * half] = parts[i]
        for k in range(4):
            into = 2 * width + 2 * k * half + i * half
            cross_ref[:, into : into + half] = parts[i][k * rows : (k + 1) * rows]
    none = jnp.zeros_like(parts[0])
    stacked = jnp.concatenate(
        [jnp.concatenate([parts[0], none], axis=1), jnp.concatenate([none, parts[1]], axis=1)], axis=0
    )
    for out_ref, part, share in (
        (send_ref, 0, shares[2]),
        (send_ref, 1, shares[3]),
        (keep_ref, 0, shares[0]),
        (keep_ref, 1, shares[1]),
    ):
        lanes = pl.ds(pl.multiple_of(share * width, width), width)
        both = jnp.dot(stacked, down_ref[:, lanes], preferred_element_type=F32)
        value = both[:slots] * down_scale_ref[:1, lanes] + both[slots:] * down_scale_ref[1:, lanes]
        out_ref[:, part * width : (part + 1) * width] = value.astype(BF16)
    for part in range(2):
        lanes, turned = slice(part * width, (part + 1) * width), slice((1 - part) * width, (2 - part) * width)
        value = send_ref[:rows, turned].astype(F32) * zero + keep_ref[:rows, lanes].astype(F32) * (1.0 - zero)
        cross_ref[:, lanes] = value.astype(BF16)


def chip_sum_kernel(keep_ref, sent_ref, *out_refs):
    rows, width = out_refs[0].shape
    for k, out_ref in enumerate(out_refs):
        at = slice(k * rows, (k + 1) * rows)
        out_ref[...] = (keep_ref[at, :].astype(F32) + sent_ref[at, :width].astype(F32)).astype(BF16)


def unpack_kernel(crossed_ref, out_ref):
    width = out_ref.shape[1]
    rows = out_ref.shape[0] // 4
    start = crossed_ref.shape[1] - 4 * width
    for k in range(4):
        out_ref[k * rows : (k + 1) * rows, :] = crossed_ref[:, start + k * width : start + (k + 1) * width]


def hessian_kernel(count_ref, own_ref, sent_ref, far_ref, other_far_ref, out_ref, done_ref):
    m = lax.axis_index("mp")
    width = out_ref.shape[0]
    rows = count_ref.shape[0] // 4
    counts = [count_ref[k * rows : k * rows + 1, :].astype(F32)[:, :1] for k in range(4)]
    factor = 2.0 / (counts[0] + counts[1] + counts[2] + counts[3])
    own = own_ref[...]
    others = ((m, own), (m ^ 1, sent_ref[:, sent_ref.shape[1] - width :]), (m ^ 2, far_ref[...]), (m ^ 3, other_far_ref[...]))
    for share, other in others:
        block = lax.dot_general(own, other, (((0,), (0,)), ((), ())), preferred_element_type=F32)
        out_ref[:, pl.ds(pl.multiple_of(share * width, width), width)] = block * factor
    done_ref[...] = jnp.zeros_like(done_ref)


def collect_back_kernel(summed_ref, crossed_ref, three_ref, two_ref, one_ref, _, mine_ref, other_ref):
    rows, width = one_ref.shape[0], mine_ref.shape[1]
    crossed = crossed_ref[:, : 2 * width].astype(F32)
    value = (crossed + summed_ref[...].astype(F32) * on_core(0)).astype(BF16)
    for k, rows_in in enumerate((value, one_ref[...], two_ref[...], three_ref[...])):
        mine_ref[k * rows : (k + 1) * rows, :] = rows_in[:, :width]
        other_ref[k * rows : (k + 1) * rows, :] = rows_in[:, width:]


def combine_kernel(coef_ref, near_ref, far_ref, out_ref):
    slots, width = coef_ref.shape[0], out_ref.shape[1]
    result = (near_ref[...].astype(F32) + far_ref[...].astype(F32)).astype(BF16)
    coef = coef_ref[...]
    terms = []
    for _ in range(3):
        terms.append(coef.astype(BF16))
        coef = coef - terms[-1].astype(F32)
    out = lax.dot_general(
        jnp.concatenate(terms, axis=0),
        jnp.concatenate([result] * 3, axis=0),
        (((0,), (0,)), ((), ())),
        preferred_element_type=F32,
    )
    out_ref[...] = out.astype(BF16)


def on_device(
    tokens,
    route_ids,
    route_weights,
    gate_weight,
    gate_scale,
    up_weight,
    up_scale,
    down_weight,
    down_scale,
):
    rows, width = tokens.shape
    capacity = 2 * rows * TOP // ROUTED_ALL
    slots = 4 * capacity
    hidden_width = gate_weight.shape[2]
    shape = jax.ShapeDtypeStruct

    def call(kernel, name, outs, args, scalars=0, flops=0):
        single = not isinstance(outs, tuple)
        return pl.pallas_call(
            kernel,
            out_shape=outs,
            in_specs=[SMEM] * scalars + [VMEM] * (len(args) - scalars),
            out_specs=VMEM if single else (VMEM,) * len(outs),
            compiler_params=pltpu.CompilerParams(vmem_limit_bytes=8 * 1024 * 1024),
            cost_estimate=pl.CostEstimate(flops=flops, bytes_accessed=0, transcendentals=0) if flops else None,
            name=name,
        )(*args)

    earlier = call(earlier_kernel, "earlier", shape((rows, rows), BF16), (), flops=4 * 10**9)
    picked, cross, counts, coef = call(
        functools.partial(route_kernel, capacity),
        "route",
        (
            shape((4, capacity, width), BF16),
            shape((capacity, 2 * width + 2 * QBLK), BF16),
            shape((4, capacity, QBLK), BF16),
            shape((slots, rows), F32),
        ),
        (earlier, route_ids.T, route_weights.T, tokens),
        flops=10**11,
    )
    other = swap_cores(picked)
    crossed = across(cross)
    messages = call(
        line_up_kernel, "line_up", (shape((capacity, 2 * width + QBLK), BF16),) * 3, (picked, other, counts)
    )
    scales = call(
        spread_kernel,
        "spread",
        (shape((2, 4 * width), F32),) * 3,
        (gate_scale[0].T, up_scale[0].T, down_scale[0]),
        scalars=3,
    )
    gate, up, down = gate_weight[0], up_weight[0], down_weight[0]

    arrived, arrived_counts = call(
        collect_kernel,
        "collect",
        (shape((slots + capacity, 2 * width), BF16), shape((slots, QBLK), BF16)),
        (picked, other, counts, crossed, *[to_chips(messages[k - 1], k) for k in (3, 2, 1)], scales[0]),
    )
    swapped = swap_cores(arrived)
    near = call(
        near_kernel,
        "near",
        (shape((2 * slots, hidden_width), F32),) * 2,
        (arrived, gate, up, *scales[:2]),
    )
    send, keep, hidden, cross = call(
        hidden_kernel,
        "hidden",
        (
            shape((slots, 2 * width + hidden_width), BF16),
            shape((slots, 2 * width), BF16),
            shape((slots, hidden_width), BF16),
            shape((capacity, 2 * width + 4 * hidden_width), BF16),
        ),
        (arrived, swapped, *near, gate, up, down, *scales),
    )
    sent = swap_cores(send)
    crossed = across(cross)
    summed = call(chip_sum_kernel, "chip_sum", (shape((capacity, 2 * width), BF16),) * 4, (keep, sent))
    back = {k: to_chips(summed[k], k) for k in range(1, 4)}
    far = call(unpack_kernel, "unpack", shape((slots, hidden_width), BF16), (crossed,))
    hessian, done = call(
        hessian_kernel,
        "hessian",
        (shape((hidden_width, 4 * hidden_width), F32), shape((8, QBLK), F32)),
        (arrived_counts, hidden, sent, far, swap_cores(far)),
    )
    mine, other = call(
        collect_back_kernel,
        "collect_back",
        (shape((slots, width), BF16),) * 2,
        (summed[0], crossed, *[back[k] for k in (3, 2, 1)], done),
    )
    mixed = call(
        combine_kernel, "combine", shape((rows, width), BF16), (coef, mine, swap_cores(other))
    )
    return mixed, hessian[None]


def solution(mesh):
    placed = (
        P(("groups", "expert"), "mp"),
        P(("groups", "expert"), None),
        P(("groups", "expert"), None),
        P("expert", None, "mp"),
        P("expert", None, "mp"),
        P("expert", None, "mp"),
        P("expert", None, "mp"),
        P("expert", "mp", None),
        P("expert", "mp", None),
    )
    two_level = mesh.shape["expert"] == 4 and mesh.shape["mp"] == 4
    return jax.shard_map(
        on_device if two_level else on_device_any_mesh,
        mesh=mesh,
        in_specs=placed,
        out_specs=(P(("groups", "expert"), "mp"), P(("groups", "expert"), "mp", None)),
        check_vma=False,
    )
```

```python
import functools

import jax
import jax.numpy as jnp
from jax import lax
from jax.experimental import pallas as pl
from jax.experimental.pallas import tpu as pltpu
from jax.sharding import PartitionSpec as P

ROUTED_ALL = 256
TOP = 8
QBLK = 128


def dequant(weight, scale):
    row_blocks, col_blocks = scale.shape
    blocks = (
        weight.astype(jnp.float32).reshape(row_blocks, QBLK, col_blocks, QBLK)
        * scale[:, None, :, None]
    )
    return blocks.astype(jnp.bfloat16).reshape(weight.shape)


def route_slots(route_ids, experts, capacity):
    flat = route_ids.reshape(-1)
    onehot = (flat[:, None] == jnp.arange(experts, dtype=jnp.int32)[None, :]).astype(jnp.int32)
    position = jnp.sum((jnp.cumsum(onehot, axis=0) - 1) * onehot, axis=1)
    kept = (flat < experts) & (position < capacity)
    counts = jnp.minimum(jnp.sum(onehot, axis=0), capacity)
    targets = jnp.where(kept, flat * capacity + position, experts * capacity)
    return (targets.reshape(route_ids.shape), counts)


def on_device_any_mesh(
    tokens,
    route_ids,
    route_weights,
    gate_weight,
    gate_scale,
    up_weight,
    up_scale,
    down_weight,
    down_scale,
):
    experts = lax.axis_size("expert")
    capacity = 2 * route_ids.shape[0] * route_ids.shape[1] // ROUTED_ALL
    slot_total = experts * capacity
    targets, counts = route_slots(route_ids, experts, capacity)
    count_column = counts[:, None]
    gate_eff = dequant(gate_weight[0], gate_scale[0])
    up_eff = dequant(up_weight[0], up_scale[0])
    down_eff = dequant(down_weight[0], down_scale[0])
    token_count = route_ids.shape[0]
    source_index = jnp.full((slot_total + 1,), token_count, jnp.int32)
    source_index = source_index.at[targets.reshape(-1)].set(
        jnp.repeat(jnp.arange(token_count, dtype=jnp.int32), TOP)
    )
    source_index = source_index[:slot_total]
    features = lax.all_gather(tokens, "mp", axis=1, tiled=True)
    padded = jnp.concatenate([features, jnp.zeros((1, features.shape[1]), jnp.bfloat16)], axis=0)
    arrived = lax.all_to_all(
        padded[source_index].reshape(experts, capacity, features.shape[1]),
        "expert",
        split_axis=0,
        concat_axis=0,
        tiled=True,
    )
    arrived_counts = lax.all_to_all(count_column, "expert", split_axis=0, concat_axis=0, tiled=True)
    inputs = arrived.reshape(slot_total, features.shape[1])
    gate_proj = jnp.dot(inputs, gate_eff, preferred_element_type=jnp.float32)
    up_proj = jnp.dot(inputs, up_eff, preferred_element_type=jnp.float32)
    hidden = (jax.nn.silu(gate_proj) * up_proj).astype(jnp.bfloat16)
    row_total = jnp.sum(arrived_counts).astype(jnp.float32)
    hessian_rows = lax.dot_general(
        hidden,
        lax.all_gather(hidden, "mp", axis=1, tiled=True),
        (((0,), (0,)), ((), ())),
        preferred_element_type=jnp.float32,
    ) * (2.0 / row_total)
    partial_value = jnp.dot(hidden, down_eff, preferred_element_type=jnp.float32)
    summed = lax.psum_scatter(
        partial_value.astype(jnp.bfloat16), "mp", scatter_dimension=1, tiled=True
    )
    returned = lax.all_to_all(
        summed.reshape(experts, capacity, summed.shape[1]),
        "expert",
        split_axis=0,
        concat_axis=0,
        tiled=True,
    )
    width = returned.shape[2]
    flat_back = jnp.concatenate(
        [returned.reshape(slot_total, width), jnp.zeros((1, width), jnp.bfloat16)], axis=0
    )
    mixed = jnp.zeros((tokens.shape[0], width), jnp.float32)
    for route in range(TOP):
        mixed = mixed + route_weights[:, route : route + 1] * flat_back[targets[:, route]].astype(
            jnp.float32
        )
    return (mixed.astype(jnp.bfloat16), hessian_rows[None])


BOTH = ("expert", "mp")
VMEM = pl.BlockSpec(memory_space=pltpu.VMEM)
SMEM = pl.BlockSpec(memory_space=pltpu.SMEM)
ANY = pl.BlockSpec(memory_space=pl.ANY)
F32 = jnp.float32
BF16 = jnp.bfloat16


def swap_cores(value):
    return lax.ppermute(value, "mp", [(m, m ^ 1) for m in range(4)])


def to_chips(value, k):
    pairs = [(4 * z + m, 4 * (z ^ k) + (m ^ 2 * (m & 1))) for z in range(4) for m in range(4)]
    return lax.ppermute(value, BOTH, pairs)


def across(value):
    return lax.ppermute(value, BOTH, [(4 * z + m, 4 * z + (m ^ 2)) for z in range(4) for m in range(4)])


def earlier_kernel(out_ref):
    row, column = (lax.broadcasted_iota(jnp.int32, out_ref.shape, i) for i in range(2))
    out_ref[...] = jnp.where(row < column, 1.0, 0.0).astype(BF16)


def route_kernel(capacity, earlier_ref, ids_ref, weights_ref, tokens_ref, rows_ref, cross_ref, count_ref, coef_ref):
    z = lax.axis_index("expert")
    ids, weights = ids_ref[...], weights_ref[...]
    rows = ids.shape[1]
    live, weight = [], []
    for k in range(4):
        hit = ids == (z ^ k)
        live.append(jnp.sum(jnp.where(hit, 1.0, 0.0), axis=0, keepdims=True))
        weight.append(jnp.sum(jnp.where(hit, weights, 0.0), axis=0, keepdims=True))
    position = jnp.dot(
        jnp.concatenate(live, axis=0).astype(BF16),
        earlier_ref[...],
        preferred_element_type=F32,
    )
    slot = lax.broadcasted_iota(jnp.int32, (capacity, rows), 0).astype(F32)
    chosen = []
    for k in range(4):
        kept = (live[k] > 0.5) & (position[k : k + 1] == slot)
        one = jnp.where(kept, 1.0, 0.0)
        chosen.append(one)
        coef_ref[capacity * k : capacity * (k + 1), :] = one * weight[k]
        total = jnp.minimum(jnp.sum(live[k], axis=1, keepdims=True), float(capacity))
        count_ref[k] = jnp.broadcast_to(total, count_ref.shape[1:]).astype(BF16)
    picked = jnp.dot(
        jnp.concatenate(chosen, axis=0).astype(BF16), tokens_ref[...], preferred_element_type=F32
    ).astype(BF16)
    rows_ref[...] = picked.reshape(rows_ref.shape)
    cross_ref[...] = jnp.zeros_like(cross_ref)
    cross_ref[:, : picked.shape[1]] = picked[:capacity]


def spread_kernel(*refs):
    for scale_ref, out_ref in zip(refs[:3], refs[3:]):
        for at in range(scale_ref.shape[1]):
            for i in range(2):
                out_ref[i : i + 1, at * QBLK : (at + 1) * QBLK] = jnp.full((1, QBLK), scale_ref[i, at], F32)


def line_up_kernel(own_ref, other_ref, count_ref, *out_refs):
    for k, out_ref in enumerate(out_refs, 1):
        out_ref[...] = jnp.concatenate([own_ref[k], other_ref[k], count_ref[k]], axis=1)


def on_core(core):
    return (lax.axis_index("mp") % 2 == core).astype(F32)


def collect_kernel(own_ref, other_ref, count_ref, crossed_ref, swapped_ref, three_ref, two_ref, one_ref, _, out_ref, counts_ref):
    rows, width = crossed_ref.shape[0], out_ref.shape[1] // 2
    zero = on_core(0)
    for ref, far_ref, lanes in ((own_ref, crossed_ref, slice(0, width)), (other_ref, swapped_ref, slice(width, 2 * width))):
        value = ref[0].astype(F32) * zero + far_ref[:, :width].astype(F32) * (1.0 - zero)
        out_ref[:rows, lanes] = value.astype(BF16)
    counts_ref[:rows, :] = count_ref[0]
    for k, ref in enumerate((one_ref, two_ref, three_ref), 1):
        out_ref[k * rows : (k + 1) * rows, :] = ref[:, : 2 * width]
        counts_ref[k * rows : (k + 1) * rows, :] = ref[:, 2 * width :]


def shares_in_order():
    m = lax.axis_index("mp")
    first = m ^ (2 * (m % 2))
    return (first, first ^ 1, first ^ 3, first ^ 2)


def project(x, share, weight_ref, scale_ref):
    width = x.shape[1]
    depth = pl.ds(pl.multiple_of(share * width, width), width)
    scaled = jnp.concatenate([(x * scale_ref[i : i + 1, depth]).astype(BF16) for i in range(2)], axis=0)
    return jnp.dot(scaled, weight_ref[depth, :], preferred_element_type=F32)


def near_kernel(x_ref, gate_ref, up_ref, gate_scale_ref, up_scale_ref, _, gate_out_ref, up_out_ref):
    width = x_ref.shape[1] // 2
    gate, up = 0.0, 0.0
    for part, share in enumerate(shares_in_order()[:2]):
        x = x_ref[:, part * width : (part + 1) * width].astype(F32)
        gate += project(x, share, gate_ref, gate_scale_ref)
        up += project(x, share, up_ref, up_scale_ref)
    gate_out_ref[...] = gate
    up_out_ref[...] = up


def hidden_kernel(
    x_ref,
    near_gate_ref,
    near_up_ref,
    gate_ref,
    up_ref,
    down_ref,
    gate_scale_ref,
    up_scale_ref,
    down_scale_ref,
    send_ref,
    hidden_ref,
):
    shares = shares_in_order()
    slots, half = near_gate_ref.shape[0] // 2, gate_ref.shape[1] // 2
    width = x_ref.shape[1] // 2
    gate, up = near_gate_ref[...], near_up_ref[...]
    for part, share in enumerate(shares[2:]):
        x = x_ref[:, part * width : (part + 1) * width].astype(F32)
        gate += project(x, share, gate_ref, gate_scale_ref)
        up += project(x, share, up_ref, up_scale_ref)
    parts = []
    for i in range(2):
        g = gate[i * slots : (i + 1) * slots, i * half : (i + 1) * half]
        u = up[i * slots : (i + 1) * slots, i * half : (i + 1) * half]
        parts.append((g / (1.0 + jnp.exp(-g)) * u).astype(BF16))
        lanes = slice(i * half, (i + 1) * half)
        hidden_ref[:, lanes] = parts[i]
        send_ref[:, 2 * width + i * half : 2 * width + (i + 1) * half] = parts[i]
    project_down(hidden_ref, shares[2:], down_ref, down_scale_ref, send_ref)


def project_down(hidden_ref, shares, down_ref, scale_ref, out_ref):
    slots, half, width = hidden_ref.shape[0], hidden_ref.shape[1] // 2, down_ref.shape[1] // 4
    parts = (hidden_ref[:, :half], hidden_ref[:, half:])
    none = jnp.zeros_like(parts[0])
    stacked = jnp.concatenate(
        [jnp.concatenate([parts[0], none], axis=1), jnp.concatenate([none, parts[1]], axis=1)], axis=0
    )
    for part, share in enumerate(shares):
        lanes = pl.ds(pl.multiple_of(share * width, width), width)
        both = jnp.dot(stacked, down_ref[:, lanes], preferred_element_type=F32)
        value = both[:slots] * scale_ref[:1, lanes] + both[slots:] * scale_ref[1:, lanes]
        out_ref[:, part * width : (part + 1) * width] = value.astype(BF16)


def keep_kernel(hidden_ref, send_ref, down_ref, down_scale_ref, keep_ref, cross_ref):
    project_down(hidden_ref, shares_in_order()[:2], down_ref, down_scale_ref, keep_ref)
    rows, width = cross_ref.shape[0], down_ref.shape[1] // 4
    zero = on_core(0)
    for part in range(2):
        lanes, turned = slice(part * width, (part + 1) * width), slice((1 - part) * width, (2 - part) * width)
        value = send_ref[:rows, turned].astype(F32) * zero + keep_ref[:rows, lanes].astype(F32) * (1.0 - zero)
        cross_ref[:, lanes] = value.astype(BF16)
    for k in range(4):
        into = 2 * width + k * hidden_ref.shape[1]
        cross_ref[:, into : into + hidden_ref.shape[1]] = hidden_ref[k * rows : (k + 1) * rows, :]


def chip_sum_kernel(keep_ref, sent_ref, *out_refs):
    rows, width = out_refs[0].shape
    for k, out_ref in enumerate(out_refs):
        at = slice(k * rows, (k + 1) * rows)
        out_ref[...] = (keep_ref[at, :].astype(F32) + sent_ref[at, :width].astype(F32)).astype(BF16)


def hessian_factor(count_ref):
    rows = count_ref.shape[0] // 4
    counts = [count_ref[k * rows : k * rows + 1, :].astype(F32)[:, :1] for k in range(4)]
    return 2.0 / (counts[0] + counts[1] + counts[2] + counts[3])


def hessian_block(own_ref, other, factor):
    return lax.dot_general(own_ref[...], other, (((0,), (0,)), ((), ())), preferred_element_type=F32) * factor


def hessian_kernel(count_ref, own_ref, sent_ref, crossed_ref, out_ref, far_ref):
    m = lax.axis_index("mp")
    width = out_ref.shape[0]
    rows = far_ref.shape[0] // 4
    start = crossed_ref.shape[1] - 4 * width
    for k in range(4):
        far_ref[k * rows : (k + 1) * rows, :] = crossed_ref[:, start + k * width : start + (k + 1) * width]
    factor = hessian_factor(count_ref)
    others = ((m, own_ref[...]), (m ^ 1, sent_ref[:, sent_ref.shape[1] - width :]), (m ^ 2, far_ref[...]))
    for share, other in others:
        out_ref[:, pl.ds(pl.multiple_of(share * width, width), width)] = hessian_block(own_ref, other, factor)


def collect_back_kernel(summed_ref, crossed_ref, three_ref, two_ref, one_ref, far_ref, mine_ref, other_ref):
    rows, width = one_ref.shape[0], mine_ref.shape[1]
    crossed = crossed_ref[:, : 2 * width].astype(F32)
    value = (crossed + summed_ref[...].astype(F32) * on_core(0)).astype(BF16)
    for k, rows_in in enumerate((value, one_ref[...], two_ref[...], three_ref[...])):
        mine_ref[k * rows : (k + 1) * rows, :] = rows_in[:, :width]
        other_ref[k * rows : (k + 1) * rows, :width] = rows_in[:, width:]
    other_ref[:, width:] = far_ref[...]


def combine_kernel(
    coef_ref, near_ref, far_ref, count_ref, own_ref, _, mixed_hbm, hessian_hbm, mixed_ref, block_ref, sems
):
    width, hidden_width = near_ref.shape[1], block_ref.shape[0]
    result = (near_ref[...].astype(F32) + far_ref[:, :width].astype(F32)).astype(BF16)
    coef = coef_ref[...]
    terms = []
    for _ in range(3):
        terms.append(coef.astype(BF16))
        coef = coef - terms[-1].astype(F32)
    out = lax.dot_general(
        jnp.concatenate(terms, axis=0),
        jnp.concatenate([result] * 3, axis=0),
        (((0,), (0,)), ((), ())),
        preferred_element_type=F32,
    )
    mixed_ref[...] = out.astype(BF16)
    mixed_copy = pltpu.make_async_copy(mixed_ref, mixed_hbm, sems.at[0])
    mixed_copy.start()
    block_ref[...] = hessian_block(own_ref, far_ref[:, width:], hessian_factor(count_ref))
    share = lax.axis_index("mp") ^ 3
    lanes = pl.ds(pl.multiple_of(share * hidden_width, hidden_width), hidden_width)
    block_copy = pltpu.make_async_copy(block_ref, hessian_hbm.at[:, lanes], sems.at[1])
    block_copy.start()
    mixed_copy.wait()
    block_copy.wait()


def on_device(
    tokens,
    route_ids,
    route_weights,
    gate_weight,
    gate_scale,
    up_weight,
    up_scale,
    down_weight,
    down_scale,
):
    rows, width = tokens.shape
    capacity = 2 * rows * TOP // ROUTED_ALL
    slots = 4 * capacity
    hidden_width = gate_weight.shape[2]
    shape = jax.ShapeDtypeStruct

    def call(kernel, name, outs, args, scalars=0, flops=0):
        single = not isinstance(outs, tuple)
        return pl.pallas_call(
            kernel,
            out_shape=outs,
            in_specs=[SMEM] * scalars + [VMEM] * (len(args) - scalars),
            out_specs=VMEM if single else (VMEM,) * len(outs),
            compiler_params=pltpu.CompilerParams(vmem_limit_bytes=8 * 1024 * 1024),
            cost_estimate=pl.CostEstimate(flops=flops, bytes_accessed=0, transcendentals=0) if flops else None,
            name=name,
        )(*args)

    earlier = call(earlier_kernel, "earlier", shape((rows, rows), BF16), (), flops=4 * 10**9)
    picked, cross, counts, coef = call(
        functools.partial(route_kernel, capacity),
        "route",
        (
            shape((4, capacity, width), BF16),
            shape((capacity, 2 * width + 2 * QBLK), BF16),
            shape((4, capacity, QBLK), BF16),
            shape((slots, rows), F32),
        ),
        (earlier, route_ids.T, route_weights.T, tokens),
        flops=10**11,
    )
    other = swap_cores(picked)
    crossed = across(cross)
    messages = call(
        line_up_kernel, "line_up", (shape((capacity, 2 * width + QBLK), BF16),) * 3, (picked, other, counts)
    )
    scales = call(
        spread_kernel,
        "spread",
        (shape((2, 4 * width), F32),) * 3,
        (gate_scale[0].T, up_scale[0].T, down_scale[0]),
        scalars=3,
    )
    gate, up, down = gate_weight[0], up_weight[0], down_weight[0]

    arrived, arrived_counts = call(
        collect_kernel,
        "collect",
        (shape((slots, 2 * width), BF16), shape((slots, QBLK), BF16)),
        (picked, other, counts, crossed, swap_cores(crossed[:, :width]), *[to_chips(messages[k - 1], k) for k in (3, 2, 1)], scales[0]),
    )
    swapped = swap_cores(arrived)
    near = call(
        near_kernel,
        "near",
        (shape((2 * slots, hidden_width), F32),) * 2,
        (arrived, gate, up, *scales[:2], down),
    )
    send, hidden = call(
        hidden_kernel,
        "hidden",
        (
            shape((slots, 2 * width + hidden_width), BF16),
            shape((slots, hidden_width), BF16),
        ),
        (swapped, *near, gate, up, down, *scales),
    )
    sent = swap_cores(send)
    keep, cross = call(
        keep_kernel,
        "keep",
        (shape((slots, 2 * width), BF16), shape((capacity, 2 * width + 4 * hidden_width), BF16)),
        (hidden, send, down, scales[2]),
    )
    crossed = across(cross)
    summed = call(chip_sum_kernel, "chip_sum", (shape((capacity, 2 * width), BF16),) * 4, (keep, sent))
    back = {k: to_chips(summed[k], k) for k in range(1, 4)}
    hessian, far = call(
        hessian_kernel,
        "hessian",
        (shape((hidden_width, 4 * hidden_width), F32), shape((slots, hidden_width), BF16)),
        (arrived_counts, hidden, sent, crossed),
    )
    mine, other = call(
        collect_back_kernel,
        "collect_back",
        (shape((slots, width), BF16), shape((slots, width + hidden_width), BF16)),
        (summed[0], crossed, *[back[k] for k in (3, 2, 1)], far),
    )
    mixed, hessian = pl.pallas_call(
        combine_kernel,
        out_shape=(shape((rows, width), BF16), shape((hidden_width, 4 * hidden_width), F32)),
        in_specs=[VMEM] * 5 + [ANY],
        out_specs=(ANY, ANY),
        scratch_shapes=[
            pltpu.VMEM((rows, width), BF16),
            pltpu.VMEM((hidden_width, hidden_width), F32),
            pltpu.SemaphoreType.DMA((2,)),
        ],
        input_output_aliases={5: 1},
        compiler_params=pltpu.CompilerParams(vmem_limit_bytes=8 * 1024 * 1024),
        name="combine",
    )(coef, mine, swap_cores(other), arrived_counts, hidden, hessian)
    return mixed, hessian[None]


def solution(mesh):
    placed = (
        P(("groups", "expert"), "mp"),
        P(("groups", "expert"), None),
        P(("groups", "expert"), None),
        P("expert", None, "mp"),
        P("expert", None, "mp"),
        P("expert", None, "mp"),
        P("expert", None, "mp"),
        P("expert", "mp", None),
        P("expert", "mp", None),
    )
    two_level = mesh.shape["expert"] == 4 and mesh.shape["mp"] == 4
    return jax.shard_map(
        on_device if two_level else on_device_any_mesh,
        mesh=mesh,
        in_specs=placed,
        out_specs=(P(("groups", "expert"), "mp"), P(("groups", "expert"), "mp", None)),
        check_vma=False,
    )
```

```python
import functools

import jax
import jax.numpy as jnp
from jax import lax
from jax.experimental import pallas as pl
from jax.experimental.pallas import tpu as pltpu
from jax.sharding import PartitionSpec as P

ROUTED_ALL = 256
TOP = 8
QBLK = 128


def dequant(weight, scale):
    row_blocks, col_blocks = scale.shape
    blocks = (
        weight.astype(jnp.float32).reshape(row_blocks, QBLK, col_blocks, QBLK)
        * scale[:, None, :, None]
    )
    return blocks.astype(jnp.bfloat16).reshape(weight.shape)


def route_slots(route_ids, experts, capacity):
    flat = route_ids.reshape(-1)
    onehot = (flat[:, None] == jnp.arange(experts, dtype=jnp.int32)[None, :]).astype(jnp.int32)
    position = jnp.sum((jnp.cumsum(onehot, axis=0) - 1) * onehot, axis=1)
    kept = (flat < experts) & (position < capacity)
    counts = jnp.minimum(jnp.sum(onehot, axis=0), capacity)
    targets = jnp.where(kept, flat * capacity + position, experts * capacity)
    return (targets.reshape(route_ids.shape), counts)


def on_device_any_mesh(
    tokens,
    route_ids,
    route_weights,
    gate_weight,
    gate_scale,
    up_weight,
    up_scale,
    down_weight,
    down_scale,
):
    experts = lax.axis_size("expert")
    capacity = 2 * route_ids.shape[0] * route_ids.shape[1] // ROUTED_ALL
    slot_total = experts * capacity
    targets, counts = route_slots(route_ids, experts, capacity)
    count_column = counts[:, None]
    gate_eff = dequant(gate_weight[0], gate_scale[0])
    up_eff = dequant(up_weight[0], up_scale[0])
    down_eff = dequant(down_weight[0], down_scale[0])
    token_count = route_ids.shape[0]
    source_index = jnp.full((slot_total + 1,), token_count, jnp.int32)
    source_index = source_index.at[targets.reshape(-1)].set(
        jnp.repeat(jnp.arange(token_count, dtype=jnp.int32), TOP)
    )
    source_index = source_index[:slot_total]
    features = lax.all_gather(tokens, "mp", axis=1, tiled=True)
    padded = jnp.concatenate([features, jnp.zeros((1, features.shape[1]), jnp.bfloat16)], axis=0)
    arrived = lax.all_to_all(
        padded[source_index].reshape(experts, capacity, features.shape[1]),
        "expert",
        split_axis=0,
        concat_axis=0,
        tiled=True,
    )
    arrived_counts = lax.all_to_all(count_column, "expert", split_axis=0, concat_axis=0, tiled=True)
    inputs = arrived.reshape(slot_total, features.shape[1])
    gate_proj = jnp.dot(inputs, gate_eff, preferred_element_type=jnp.float32)
    up_proj = jnp.dot(inputs, up_eff, preferred_element_type=jnp.float32)
    hidden = (jax.nn.silu(gate_proj) * up_proj).astype(jnp.bfloat16)
    row_total = jnp.sum(arrived_counts).astype(jnp.float32)
    hessian_rows = lax.dot_general(
        hidden,
        lax.all_gather(hidden, "mp", axis=1, tiled=True),
        (((0,), (0,)), ((), ())),
        preferred_element_type=jnp.float32,
    ) * (2.0 / row_total)
    partial_value = jnp.dot(hidden, down_eff, preferred_element_type=jnp.float32)
    summed = lax.psum_scatter(
        partial_value.astype(jnp.bfloat16), "mp", scatter_dimension=1, tiled=True
    )
    returned = lax.all_to_all(
        summed.reshape(experts, capacity, summed.shape[1]),
        "expert",
        split_axis=0,
        concat_axis=0,
        tiled=True,
    )
    width = returned.shape[2]
    flat_back = jnp.concatenate(
        [returned.reshape(slot_total, width), jnp.zeros((1, width), jnp.bfloat16)], axis=0
    )
    mixed = jnp.zeros((tokens.shape[0], width), jnp.float32)
    for route in range(TOP):
        mixed = mixed + route_weights[:, route : route + 1] * flat_back[targets[:, route]].astype(
            jnp.float32
        )
    return (mixed.astype(jnp.bfloat16), hessian_rows[None])


BOTH = ("expert", "mp")
VMEM = pl.BlockSpec(memory_space=pltpu.VMEM)
SMEM = pl.BlockSpec(memory_space=pltpu.SMEM)
ANY = pl.BlockSpec(memory_space=pl.ANY)
F32 = jnp.float32
BF16 = jnp.bfloat16


def swap_cores(value):
    return lax.ppermute(value, "mp", [(m, m ^ 1) for m in range(4)])


def to_chips(value, k):
    pairs = [(4 * z + m, 4 * (z ^ k) + (m ^ 2 * (m & 1))) for z in range(4) for m in range(4)]
    return lax.ppermute(value, BOTH, pairs)


def across(value):
    return lax.ppermute(value, BOTH, [(4 * z + m, 4 * z + (m ^ 2)) for z in range(4) for m in range(4)])


def earlier_kernel(out_ref):
    row, column = (lax.broadcasted_iota(jnp.int32, out_ref.shape, i) for i in range(2))
    out_ref[...] = jnp.where(row < column, 1.0, 0.0).astype(BF16)


def pick(chosen_ref, tokens_ref):
    return jnp.dot(chosen_ref[...], tokens_ref[...], preferred_element_type=F32).astype(BF16)


def route_kernel(capacity, earlier_ref, ids_ref, weights_ref, tokens_ref, chosen_ref, rows_ref, cross_ref, count_ref, coef_ref):
    z = lax.axis_index("expert")
    ids, weights = ids_ref[...], weights_ref[...]
    rows = ids.shape[1]
    live, weight = [], []
    for k in range(4):
        hit = ids == (z ^ k)
        live.append(jnp.sum(jnp.where(hit, 1.0, 0.0), axis=0, keepdims=True))
        weight.append(jnp.sum(jnp.where(hit, weights, 0.0), axis=0, keepdims=True))
    position = jnp.dot(
        jnp.concatenate(live, axis=0).astype(BF16),
        earlier_ref[...],
        preferred_element_type=F32,
    )
    slot = lax.broadcasted_iota(jnp.int32, (capacity, rows), 0).astype(F32)
    chosen = []
    for k in range(4):
        kept = (live[k] > 0.5) & (position[k : k + 1] == slot)
        one = jnp.where(kept, 1.0, 0.0)
        chosen.append(one)
        coef_ref[capacity * k : capacity * (k + 1), :] = one * weight[k]
        total = jnp.minimum(jnp.sum(live[k], axis=1, keepdims=True), float(capacity))
        count_ref[k] = jnp.broadcast_to(total, count_ref.shape[1:]).astype(BF16)
    chosen_ref[...] = jnp.concatenate(chosen, axis=0).astype(BF16)
    picked = pick(chosen_ref, tokens_ref)
    rows_ref[...] = picked.reshape(rows_ref.shape)
    cross_ref[...] = jnp.zeros_like(cross_ref)
    cross_ref[:, : picked.shape[1]] = picked[:capacity]


def spread_kernel(*refs):
    for scale_ref, out_ref in zip(refs[:3], refs[3:]):
        for at in range(scale_ref.shape[1]):
            for i in range(2):
                out_ref[i : i + 1, at * QBLK : (at + 1) * QBLK] = jnp.full((1, QBLK), scale_ref[i, at], F32)


def line_up_kernel(chosen_ref, tokens_ref, own_ref, count_ref, other_ref, *out_refs):
    rows = other_ref.shape[0]
    other = pick(chosen_ref, tokens_ref)
    other_ref[...] = other[:rows]
    for k, out_ref in enumerate(out_refs, 1):
        out_ref[...] = jnp.concatenate([own_ref[k], other[k * rows : (k + 1) * rows], count_ref[k]], axis=1)


def on_core(core):
    return (lax.axis_index("mp") % 2 == core).astype(F32)


def collect_kernel(own_ref, other_ref, count_ref, crossed_ref, swapped_ref, three_ref, two_ref, one_ref, _, out_ref, counts_ref):
    rows, width = crossed_ref.shape[0], out_ref.shape[1] // 2
    zero = on_core(0)
    for own, far_ref, lanes in (
        (own_ref[0], crossed_ref, slice(0, width)),
        (other_ref[...], swapped_ref, slice(width, 2 * width)),
    ):
        value = own.astype(F32) * zero + far_ref[:, :width].astype(F32) * (1.0 - zero)
        out_ref[:rows, lanes] = value.astype(BF16)
    counts_ref[:rows, :] = count_ref[0]
    for k, ref in enumerate((one_ref, two_ref, three_ref), 1):
        out_ref[k * rows : (k + 1) * rows, :] = ref[:, : 2 * width]
        counts_ref[k * rows : (k + 1) * rows, :] = ref[:, 2 * width :]


def shares_in_order():
    m = lax.axis_index("mp")
    first = m ^ (2 * (m % 2))
    return (first, first ^ 1, first ^ 3, first ^ 2)


def project(x, share, weight_ref, scale_ref):
    width = x.shape[1]
    depth = pl.ds(pl.multiple_of(share * width, width), width)
    scaled = jnp.concatenate([(x * scale_ref[i : i + 1, depth]).astype(BF16) for i in range(2)], axis=0)
    return jnp.dot(scaled, weight_ref[depth, :], preferred_element_type=F32)


def near_kernel(x_ref, gate_ref, up_ref, gate_scale_ref, up_scale_ref, _, gate_out_ref, up_out_ref):
    width = x_ref.shape[1] // 2
    gate, up = 0.0, 0.0
    for part, share in enumerate(shares_in_order()[:2]):
        x = x_ref[:, part * width : (part + 1) * width].astype(F32)
        gate += project(x, share, gate_ref, gate_scale_ref)
        up += project(x, share, up_ref, up_scale_ref)
    gate_out_ref[...] = gate
    up_out_ref[...] = up


def hidden_kernel(
    x_ref,
    near_gate_ref,
    near_up_ref,
    gate_ref,
    up_ref,
    down_ref,
    gate_scale_ref,
    up_scale_ref,
    down_scale_ref,
    send_ref,
    hidden_ref,
):
    shares = shares_in_order()
    slots, half = near_gate_ref.shape[0] // 2, gate_ref.shape[1] // 2
    width = x_ref.shape[1] // 2
    gate, up = near_gate_ref[...], near_up_ref[...]
    for part, share in enumerate(shares[2:]):
        x = x_ref[:, part * width : (part + 1) * width].astype(F32)
        gate += project(x, share, gate_ref, gate_scale_ref)
        up += project(x, share, up_ref, up_scale_ref)
    parts = []
    for i in range(2):
        g = gate[i * slots : (i + 1) * slots, i * half : (i + 1) * half]
        u = up[i * slots : (i + 1) * slots, i * half : (i + 1) * half]
        parts.append((g / (1.0 + jnp.exp(-g)) * u).astype(BF16))
        lanes = slice(i * half, (i + 1) * half)
        hidden_ref[:, lanes] = parts[i]
        send_ref[:, 2 * width + i * half : 2 * width + (i + 1) * half] = parts[i]
    project_down(hidden_ref, shares[2:], down_ref, down_scale_ref, send_ref)


def project_down(hidden_ref, shares, down_ref, scale_ref, out_ref):
    slots, half, width = hidden_ref.shape[0], hidden_ref.shape[1] // 2, down_ref.shape[1] // 4
    parts = (hidden_ref[:, :half], hidden_ref[:, half:])
    none = jnp.zeros_like(parts[0])
    stacked = jnp.concatenate(
        [jnp.concatenate([parts[0], none], axis=1), jnp.concatenate([none, parts[1]], axis=1)], axis=0
    )
    for part, share in enumerate(shares):
        lanes = pl.ds(pl.multiple_of(share * width, width), width)
        both = jnp.dot(stacked, down_ref[:, lanes], preferred_element_type=F32)
        value = both[:slots] * scale_ref[:1, lanes] + both[slots:] * scale_ref[1:, lanes]
        out_ref[:, part * width : (part + 1) * width] = value.astype(BF16)


def keep_kernel(hidden_ref, send_ref, down_ref, down_scale_ref, keep_ref, cross_ref):
    project_down(hidden_ref, shares_in_order()[:2], down_ref, down_scale_ref, keep_ref)
    rows, width = cross_ref.shape[0], down_ref.shape[1] // 4
    zero = on_core(0)
    for part in range(2):
        lanes, turned = slice(part * width, (part + 1) * width), slice((1 - part) * width, (2 - part) * width)
        value = send_ref[:rows, turned].astype(F32) * zero + keep_ref[:rows, lanes].astype(F32) * (1.0 - zero)
        cross_ref[:, lanes] = value.astype(BF16)
    for k in range(4):
        into = 2 * width + k * hidden_ref.shape[1]
        cross_ref[:, into : into + hidden_ref.shape[1]] = hidden_ref[k * rows : (k + 1) * rows, :]


def chip_sum_kernel(keep_ref, sent_ref, *out_refs):
    rows, width = out_refs[0].shape
    for k, out_ref in enumerate(out_refs):
        at = slice(k * rows, (k + 1) * rows)
        out_ref[...] = (keep_ref[at, :].astype(F32) + sent_ref[at, :width].astype(F32)).astype(BF16)


def hessian_factor(count_ref):
    rows = count_ref.shape[0] // 4
    counts = [count_ref[k * rows : k * rows + 1, :].astype(F32)[:, :1] for k in range(4)]
    return 2.0 / (counts[0] + counts[1] + counts[2] + counts[3])


def hessian_block(own_ref, other, factor):
    return lax.dot_general(own_ref[...], other, (((0,), (0,)), ((), ())), preferred_element_type=F32) * factor


def hessian_kernel(count_ref, own_ref, sent_ref, crossed_ref, out_ref, far_ref):
    m = lax.axis_index("mp")
    width = out_ref.shape[0]
    rows = far_ref.shape[0] // 4
    start = crossed_ref.shape[1] - 4 * width
    for k in range(4):
        far_ref[k * rows : (k + 1) * rows, :] = crossed_ref[:, start + k * width : start + (k + 1) * width]
    factor = hessian_factor(count_ref)
    others = ((m, own_ref[...]), (m ^ 1, sent_ref[:, sent_ref.shape[1] - width :]), (m ^ 2, far_ref[...]))
    for share, other in others:
        out_ref[:, pl.ds(pl.multiple_of(share * width, width), width)] = hessian_block(own_ref, other, factor)


def collect_back_kernel(summed_ref, crossed_ref, three_ref, two_ref, one_ref, far_ref, mine_ref, other_ref):
    rows, width = one_ref.shape[0], mine_ref.shape[1]
    crossed = crossed_ref[:, : 2 * width].astype(F32)
    value = (crossed + summed_ref[...].astype(F32) * on_core(0)).astype(BF16)
    for k, rows_in in enumerate((value, one_ref[...], two_ref[...], three_ref[...])):
        mine_ref[k * rows : (k + 1) * rows, :] = rows_in[:, :width]
        other_ref[k * rows : (k + 1) * rows, :width] = rows_in[:, width:]
    other_ref[:, width:] = far_ref[...]


def combine_kernel(
    coef_ref, near_ref, far_ref, count_ref, own_ref, _, mixed_hbm, hessian_hbm, mixed_ref, block_ref, sems
):
    width, hidden_width = near_ref.shape[1], block_ref.shape[0]
    result = (near_ref[...].astype(F32) + far_ref[:, :width].astype(F32)).astype(BF16)
    coef = coef_ref[...]
    terms = []
    for _ in range(3):
        terms.append(coef.astype(BF16))
        coef = coef - terms[-1].astype(F32)
    out = lax.dot_general(
        jnp.concatenate(terms, axis=0),
        jnp.concatenate([result] * 3, axis=0),
        (((0,), (0,)), ((), ())),
        preferred_element_type=F32,
    )
    mixed_ref[...] = out.astype(BF16)
    mixed_copy = pltpu.make_async_copy(mixed_ref, mixed_hbm, sems.at[0])
    mixed_copy.start()
    block_ref[...] = hessian_block(own_ref, far_ref[:, width:], hessian_factor(count_ref))
    share = lax.axis_index("mp") ^ 3
    lanes = pl.ds(pl.multiple_of(share * hidden_width, hidden_width), hidden_width)
    block_copy = pltpu.make_async_copy(block_ref, hessian_hbm.at[:, lanes], sems.at[1])
    block_copy.start()
    mixed_copy.wait()
    block_copy.wait()


def on_device(
    tokens,
    route_ids,
    route_weights,
    gate_weight,
    gate_scale,
    up_weight,
    up_scale,
    down_weight,
    down_scale,
):
    rows, width = tokens.shape
    capacity = 2 * rows * TOP // ROUTED_ALL
    slots = 4 * capacity
    hidden_width = gate_weight.shape[2]
    shape = jax.ShapeDtypeStruct

    def call(kernel, name, outs, args, scalars=0, flops=0):
        single = not isinstance(outs, tuple)
        return pl.pallas_call(
            kernel,
            out_shape=outs,
            in_specs=[SMEM] * scalars + [VMEM] * (len(args) - scalars),
            out_specs=VMEM if single else (VMEM,) * len(outs),
            compiler_params=pltpu.CompilerParams(vmem_limit_bytes=8 * 1024 * 1024),
            cost_estimate=pl.CostEstimate(flops=flops, bytes_accessed=0, transcendentals=0) if flops else None,
            name=name,
        )(*args)

    earlier = call(earlier_kernel, "earlier", shape((rows, rows), BF16), (), flops=4 * 10**9)
    other_tokens = swap_cores(tokens)
    chosen, picked, cross, counts, coef = call(
        functools.partial(route_kernel, capacity),
        "route",
        (
            shape((slots, rows), BF16),
            shape((4, capacity, width), BF16),
            shape((capacity, 2 * width + 2 * QBLK), BF16),
            shape((4, capacity, QBLK), BF16),
            shape((slots, rows), F32),
        ),
        (earlier, route_ids.T, route_weights.T, tokens),
        flops=10**11,
    )
    crossed = across(cross)
    other, *messages = call(
        line_up_kernel,
        "line_up",
        (shape((capacity, width), BF16), *[shape((capacity, 2 * width + QBLK), BF16)] * 3),
        (chosen, other_tokens, picked, counts),
    )
    scales = call(
        spread_kernel,
        "spread",
        (shape((2, 4 * width), F32),) * 3,
        (gate_scale[0].T, up_scale[0].T, down_scale[0]),
        scalars=3,
    )
    gate, up, down = gate_weight[0], up_weight[0], down_weight[0]

    arrived, arrived_counts = call(
        collect_kernel,
        "collect",
        (shape((slots, 2 * width), BF16), shape((slots, QBLK), BF16)),
        (picked, other, counts, crossed, swap_cores(crossed[:, :width]), *[to_chips(messages[k - 1], k) for k in (3, 2, 1)], scales[0]),
    )
    swapped = swap_cores(arrived)
    near = call(
        near_kernel,
        "near",
        (shape((2 * slots, hidden_width), F32),) * 2,
        (arrived, gate, up, *scales[:2], down),
    )
    send, hidden = call(
        hidden_kernel,
        "hidden",
        (
            shape((slots, 2 * width + hidden_width), BF16),
            shape((slots, hidden_width), BF16),
        ),
        (swapped, *near, gate, up, down, *scales),
    )
    sent = swap_cores(send)
    keep, cross = call(
        keep_kernel,
        "keep",
        (shape((slots, 2 * width), BF16), shape((capacity, 2 * width + 4 * hidden_width), BF16)),
        (hidden, send, down, scales[2]),
    )
    crossed = across(cross)
    summed = call(chip_sum_kernel, "chip_sum", (shape((capacity, 2 * width), BF16),) * 4, (keep, sent))
    back = {k: to_chips(summed[k], k) for k in range(1, 4)}
    hessian, far = call(
        hessian_kernel,
        "hessian",
        (shape((hidden_width, 4 * hidden_width), F32), shape((slots, hidden_width), BF16)),
        (arrived_counts, hidden, sent, crossed),
    )
    mine, other = call(
        collect_back_kernel,
        "collect_back",
        (shape((slots, width), BF16), shape((slots, width + hidden_width), BF16)),
        (summed[0], crossed, *[back[k] for k in (3, 2, 1)], far),
    )
    mixed, hessian = pl.pallas_call(
        combine_kernel,
        out_shape=(shape((rows, width), BF16), shape((hidden_width, 4 * hidden_width), F32)),
        in_specs=[VMEM] * 5 + [ANY],
        out_specs=(ANY, ANY),
        scratch_shapes=[
            pltpu.VMEM((rows, width), BF16),
            pltpu.VMEM((hidden_width, hidden_width), F32),
            pltpu.SemaphoreType.DMA((2,)),
        ],
        input_output_aliases={5: 1},
        compiler_params=pltpu.CompilerParams(vmem_limit_bytes=8 * 1024 * 1024),
        name="combine",
    )(coef, mine, swap_cores(other), arrived_counts, hidden, hessian)
    return mixed, hessian[None]


def solution(mesh):
    placed = (
        P(("groups", "expert"), "mp"),
        P(("groups", "expert"), None),
        P(("groups", "expert"), None),
        P("expert", None, "mp"),
        P("expert", None, "mp"),
        P("expert", None, "mp"),
        P("expert", None, "mp"),
        P("expert", "mp", None),
        P("expert", "mp", None),
    )
    two_level = mesh.shape["expert"] == 4 and mesh.shape["mp"] == 4
    return jax.shard_map(
        on_device if two_level else on_device_any_mesh,
        mesh=mesh,
        in_specs=placed,
        out_specs=(P(("groups", "expert"), "mp"), P(("groups", "expert"), "mp", None)),
        check_vma=False,
    )
```

```python
import functools

import jax
import jax.numpy as jnp
from jax import lax
from jax.experimental import pallas as pl
from jax.experimental.pallas import tpu as pltpu
from jax.sharding import PartitionSpec as P

ROUTED_ALL = 256
TOP = 8
QBLK = 128


def dequant(weight, scale):
    row_blocks, col_blocks = scale.shape
    blocks = (
        weight.astype(jnp.float32).reshape(row_blocks, QBLK, col_blocks, QBLK)
        * scale[:, None, :, None]
    )
    return blocks.astype(jnp.bfloat16).reshape(weight.shape)


def route_slots(route_ids, experts, capacity):
    flat = route_ids.reshape(-1)
    onehot = (flat[:, None] == jnp.arange(experts, dtype=jnp.int32)[None, :]).astype(jnp.int32)
    position = jnp.sum((jnp.cumsum(onehot, axis=0) - 1) * onehot, axis=1)
    kept = (flat < experts) & (position < capacity)
    counts = jnp.minimum(jnp.sum(onehot, axis=0), capacity)
    targets = jnp.where(kept, flat * capacity + position, experts * capacity)
    return (targets.reshape(route_ids.shape), counts)


def on_device_any_mesh(
    tokens,
    route_ids,
    route_weights,
    gate_weight,
    gate_scale,
    up_weight,
    up_scale,
    down_weight,
    down_scale,
):
    experts = lax.axis_size("expert")
    capacity = 2 * route_ids.shape[0] * route_ids.shape[1] // ROUTED_ALL
    slot_total = experts * capacity
    targets, counts = route_slots(route_ids, experts, capacity)
    count_column = counts[:, None]
    gate_eff = dequant(gate_weight[0], gate_scale[0])
    up_eff = dequant(up_weight[0], up_scale[0])
    down_eff = dequant(down_weight[0], down_scale[0])
    token_count = route_ids.shape[0]
    source_index = jnp.full((slot_total + 1,), token_count, jnp.int32)
    source_index = source_index.at[targets.reshape(-1)].set(
        jnp.repeat(jnp.arange(token_count, dtype=jnp.int32), TOP)
    )
    source_index = source_index[:slot_total]
    features = lax.all_gather(tokens, "mp", axis=1, tiled=True)
    padded = jnp.concatenate([features, jnp.zeros((1, features.shape[1]), jnp.bfloat16)], axis=0)
    arrived = lax.all_to_all(
        padded[source_index].reshape(experts, capacity, features.shape[1]),
        "expert",
        split_axis=0,
        concat_axis=0,
        tiled=True,
    )
    arrived_counts = lax.all_to_all(count_column, "expert", split_axis=0, concat_axis=0, tiled=True)
    inputs = arrived.reshape(slot_total, features.shape[1])
    gate_proj = jnp.dot(inputs, gate_eff, preferred_element_type=jnp.float32)
    up_proj = jnp.dot(inputs, up_eff, preferred_element_type=jnp.float32)
    hidden = (jax.nn.silu(gate_proj) * up_proj).astype(jnp.bfloat16)
    row_total = jnp.sum(arrived_counts).astype(jnp.float32)
    hessian_rows = lax.dot_general(
        hidden,
        lax.all_gather(hidden, "mp", axis=1, tiled=True),
        (((0,), (0,)), ((), ())),
        preferred_element_type=jnp.float32,
    ) * (2.0 / row_total)
    partial_value = jnp.dot(hidden, down_eff, preferred_element_type=jnp.float32)
    summed = lax.psum_scatter(
        partial_value.astype(jnp.bfloat16), "mp", scatter_dimension=1, tiled=True
    )
    returned = lax.all_to_all(
        summed.reshape(experts, capacity, summed.shape[1]),
        "expert",
        split_axis=0,
        concat_axis=0,
        tiled=True,
    )
    width = returned.shape[2]
    flat_back = jnp.concatenate(
        [returned.reshape(slot_total, width), jnp.zeros((1, width), jnp.bfloat16)], axis=0
    )
    mixed = jnp.zeros((tokens.shape[0], width), jnp.float32)
    for route in range(TOP):
        mixed = mixed + route_weights[:, route : route + 1] * flat_back[targets[:, route]].astype(
            jnp.float32
        )
    return (mixed.astype(jnp.bfloat16), hessian_rows[None])


BOTH = ("expert", "mp")
VMEM = pl.BlockSpec(memory_space=pltpu.VMEM)
SMEM = pl.BlockSpec(memory_space=pltpu.SMEM)
ANY = pl.BlockSpec(memory_space=pl.ANY)
F32 = jnp.float32
BF16 = jnp.bfloat16


def swap_cores(value):
    return lax.ppermute(value, "mp", [(m, m ^ 1) for m in range(4)])


def to_chips(value, k):
    pairs = [(4 * z + m, 4 * (z ^ k) + (m ^ 2 * (m & 1))) for z in range(4) for m in range(4)]
    return lax.ppermute(value, BOTH, pairs)


def across(value):
    return lax.ppermute(value, BOTH, [(4 * z + m, 4 * z + (m ^ 2)) for z in range(4) for m in range(4)])


def earlier_kernel(out_ref):
    row, column = (lax.broadcasted_iota(jnp.int32, out_ref.shape, i) for i in range(2))
    out_ref[...] = jnp.where(row < column, 1.0, 0.0).astype(BF16)


def pick(chosen_ref, tokens_ref):
    return jnp.dot(chosen_ref[...], tokens_ref[...], preferred_element_type=F32).astype(BF16)


def route_kernel(capacity, earlier_ref, ids_ref, chosen_ref, count_ref):
    z = lax.axis_index("expert")
    ids = ids_ref[...]
    rows = ids.shape[1]
    live = [jnp.sum(jnp.where(ids == (z ^ k), 1.0, 0.0), axis=0, keepdims=True) for k in range(4)]
    position = jnp.dot(
        jnp.concatenate(live, axis=0).astype(BF16), earlier_ref[...], preferred_element_type=F32
    )
    slot = lax.broadcasted_iota(jnp.int32, (capacity, rows), 0).astype(F32)
    chosen = []
    for k in range(4):
        kept = (live[k] > 0.5) & (position[k : k + 1] == slot)
        chosen.append(jnp.where(kept, 1.0, 0.0))
        total = jnp.minimum(jnp.sum(live[k], axis=1, keepdims=True), float(capacity))
        count_ref[k] = jnp.broadcast_to(total, count_ref.shape[1:]).astype(BF16)
    chosen_ref[...] = jnp.concatenate(chosen, axis=0).astype(BF16)


def own_kernel(chosen_ref, tokens_ref, rows_ref, cross_ref):
    picked = pick(chosen_ref, tokens_ref)
    rows, width = rows_ref.shape[1:]
    rows_ref[...] = picked.reshape(rows_ref.shape)
    cross_ref[:, :width] = picked[:rows]
    cross_ref[:, width:] = jnp.zeros((rows, cross_ref.shape[1] - width), BF16)


def prepare_kernel(
    gate_scale_ref, up_scale_ref, down_scale_ref, ids_ref, weights_ref, chosen_ref, gate_out, up_out, down_out, coef_ref
):
    for scale_ref, out_ref in ((gate_scale_ref, gate_out), (up_scale_ref, up_out), (down_scale_ref, down_out)):
        for at in range(scale_ref.shape[1]):
            for i in range(2):
                out_ref[i : i + 1, at * QBLK : (at + 1) * QBLK] = jnp.full((1, QBLK), scale_ref[i, at], F32)
    z = lax.axis_index("expert")
    slots = chosen_ref.shape[0]
    capacity = slots // 4
    coef = []
    for k in range(4):
        weight = jnp.sum(jnp.where(ids_ref[...] == (z ^ k), weights_ref[...], 0.0), axis=0, keepdims=True)
        coef.append(chosen_ref[k * capacity : (k + 1) * capacity, :].astype(F32) * weight)
    coef = jnp.concatenate(coef, axis=0)
    terms = []
    for _ in range(3):
        terms.append(coef.astype(BF16).astype(F32))
        coef = coef - terms[-1]
    terms.append(jnp.zeros_like(coef))
    coef_ref[...] = jnp.concatenate(terms, axis=0).T.astype(BF16)


def line_up_kernel(chosen_ref, tokens_ref, own_ref, count_ref, other_ref, *out_refs):
    rows = other_ref.shape[0]
    other = pick(chosen_ref, tokens_ref)
    other_ref[...] = other[:rows]
    for k, out_ref in enumerate(out_refs, 1):
        out_ref[...] = jnp.concatenate([own_ref[k], other[k * rows : (k + 1) * rows], count_ref[k]], axis=1)


def on_core(core):
    return (lax.axis_index("mp") % 2 == core).astype(F32)


def collect_kernel(own_ref, other_ref, count_ref, crossed_ref, swapped_ref, three_ref, two_ref, one_ref, _, out_ref, counts_ref):
    rows, width = crossed_ref.shape[0], out_ref.shape[1] // 2
    zero = on_core(0)
    for own, far_ref, lanes in (
        (own_ref[0], crossed_ref, slice(0, width)),
        (other_ref[...], swapped_ref, slice(width, 2 * width)),
    ):
        value = own.astype(F32) * zero + far_ref[:, :width].astype(F32) * (1.0 - zero)
        out_ref[:rows, lanes] = value.astype(BF16)
    counts_ref[:rows, :] = count_ref[0]
    for k, ref in enumerate((one_ref, two_ref, three_ref), 1):
        out_ref[k * rows : (k + 1) * rows, :] = ref[:, : 2 * width]
        counts_ref[k * rows : (k + 1) * rows, :] = ref[:, 2 * width :]


def shares_in_order():
    m = lax.axis_index("mp")
    first = m ^ (2 * (m % 2))
    return (first, first ^ 1, first ^ 3, first ^ 2)


def project(x, share, weight_ref, scale_ref):
    width = x.shape[1]
    depth = pl.ds(pl.multiple_of(share * width, width), width)
    scaled = jnp.concatenate([(x * scale_ref[i : i + 1, depth]).astype(BF16) for i in range(2)], axis=0)
    return jnp.dot(scaled, weight_ref[depth, :], preferred_element_type=F32)


def near_kernel(x_ref, gate_ref, up_ref, gate_scale_ref, up_scale_ref, _, gate_out_ref, up_out_ref):
    width = x_ref.shape[1] // 2
    gate, up = 0.0, 0.0
    for part, share in enumerate(shares_in_order()[:2]):
        x = x_ref[:, part * width : (part + 1) * width].astype(F32)
        gate += project(x, share, gate_ref, gate_scale_ref)
        up += project(x, share, up_ref, up_scale_ref)
    gate_out_ref[...] = gate
    up_out_ref[...] = up


def hidden_kernel(
    x_ref,
    near_gate_ref,
    near_up_ref,
    gate_ref,
    up_ref,
    down_ref,
    gate_scale_ref,
    up_scale_ref,
    down_scale_ref,
    send_ref,
    hidden_ref,
):
    shares = shares_in_order()
    slots, half = near_gate_ref.shape[0] // 2, gate_ref.shape[1] // 2
    width = x_ref.shape[1] // 2
    gate, up = near_gate_ref[...], near_up_ref[...]
    for part, share in enumerate(shares[2:]):
        x = x_ref[:, part * width : (part + 1) * width].astype(F32)
        gate += project(x, share, gate_ref, gate_scale_ref)
        up += project(x, share, up_ref, up_scale_ref)
    parts = []
    for i in range(2):
        g = gate[i * slots : (i + 1) * slots, i * half : (i + 1) * half]
        u = up[i * slots : (i + 1) * slots, i * half : (i + 1) * half]
        parts.append((g / (1.0 + jnp.exp(-g)) * u).astype(BF16))
        lanes = slice(i * half, (i + 1) * half)
        hidden_ref[:, lanes] = parts[i]
        send_ref[:, 2 * width + i * half : 2 * width + (i + 1) * half] = parts[i]
    project_down(hidden_ref, shares[2:], down_ref, down_scale_ref, send_ref)


def project_down(hidden_ref, shares, down_ref, scale_ref, out_ref):
    slots, half, width = hidden_ref.shape[0], hidden_ref.shape[1] // 2, down_ref.shape[1] // 4
    parts = (hidden_ref[:, :half], hidden_ref[:, half:])
    none = jnp.zeros_like(parts[0])
    stacked = jnp.concatenate(
        [jnp.concatenate([parts[0], none], axis=1), jnp.concatenate([none, parts[1]], axis=1)], axis=0
    )
    for part, share in enumerate(shares):
        lanes = pl.ds(pl.multiple_of(share * width, width), width)
        both = jnp.dot(stacked, down_ref[:, lanes], preferred_element_type=F32)
        value = both[:slots] * scale_ref[:1, lanes] + both[slots:] * scale_ref[1:, lanes]
        out_ref[:, part * width : (part + 1) * width] = value.astype(BF16)


def keep_kernel(hidden_ref, send_ref, down_ref, down_scale_ref, keep_ref, cross_ref):
    project_down(hidden_ref, shares_in_order()[:2], down_ref, down_scale_ref, keep_ref)
    rows, width = cross_ref.shape[0], down_ref.shape[1] // 4
    zero = on_core(0)
    for part in range(2):
        lanes, turned = slice(part * width, (part + 1) * width), slice((1 - part) * width, (2 - part) * width)
        value = send_ref[:rows, turned].astype(F32) * zero + keep_ref[:rows, lanes].astype(F32) * (1.0 - zero)
        cross_ref[:, lanes] = value.astype(BF16)
    for k in range(4):
        into = 2 * width + k * hidden_ref.shape[1]
        cross_ref[:, into : into + hidden_ref.shape[1]] = hidden_ref[k * rows : (k + 1) * rows, :]


def chip_sum_kernel(keep_ref, sent_ref, *out_refs):
    rows, width = out_refs[0].shape
    for k, out_ref in enumerate(out_refs):
        at = slice(k * rows, (k + 1) * rows)
        out_ref[...] = (keep_ref[at, :].astype(F32) + sent_ref[at, :width].astype(F32)).astype(BF16)


def hessian_factor(count_ref):
    rows = count_ref.shape[0] // 4
    counts = [count_ref[k * rows : k * rows + 1, :].astype(F32)[:, :1] for k in range(4)]
    return 2.0 / (counts[0] + counts[1] + counts[2] + counts[3])


def hessian_kernel(count_ref, own_ref, sent_ref, crossed_ref, out_ref, far_ref, turned_ref):
    m = lax.axis_index("mp")
    width = out_ref.shape[0]
    rows = far_ref.shape[0] // 4
    start = crossed_ref.shape[1] - 4 * width
    for k in range(4):
        far_ref[k * rows : (k + 1) * rows, :] = crossed_ref[:, start + k * width : start + (k + 1) * width]
    factor = hessian_factor(count_ref)
    turned_ref[...] = own_ref[...].astype(F32).T.astype(BF16)
    others = ((m, own_ref[...]), (m ^ 1, sent_ref[:, sent_ref.shape[1] - width :]), (m ^ 2, far_ref[...]))
    for share, other in others:
        block = jnp.dot(turned_ref[...], other, preferred_element_type=F32) * factor
        out_ref[:, pl.ds(pl.multiple_of(share * width, width), width)] = block


def collect_back_kernel(summed_ref, crossed_ref, three_ref, two_ref, one_ref, far_ref, mine_ref, other_ref):
    rows, width = one_ref.shape[0], mine_ref.shape[1]
    crossed = crossed_ref[:, : 2 * width].astype(F32)
    value = (crossed + summed_ref[...].astype(F32) * on_core(0)).astype(BF16)
    for k, rows_in in enumerate((value, one_ref[...], two_ref[...], three_ref[...])):
        mine_ref[k * rows : (k + 1) * rows, :] = rows_in[:, :width]
        other_ref[k * rows : (k + 1) * rows, :width] = rows_in[:, width:]
    other_ref[:, width:] = far_ref[...]


def combine_kernel(
    coef_ref, near_ref, far_ref, count_ref, turned_ref, _, mixed_hbm, hessian_hbm, mixed_ref, block_ref, sems
):
    width, hidden_width = near_ref.shape[1], block_ref.shape[0]
    block = jnp.dot(turned_ref[...], far_ref[:, width:], preferred_element_type=F32)
    block_ref[...] = block * hessian_factor(count_ref)
    share = lax.axis_index("mp") ^ 3
    lanes = pl.ds(pl.multiple_of(share * hidden_width, hidden_width), hidden_width)
    block_copy = pltpu.make_async_copy(block_ref, hessian_hbm.at[:, lanes], sems.at[0])
    block_copy.start()
    result = (near_ref[...].astype(F32) + far_ref[:, :width].astype(F32)).astype(BF16)
    out = jnp.dot(coef_ref[...], jnp.concatenate([result] * 4, axis=0), preferred_element_type=F32)
    mixed_ref[...] = out.astype(BF16)
    mixed_copy = pltpu.make_async_copy(mixed_ref, mixed_hbm, sems.at[1])
    mixed_copy.start()
    block_copy.wait()
    mixed_copy.wait()


def on_device(
    tokens,
    route_ids,
    route_weights,
    gate_weight,
    gate_scale,
    up_weight,
    up_scale,
    down_weight,
    down_scale,
):
    rows, width = tokens.shape
    capacity = 2 * rows * TOP // ROUTED_ALL
    slots = 4 * capacity
    hidden_width = gate_weight.shape[2]
    shape = jax.ShapeDtypeStruct

    def call(kernel, name, outs, args, scalars=0, flops=0):
        single = not isinstance(outs, tuple)
        return pl.pallas_call(
            kernel,
            out_shape=outs,
            in_specs=[SMEM] * scalars + [VMEM] * (len(args) - scalars),
            out_specs=VMEM if single else (VMEM,) * len(outs),
            compiler_params=pltpu.CompilerParams(vmem_limit_bytes=8 * 1024 * 1024),
            cost_estimate=pl.CostEstimate(flops=flops, bytes_accessed=0, transcendentals=0) if flops else None,
            name=name,
        )(*args)

    earlier = call(earlier_kernel, "earlier", shape((rows, rows), BF16), (), flops=4 * 10**9)
    other_tokens = swap_cores(tokens)
    chosen, counts = call(
        functools.partial(route_kernel, capacity),
        "route",
        (shape((slots, rows), BF16), shape((4, capacity, QBLK), BF16)),
        (earlier, route_ids.T),
    )
    picked, cross = call(
        own_kernel,
        "own",
        (shape((4, capacity, width), BF16), shape((capacity, 2 * width + 2 * QBLK), BF16)),
        (chosen, tokens),
        flops=10**11,
    )
    crossed = across(cross)
    other, *messages = call(
        line_up_kernel,
        "line_up",
        (shape((capacity, width), BF16), *[shape((capacity, 2 * width + QBLK), BF16)] * 3),
        (chosen, other_tokens, picked, counts),
    )
    *scales, coef = call(
        prepare_kernel,
        "prepare",
        (*[shape((2, 4 * width), F32)] * 3, shape((rows, 4 * slots), BF16)),
        (gate_scale[0].T, up_scale[0].T, down_scale[0], route_ids.T, route_weights.T, chosen),
        scalars=3,
    )
    gate, up, down = gate_weight[0], up_weight[0], down_weight[0]

    arrived, arrived_counts = call(
        collect_kernel,
        "collect",
        (shape((slots, 2 * width), BF16), shape((slots, QBLK), BF16)),
        (picked, other, counts, crossed, swap_cores(crossed[:, :width]), *[to_chips(messages[k - 1], k) for k in (3, 2, 1)], scales[0]),
    )
    swapped = swap_cores(arrived)
    near = call(
        near_kernel,
        "near",
        (shape((2 * slots, hidden_width), F32),) * 2,
        (arrived, gate, up, *scales[:2], down),
    )
    send, hidden = call(
        hidden_kernel,
        "hidden",
        (
            shape((slots, 2 * width + hidden_width), BF16),
            shape((slots, hidden_width), BF16),
        ),
        (swapped, *near, gate, up, down, *scales),
    )
    sent = swap_cores(send)
    keep, cross = call(
        keep_kernel,
        "keep",
        (shape((slots, 2 * width), BF16), shape((capacity, 2 * width + 4 * hidden_width), BF16)),
        (hidden, send, down, scales[2]),
    )
    crossed = across(cross)
    summed = call(chip_sum_kernel, "chip_sum", (shape((capacity, 2 * width), BF16),) * 4, (keep, sent))
    back = {k: to_chips(summed[k], k) for k in range(1, 4)}
    hessian, far, turned = call(
        hessian_kernel,
        "hessian",
        (
            shape((hidden_width, 4 * hidden_width), F32),
            shape((slots, hidden_width), BF16),
            shape((hidden_width, slots), BF16),
        ),
        (arrived_counts, hidden, sent, crossed),
    )
    mine, other = call(
        collect_back_kernel,
        "collect_back",
        (shape((slots, width), BF16), shape((slots, width + hidden_width), BF16)),
        (summed[0], crossed, *[back[k] for k in (3, 2, 1)], far),
    )
    mixed, hessian = pl.pallas_call(
        combine_kernel,
        out_shape=(shape((rows, width), BF16), shape((hidden_width, 4 * hidden_width), F32)),
        in_specs=[VMEM] * 5 + [ANY],
        out_specs=(ANY, ANY),
        scratch_shapes=[
            pltpu.VMEM((rows, width), BF16),
            pltpu.VMEM((hidden_width, hidden_width), F32),
            pltpu.SemaphoreType.DMA((2,)),
        ],
        input_output_aliases={5: 1},
        compiler_params=pltpu.CompilerParams(vmem_limit_bytes=8 * 1024 * 1024),
        name="combine",
    )(coef, mine, swap_cores(other), arrived_counts, turned, hessian)
    return mixed, hessian[None]


def solution(mesh):
    placed = (
        P(("groups", "expert"), "mp"),
        P(("groups", "expert"), None),
        P(("groups", "expert"), None),
        P("expert", None, "mp"),
        P("expert", None, "mp"),
        P("expert", None, "mp"),
        P("expert", None, "mp"),
        P("expert", "mp", None),
        P("expert", "mp", None),
    )
    two_level = mesh.shape["expert"] == 4 and mesh.shape["mp"] == 4
    return jax.shard_map(
        on_device if two_level else on_device_any_mesh,
        mesh=mesh,
        in_specs=placed,
        out_specs=(P(("groups", "expert"), "mp"), P(("groups", "expert"), "mp", None)),
        check_vma=False,
    )
```

```python
import functools

import jax
import jax.numpy as jnp
from jax import lax
from jax.experimental import pallas as pl
from jax.experimental.pallas import tpu as pltpu
from jax.sharding import PartitionSpec as P

ROUTED_ALL = 256
TOP = 8
QBLK = 128


def dequant(weight, scale):
    row_blocks, col_blocks = scale.shape
    blocks = (
        weight.astype(jnp.float32).reshape(row_blocks, QBLK, col_blocks, QBLK)
        * scale[:, None, :, None]
    )
    return blocks.astype(jnp.bfloat16).reshape(weight.shape)


def route_slots(route_ids, experts, capacity):
    flat = route_ids.reshape(-1)
    onehot = (flat[:, None] == jnp.arange(experts, dtype=jnp.int32)[None, :]).astype(jnp.int32)
    position = jnp.sum((jnp.cumsum(onehot, axis=0) - 1) * onehot, axis=1)
    kept = (flat < experts) & (position < capacity)
    counts = jnp.minimum(jnp.sum(onehot, axis=0), capacity)
    targets = jnp.where(kept, flat * capacity + position, experts * capacity)
    return (targets.reshape(route_ids.shape), counts)


def on_device_any_mesh(
    tokens,
    route_ids,
    route_weights,
    gate_weight,
    gate_scale,
    up_weight,
    up_scale,
    down_weight,
    down_scale,
):
    experts = lax.axis_size("expert")
    capacity = 2 * route_ids.shape[0] * route_ids.shape[1] // ROUTED_ALL
    slot_total = experts * capacity
    targets, counts = route_slots(route_ids, experts, capacity)
    count_column = counts[:, None]
    gate_eff = dequant(gate_weight[0], gate_scale[0])
    up_eff = dequant(up_weight[0], up_scale[0])
    down_eff = dequant(down_weight[0], down_scale[0])
    token_count = route_ids.shape[0]
    source_index = jnp.full((slot_total + 1,), token_count, jnp.int32)
    source_index = source_index.at[targets.reshape(-1)].set(
        jnp.repeat(jnp.arange(token_count, dtype=jnp.int32), TOP)
    )
    source_index = source_index[:slot_total]
    features = lax.all_gather(tokens, "mp", axis=1, tiled=True)
    padded = jnp.concatenate([features, jnp.zeros((1, features.shape[1]), jnp.bfloat16)], axis=0)
    arrived = lax.all_to_all(
        padded[source_index].reshape(experts, capacity, features.shape[1]),
        "expert",
        split_axis=0,
        concat_axis=0,
        tiled=True,
    )
    arrived_counts = lax.all_to_all(count_column, "expert", split_axis=0, concat_axis=0, tiled=True)
    inputs = arrived.reshape(slot_total, features.shape[1])
    gate_proj = jnp.dot(inputs, gate_eff, preferred_element_type=jnp.float32)
    up_proj = jnp.dot(inputs, up_eff, preferred_element_type=jnp.float32)
    hidden = (jax.nn.silu(gate_proj) * up_proj).astype(jnp.bfloat16)
    row_total = jnp.sum(arrived_counts).astype(jnp.float32)
    hessian_rows = lax.dot_general(
        hidden,
        lax.all_gather(hidden, "mp", axis=1, tiled=True),
        (((0,), (0,)), ((), ())),
        preferred_element_type=jnp.float32,
    ) * (2.0 / row_total)
    partial_value = jnp.dot(hidden, down_eff, preferred_element_type=jnp.float32)
    summed = lax.psum_scatter(
        partial_value.astype(jnp.bfloat16), "mp", scatter_dimension=1, tiled=True
    )
    returned = lax.all_to_all(
        summed.reshape(experts, capacity, summed.shape[1]),
        "expert",
        split_axis=0,
        concat_axis=0,
        tiled=True,
    )
    width = returned.shape[2]
    flat_back = jnp.concatenate(
        [returned.reshape(slot_total, width), jnp.zeros((1, width), jnp.bfloat16)], axis=0
    )
    mixed = jnp.zeros((tokens.shape[0], width), jnp.float32)
    for route in range(TOP):
        mixed = mixed + route_weights[:, route : route + 1] * flat_back[targets[:, route]].astype(
            jnp.float32
        )
    return (mixed.astype(jnp.bfloat16), hessian_rows[None])


BOTH = ("expert", "mp")
VMEM = pl.BlockSpec(memory_space=pltpu.VMEM)
SMEM = pl.BlockSpec(memory_space=pltpu.SMEM)
ANY = pl.BlockSpec(memory_space=pl.ANY)
F32 = jnp.float32
BF16 = jnp.bfloat16


def swap_cores(value):
    return lax.ppermute(value, "mp", [(m, m ^ 1) for m in range(4)])


def to_chips(value, k):
    pairs = [(4 * z + m, 4 * (z ^ k) + (m ^ 2 * (m & 1))) for z in range(4) for m in range(4)]
    return lax.ppermute(value, BOTH, pairs)


def across(value):
    return lax.ppermute(value, BOTH, [(4 * z + m, 4 * z + (m ^ 2)) for z in range(4) for m in range(4)])


def earlier_kernel(out_ref):
    row, column = (lax.broadcasted_iota(jnp.int32, out_ref.shape, i) for i in range(2))
    out_ref[...] = jnp.where(row < column, 1.0, 0.0).astype(BF16)


def pick(chosen_ref, tokens_ref):
    return jnp.dot(chosen_ref[...], tokens_ref[...], preferred_element_type=F32).astype(BF16)


def route_kernel(capacity, earlier_ref, ids_ref, chosen_ref, count_ref):
    z = lax.axis_index("expert")
    ids = ids_ref[...]
    rows = ids.shape[1]
    live = [jnp.sum(jnp.where(ids == (z ^ k), 1.0, 0.0), axis=0, keepdims=True) for k in range(4)]
    position = jnp.dot(
        jnp.concatenate(live, axis=0).astype(BF16), earlier_ref[...], preferred_element_type=F32
    )
    slot = lax.broadcasted_iota(jnp.int32, (capacity, rows), 0).astype(F32)
    chosen = []
    for k in range(4):
        kept = (live[k] > 0.5) & (position[k : k + 1] == slot)
        chosen.append(jnp.where(kept, 1.0, 0.0))
        total = jnp.minimum(jnp.sum(live[k], axis=1, keepdims=True), float(capacity))
        count_ref[k] = jnp.broadcast_to(total, count_ref.shape[1:]).astype(BF16)
    chosen_ref[...] = jnp.concatenate(chosen, axis=0).astype(BF16)


def own_kernel(chosen_ref, tokens_ref, rows_ref, cross_ref):
    picked = pick(chosen_ref, tokens_ref)
    rows, width = rows_ref.shape[1:]
    rows_ref[...] = picked.reshape(rows_ref.shape)
    cross_ref[:, :width] = picked[:rows]
    cross_ref[:, width:] = jnp.zeros((rows, cross_ref.shape[1] - width), BF16)


def prepare_kernel(
    gate_scale_ref, up_scale_ref, down_scale_ref, ids_ref, weights_ref, chosen_ref, gate_out, up_out, down_out, coef_ref
):
    for scale_ref, out_ref in ((gate_scale_ref, gate_out), (up_scale_ref, up_out), (down_scale_ref, down_out)):
        for at in range(scale_ref.shape[1]):
            for i in range(2):
                out_ref[i : i + 1, at * QBLK : (at + 1) * QBLK] = jnp.full((1, QBLK), scale_ref[i, at], F32)
    z = lax.axis_index("expert")
    slots = chosen_ref.shape[0]
    capacity = slots // 4
    coef = []
    for k in range(4):
        weight = jnp.sum(jnp.where(ids_ref[...] == (z ^ k), weights_ref[...], 0.0), axis=0, keepdims=True)
        coef.append(chosen_ref[k * capacity : (k + 1) * capacity, :].astype(F32) * weight)
    coef = jnp.concatenate(coef, axis=0)
    terms = []
    for _ in range(3):
        terms.append(coef.astype(BF16).astype(F32))
        coef = coef - terms[-1]
    terms.append(jnp.zeros_like(coef))
    coef_ref[...] = jnp.concatenate(terms, axis=0).T.astype(BF16)


def line_up_kernel(chosen_ref, tokens_ref, own_ref, count_ref, other_ref, *out_refs):
    rows = other_ref.shape[0]
    other = pick(chosen_ref, tokens_ref)
    other_ref[...] = other[:rows]
    for k, out_ref in enumerate(out_refs, 1):
        out_ref[...] = jnp.concatenate([own_ref[k], other[k * rows : (k + 1) * rows], count_ref[k]], axis=1)


def on_core(core):
    return (lax.axis_index("mp") % 2 == core).astype(F32)


def collect_kernel(own_ref, other_ref, count_ref, crossed_ref, swapped_ref, three_ref, two_ref, one_ref, _, out_ref, counts_ref):
    rows, width = crossed_ref.shape[0], out_ref.shape[1] // 2
    zero = on_core(0)
    for own, far_ref, lanes in (
        (own_ref[0], crossed_ref, slice(0, width)),
        (other_ref[...], swapped_ref, slice(width, 2 * width)),
    ):
        value = own.astype(F32) * zero + far_ref[:, :width].astype(F32) * (1.0 - zero)
        out_ref[:rows, lanes] = value.astype(BF16)
    counts_ref[:rows, :] = count_ref[0]
    for k, ref in enumerate((one_ref, two_ref, three_ref), 1):
        out_ref[k * rows : (k + 1) * rows, :] = ref[:, : 2 * width]
        counts_ref[k * rows : (k + 1) * rows, :] = ref[:, 2 * width :]


def shares_in_order():
    m = lax.axis_index("mp")
    first = m ^ (2 * (m % 2))
    return (first, first ^ 1, first ^ 3, first ^ 2)


def project(x, share, weight_ref, scale_ref):
    slots, width = x.shape
    depth = pl.ds(pl.multiple_of(share * width, width), width)
    terms = []
    for i in range(2):
        scaled = x * scale_ref[i : i + 1, depth]
        terms.append(scaled.astype(BF16))
        terms.append((scaled - terms[-1].astype(F32)).astype(BF16))
    out = jnp.dot(jnp.concatenate(terms, axis=0), weight_ref[depth, :], preferred_element_type=F32)
    return jnp.concatenate([out[:slots] + out[slots : 2 * slots], out[2 * slots : 3 * slots] + out[3 * slots :]], axis=0)


def near_kernel(x_ref, gate_ref, up_ref, gate_scale_ref, up_scale_ref, _, gate_out_ref, up_out_ref):
    width = x_ref.shape[1] // 2
    gate, up = 0.0, 0.0
    for part, share in enumerate(shares_in_order()[:2]):
        x = x_ref[:, part * width : (part + 1) * width].astype(F32)
        gate += project(x, share, gate_ref, gate_scale_ref)
        up += project(x, share, up_ref, up_scale_ref)
    gate_out_ref[...] = gate
    up_out_ref[...] = up


def hidden_kernel(
    x_ref,
    near_gate_ref,
    near_up_ref,
    gate_ref,
    up_ref,
    down_ref,
    gate_scale_ref,
    up_scale_ref,
    down_scale_ref,
    send_ref,
    hidden_ref,
):
    shares = shares_in_order()
    slots, half = near_gate_ref.shape[0] // 2, gate_ref.shape[1] // 2
    width = x_ref.shape[1] // 2
    gate, up = near_gate_ref[...], near_up_ref[...]
    for part, share in enumerate(shares[2:]):
        x = x_ref[:, part * width : (part + 1) * width].astype(F32)
        gate += project(x, share, gate_ref, gate_scale_ref)
        up += project(x, share, up_ref, up_scale_ref)
    parts = []
    for i in range(2):
        g = gate[i * slots : (i + 1) * slots, i * half : (i + 1) * half]
        u = up[i * slots : (i + 1) * slots, i * half : (i + 1) * half]
        parts.append((g / (1.0 + jnp.exp(-g)) * u).astype(BF16))
        lanes = slice(i * half, (i + 1) * half)
        hidden_ref[:, lanes] = parts[i]
        send_ref[:, 2 * width + i * half : 2 * width + (i + 1) * half] = parts[i]
    project_down(hidden_ref, shares[2:], down_ref, down_scale_ref, send_ref)


def project_down(hidden_ref, shares, down_ref, scale_ref, out_ref):
    slots, half, width = hidden_ref.shape[0], hidden_ref.shape[1] // 2, down_ref.shape[1] // 4
    parts = (hidden_ref[:, :half], hidden_ref[:, half:])
    none = jnp.zeros_like(parts[0])
    stacked = jnp.concatenate(
        [jnp.concatenate([parts[0], none], axis=1), jnp.concatenate([none, parts[1]], axis=1)], axis=0
    )
    for part, share in enumerate(shares):
        lanes = pl.ds(pl.multiple_of(share * width, width), width)
        both = jnp.dot(stacked, down_ref[:, lanes], preferred_element_type=F32)
        value = both[:slots] * scale_ref[:1, lanes] + both[slots:] * scale_ref[1:, lanes]
        out_ref[:, part * width : (part + 1) * width] = value.astype(BF16)


def keep_kernel(hidden_ref, send_ref, down_ref, down_scale_ref, keep_ref, cross_ref):
    project_down(hidden_ref, shares_in_order()[:2], down_ref, down_scale_ref, keep_ref)
    rows, width = cross_ref.shape[0], down_ref.shape[1] // 4
    zero = on_core(0)
    for part in range(2):
        lanes, turned = slice(part * width, (part + 1) * width), slice((1 - part) * width, (2 - part) * width)
        value = send_ref[:rows, turned].astype(F32) * zero + keep_ref[:rows, lanes].astype(F32) * (1.0 - zero)
        cross_ref[:, lanes] = value.astype(BF16)
    for k in range(4):
        into = 2 * width + k * hidden_ref.shape[1]
        cross_ref[:, into : into + hidden_ref.shape[1]] = hidden_ref[k * rows : (k + 1) * rows, :]


def chip_sum_kernel(keep_ref, sent_ref, *out_refs):
    rows, width = out_refs[0].shape
    for k, out_ref in enumerate(out_refs):
        at = slice(k * rows, (k + 1) * rows)
        out_ref[...] = (keep_ref[at, :].astype(F32) + sent_ref[at, :width].astype(F32)).astype(BF16)


def hessian_factor(count_ref):
    rows = count_ref.shape[0] // 4
    counts = [count_ref[k * rows : k * rows + 1, :].astype(F32)[:, :1] for k in range(4)]
    return 2.0 / (counts[0] + counts[1] + counts[2] + counts[3])


def hessian_kernel(count_ref, own_ref, sent_ref, crossed_ref, out_ref, far_ref, turned_ref):
    m = lax.axis_index("mp")
    width = out_ref.shape[0]
    rows = far_ref.shape[0] // 4
    start = crossed_ref.shape[1] - 4 * width
    for k in range(4):
        far_ref[k * rows : (k + 1) * rows, :] = crossed_ref[:, start + k * width : start + (k + 1) * width]
    factor = hessian_factor(count_ref)
    turned_ref[...] = own_ref[...].astype(F32).T.astype(BF16)
    others = ((m, own_ref[...]), (m ^ 1, sent_ref[:, sent_ref.shape[1] - width :]), (m ^ 2, far_ref[...]))
    for share, other in others:
        block = jnp.dot(turned_ref[...], other, preferred_element_type=F32) * factor
        out_ref[:, pl.ds(pl.multiple_of(share * width, width), width)] = block


def collect_back_kernel(summed_ref, crossed_ref, three_ref, two_ref, one_ref, far_ref, mine_ref, other_ref):
    rows, width = one_ref.shape[0], mine_ref.shape[1]
    crossed = crossed_ref[:, : 2 * width].astype(F32)
    value = (crossed + summed_ref[...].astype(F32) * on_core(0)).astype(BF16)
    for k, rows_in in enumerate((value, one_ref[...], two_ref[...], three_ref[...])):
        mine_ref[k * rows : (k + 1) * rows, :] = rows_in[:, :width]
        other_ref[k * rows : (k + 1) * rows, :width] = rows_in[:, width:]
    other_ref[:, width:] = far_ref[...]


def combine_kernel(
    coef_ref, near_ref, far_ref, count_ref, turned_ref, _, mixed_hbm, hessian_hbm, mixed_ref, block_ref, sems
):
    width, hidden_width = near_ref.shape[1], block_ref.shape[0]
    block = jnp.dot(turned_ref[...], far_ref[:, width:], preferred_element_type=F32)
    block_ref[...] = block * hessian_factor(count_ref)
    share = lax.axis_index("mp") ^ 3
    lanes = pl.ds(pl.multiple_of(share * hidden_width, hidden_width), hidden_width)
    block_copy = pltpu.make_async_copy(block_ref, hessian_hbm.at[:, lanes], sems.at[0])
    block_copy.start()
    result = (near_ref[...].astype(F32) + far_ref[:, :width].astype(F32)).astype(BF16)
    out = jnp.dot(coef_ref[...], jnp.concatenate([result] * 4, axis=0), preferred_element_type=F32)
    mixed_ref[...] = out.astype(BF16)
    mixed_copy = pltpu.make_async_copy(mixed_ref, mixed_hbm, sems.at[1])
    mixed_copy.start()
    block_copy.wait()
    mixed_copy.wait()


def on_device(
    tokens,
    route_ids,
    route_weights,
    gate_weight,
    gate_scale,
    up_weight,
    up_scale,
    down_weight,
    down_scale,
):
    rows, width = tokens.shape
    capacity = 2 * rows * TOP // ROUTED_ALL
    slots = 4 * capacity
    hidden_width = gate_weight.shape[2]
    shape = jax.ShapeDtypeStruct

    def call(kernel, name, outs, args, scalars=0, flops=0):
        single = not isinstance(outs, tuple)
        return pl.pallas_call(
            kernel,
            out_shape=outs,
            in_specs=[SMEM] * scalars + [VMEM] * (len(args) - scalars),
            out_specs=VMEM if single else (VMEM,) * len(outs),
            compiler_params=pltpu.CompilerParams(vmem_limit_bytes=8 * 1024 * 1024),
            cost_estimate=pl.CostEstimate(flops=flops, bytes_accessed=0, transcendentals=0) if flops else None,
            name=name,
        )(*args)

    earlier = call(earlier_kernel, "earlier", shape((rows, rows), BF16), (), flops=4 * 10**9)
    other_tokens = swap_cores(tokens)
    chosen, counts = call(
        functools.partial(route_kernel, capacity),
        "route",
        (shape((slots, rows), BF16), shape((4, capacity, QBLK), BF16)),
        (earlier, route_ids.T),
    )
    picked, cross = call(
        own_kernel,
        "own",
        (shape((4, capacity, width), BF16), shape((capacity, 2 * width + 2 * QBLK), BF16)),
        (chosen, tokens),
        flops=10**11,
    )
    crossed = across(cross)
    other, *messages = call(
        line_up_kernel,
        "line_up",
        (shape((capacity, width), BF16), *[shape((capacity, 2 * width + QBLK), BF16)] * 3),
        (chosen, other_tokens, picked, counts),
    )
    *scales, coef = call(
        prepare_kernel,
        "prepare",
        (*[shape((2, 4 * width), F32)] * 3, shape((rows, 4 * slots), BF16)),
        (gate_scale[0].T, up_scale[0].T, down_scale[0], route_ids.T, route_weights.T, chosen),
        scalars=3,
    )
    gate, up, down = gate_weight[0], up_weight[0], down_weight[0]

    arrived, arrived_counts = call(
        collect_kernel,
        "collect",
        (shape((slots, 2 * width), BF16), shape((slots, QBLK), BF16)),
        (picked, other, counts, crossed, swap_cores(crossed[:, :width]), *[to_chips(messages[k - 1], k) for k in (3, 2, 1)], scales[0]),
    )
    swapped = swap_cores(arrived)
    near = call(
        near_kernel,
        "near",
        (shape((2 * slots, hidden_width), F32),) * 2,
        (arrived, gate, up, *scales[:2], down),
    )
    send, hidden = call(
        hidden_kernel,
        "hidden",
        (
            shape((slots, 2 * width + hidden_width), BF16),
            shape((slots, hidden_width), BF16),
        ),
        (swapped, *near, gate, up, down, *scales),
    )
    sent = swap_cores(send)
    keep, cross = call(
        keep_kernel,
        "keep",
        (shape((slots, 2 * width), BF16), shape((capacity, 2 * width + 4 * hidden_width), BF16)),
        (hidden, send, down, scales[2]),
    )
    crossed = across(cross)
    summed = call(chip_sum_kernel, "chip_sum", (shape((capacity, 2 * width), BF16),) * 4, (keep, sent))
    back = {k: to_chips(summed[k], k) for k in range(1, 4)}
    hessian, far, turned = call(
        hessian_kernel,
        "hessian",
        (
            shape((hidden_width, 4 * hidden_width), F32),
            shape((slots, hidden_width), BF16),
            shape((hidden_width, slots), BF16),
        ),
        (arrived_counts, hidden, sent, crossed),
    )
    mine, other = call(
        collect_back_kernel,
        "collect_back",
        (shape((slots, width), BF16), shape((slots, width + hidden_width), BF16)),
        (summed[0], crossed, *[back[k] for k in (3, 2, 1)], far),
    )
    mixed, hessian = pl.pallas_call(
        combine_kernel,
        out_shape=(shape((rows, width), BF16), shape((hidden_width, 4 * hidden_width), F32)),
        in_specs=[VMEM] * 5 + [ANY],
        out_specs=(ANY, ANY),
        scratch_shapes=[
            pltpu.VMEM((rows, width), BF16),
            pltpu.VMEM((hidden_width, hidden_width), F32),
            pltpu.SemaphoreType.DMA((2,)),
        ],
        input_output_aliases={5: 1},
        compiler_params=pltpu.CompilerParams(vmem_limit_bytes=8 * 1024 * 1024),
        name="combine",
    )(coef, mine, swap_cores(other), arrived_counts, turned, hessian)
    return mixed, hessian[None]


def solution(mesh):
    placed = (
        P(("groups", "expert"), "mp"),
        P(("groups", "expert"), None),
        P(("groups", "expert"), None),
        P("expert", None, "mp"),
        P("expert", None, "mp"),
        P("expert", None, "mp"),
        P("expert", None, "mp"),
        P("expert", "mp", None),
        P("expert", "mp", None),
    )
    two_level = mesh.shape["expert"] == 4 and mesh.shape["mp"] == 4
    return jax.shard_map(
        on_device if two_level else on_device_any_mesh,
        mesh=mesh,
        in_specs=placed,
        out_specs=(P(("groups", "expert"), "mp"), P(("groups", "expert"), "mp", None)),
        check_vma=False,
    )
```

```python
import functools

import jax
import jax.numpy as jnp
from jax import lax
from jax.experimental import pallas as pl
from jax.experimental.pallas import tpu as pltpu
from jax.sharding import PartitionSpec as P

ROUTED_ALL = 256
TOP = 8
QBLK = 128


def dequant(weight, scale):
    row_blocks, col_blocks = scale.shape
    blocks = (
        weight.astype(jnp.float32).reshape(row_blocks, QBLK, col_blocks, QBLK)
        * scale[:, None, :, None]
    )
    return blocks.astype(jnp.bfloat16).reshape(weight.shape)


def route_slots(route_ids, experts, capacity):
    flat = route_ids.reshape(-1)
    onehot = (flat[:, None] == jnp.arange(experts, dtype=jnp.int32)[None, :]).astype(jnp.int32)
    position = jnp.sum((jnp.cumsum(onehot, axis=0) - 1) * onehot, axis=1)
    kept = (flat < experts) & (position < capacity)
    counts = jnp.minimum(jnp.sum(onehot, axis=0), capacity)
    targets = jnp.where(kept, flat * capacity + position, experts * capacity)
    return (targets.reshape(route_ids.shape), counts)


def on_device_any_mesh(
    tokens,
    route_ids,
    route_weights,
    gate_weight,
    gate_scale,
    up_weight,
    up_scale,
    down_weight,
    down_scale,
):
    experts = lax.axis_size("expert")
    capacity = 2 * route_ids.shape[0] * route_ids.shape[1] // ROUTED_ALL
    slot_total = experts * capacity
    targets, counts = route_slots(route_ids, experts, capacity)
    count_column = counts[:, None]
    gate_eff = dequant(gate_weight[0], gate_scale[0])
    up_eff = dequant(up_weight[0], up_scale[0])
    down_eff = dequant(down_weight[0], down_scale[0])
    token_count = route_ids.shape[0]
    source_index = jnp.full((slot_total + 1,), token_count, jnp.int32)
    source_index = source_index.at[targets.reshape(-1)].set(
        jnp.repeat(jnp.arange(token_count, dtype=jnp.int32), TOP)
    )
    source_index = source_index[:slot_total]
    features = lax.all_gather(tokens, "mp", axis=1, tiled=True)
    padded = jnp.concatenate([features, jnp.zeros((1, features.shape[1]), jnp.bfloat16)], axis=0)
    arrived = lax.all_to_all(
        padded[source_index].reshape(experts, capacity, features.shape[1]),
        "expert",
        split_axis=0,
        concat_axis=0,
        tiled=True,
    )
    arrived_counts = lax.all_to_all(count_column, "expert", split_axis=0, concat_axis=0, tiled=True)
    inputs = arrived.reshape(slot_total, features.shape[1])
    gate_proj = jnp.dot(inputs, gate_eff, preferred_element_type=jnp.float32)
    up_proj = jnp.dot(inputs, up_eff, preferred_element_type=jnp.float32)
    hidden = (jax.nn.silu(gate_proj) * up_proj).astype(jnp.bfloat16)
    row_total = jnp.sum(arrived_counts).astype(jnp.float32)
    hessian_rows = lax.dot_general(
        hidden,
        lax.all_gather(hidden, "mp", axis=1, tiled=True),
        (((0,), (0,)), ((), ())),
        preferred_element_type=jnp.float32,
    ) * (2.0 / row_total)
    partial_value = jnp.dot(hidden, down_eff, preferred_element_type=jnp.float32)
    summed = lax.psum_scatter(
        partial_value.astype(jnp.bfloat16), "mp", scatter_dimension=1, tiled=True
    )
    returned = lax.all_to_all(
        summed.reshape(experts, capacity, summed.shape[1]),
        "expert",
        split_axis=0,
        concat_axis=0,
        tiled=True,
    )
    width = returned.shape[2]
    flat_back = jnp.concatenate(
        [returned.reshape(slot_total, width), jnp.zeros((1, width), jnp.bfloat16)], axis=0
    )
    mixed = jnp.zeros((tokens.shape[0], width), jnp.float32)
    for route in range(TOP):
        mixed = mixed + route_weights[:, route : route + 1] * flat_back[targets[:, route]].astype(
            jnp.float32
        )
    return (mixed.astype(jnp.bfloat16), hessian_rows[None])


BOTH = ("expert", "mp")
VMEM = pl.BlockSpec(memory_space=pltpu.VMEM)
SMEM = pl.BlockSpec(memory_space=pltpu.SMEM)
ANY = pl.BlockSpec(memory_space=pl.ANY)
EMPTY = 64.0
F32 = jnp.float32
BF16 = jnp.bfloat16


def swap_cores(value):
    return lax.ppermute(value, "mp", [(m, m ^ 1) for m in range(4)])


def to_chips(value, k):
    pairs = [(4 * z + m, 4 * (z ^ k) + (m ^ 2 * (m & 1))) for z in range(4) for m in range(4)]
    return lax.ppermute(value, BOTH, pairs)


def across(value):
    return lax.ppermute(value, BOTH, [(4 * z + m, 4 * z + (m ^ 2)) for z in range(4) for m in range(4)])


def earlier_kernel(out_ref):
    row, column = (lax.broadcasted_iota(jnp.int32, out_ref.shape, i) for i in range(2))
    out_ref[...] = jnp.where(row < column, 1.0, 0.0).astype(BF16)


def pick(chosen_ref, tokens_ref):
    return jnp.dot(chosen_ref[...], tokens_ref[...], preferred_element_type=F32).astype(BF16)


def route_kernel(capacity, earlier_ref, ids_ref, chosen_ref, count_ref):
    z = lax.axis_index("expert")
    ids = ids_ref[...]
    rows = ids.shape[1]
    live = [jnp.sum(jnp.where(ids == (z ^ k), 1.0, 0.0), axis=0, keepdims=True) for k in range(4)]
    position = jnp.dot(
        jnp.concatenate(live, axis=0).astype(BF16), earlier_ref[...], preferred_element_type=F32
    )
    slot = lax.broadcasted_iota(jnp.int32, (capacity, rows), 0).astype(F32)
    chosen = []
    for k in range(4):
        kept = (live[k] > 0.5) & (position[k : k + 1] == slot)
        chosen.append(jnp.where(kept, 1.0, 0.0))
        total = jnp.minimum(jnp.sum(live[k], axis=1, keepdims=True), float(capacity))
        count_ref[k] = jnp.broadcast_to(total, count_ref.shape[1:]).astype(BF16)
    chosen_ref[...] = jnp.concatenate(chosen, axis=0).astype(BF16)


def own_kernel(chosen_ref, tokens_ref, rows_ref, cross_ref):
    picked = pick(chosen_ref, tokens_ref)
    rows, width = rows_ref.shape[1:]
    rows_ref[...] = picked.reshape(rows_ref.shape)
    cross_ref[:, :width] = picked[:rows]
    cross_ref[:, width:] = jnp.zeros((rows, cross_ref.shape[1] - width), BF16)


def prepare_kernel(
    gate_scale_ref, up_scale_ref, down_scale_ref, ids_ref, weights_ref, chosen_ref, gate_out, up_out, down_out, coef_ref
):
    for scale_ref, out_ref in ((gate_scale_ref, gate_out), (up_scale_ref, up_out), (down_scale_ref, down_out)):
        for at in range(scale_ref.shape[1]):
            for i in range(2):
                out_ref[i : i + 1, at * QBLK : (at + 1) * QBLK] = jnp.full((1, QBLK), scale_ref[i, at], F32)
    z = lax.axis_index("expert")
    slots = chosen_ref.shape[0]
    capacity = slots // 4
    coef = []
    for k in range(4):
        weight = jnp.sum(jnp.where(ids_ref[...] == (z ^ k), weights_ref[...], 0.0), axis=0, keepdims=True)
        coef.append(chosen_ref[k * capacity : (k + 1) * capacity, :].astype(F32) * weight)
    coef = jnp.concatenate(coef, axis=0)
    terms = []
    for _ in range(3):
        terms.append(coef.astype(BF16).astype(F32))
        coef = coef - terms[-1]
    terms.append(jnp.zeros_like(coef))
    coef_ref[...] = jnp.concatenate(terms, axis=0).T.astype(BF16)


def line_up_kernel(chosen_ref, tokens_ref, own_ref, other_ref, *out_refs):
    rows, width = other_ref.shape
    other = pick(chosen_ref, tokens_ref)
    other_ref[...] = other[:rows]
    empty = 1.0 - jnp.sum(chosen_ref[...].astype(F32), axis=1, keepdims=True)
    first = lax.broadcasted_iota(jnp.int32, (rows, QBLK), 1) == 0
    for k, out_ref in enumerate(out_refs, 1):
        at = slice(k * rows, (k + 1) * rows)
        own = own_ref[k]
        mark = jnp.where(first, empty[at] * EMPTY, 0.0)
        out_ref[:, :QBLK] = (own[:, :QBLK].astype(F32) + mark).astype(BF16)
        out_ref[:, QBLK:width] = own[:, QBLK:]
        out_ref[:, width:] = other[at]


def on_core(core):
    return (lax.axis_index("mp") % 2 == core).astype(F32)


def collect_kernel(own_ref, other_ref, count_ref, crossed_ref, swapped_ref, three_ref, two_ref, one_ref, _, out_ref, counts_ref):
    rows, width = crossed_ref.shape[0], out_ref.shape[1] // 2
    zero = on_core(0)
    for own, far_ref, lanes in (
        (own_ref[0], crossed_ref, slice(0, width)),
        (other_ref[...], swapped_ref, slice(width, 2 * width)),
    ):
        value = own.astype(F32) * zero + far_ref[:, :width].astype(F32) * (1.0 - zero)
        out_ref[:rows, lanes] = value.astype(BF16)
    counts_ref[:rows, :] = count_ref[0]
    for k, ref in enumerate((one_ref, two_ref, three_ref), 1):
        at = slice(k * rows, (k + 1) * rows)
        value = ref[:, :QBLK].astype(F32)
        empty = value > 0.5 * EMPTY
        out_ref[at, :QBLK] = jnp.where(empty, 0.0, value).astype(BF16)
        out_ref[at, QBLK:] = ref[:, QBLK:]
        kept = rows - jnp.sum(jnp.where(empty[:, :1], 1.0, 0.0), axis=0, keepdims=True)
        counts_ref[at, :] = jnp.broadcast_to(kept, (rows, QBLK)).astype(BF16)


def shares_in_order():
    m = lax.axis_index("mp")
    first = m ^ (2 * (m % 2))
    return (first, first ^ 1, first ^ 3, first ^ 2)


def project(x, share, weight_ref, scale_ref):
    slots, width = x.shape
    depth = pl.ds(pl.multiple_of(share * width, width), width)
    terms = []
    for i in range(2):
        scaled = x * scale_ref[i : i + 1, depth]
        terms.append(scaled.astype(BF16))
        terms.append((scaled - terms[-1].astype(F32)).astype(BF16))
    out = jnp.dot(jnp.concatenate(terms, axis=0), weight_ref[depth, :], preferred_element_type=F32)
    return jnp.concatenate([out[:slots] + out[slots : 2 * slots], out[2 * slots : 3 * slots] + out[3 * slots :]], axis=0)


def near_kernel(x_ref, gate_ref, up_ref, gate_scale_ref, up_scale_ref, _, gate_out_ref, up_out_ref):
    width = x_ref.shape[1] // 2
    gate, up = 0.0, 0.0
    for part, share in enumerate(shares_in_order()[:2]):
        x = x_ref[:, part * width : (part + 1) * width].astype(F32)
        gate += project(x, share, gate_ref, gate_scale_ref)
        up += project(x, share, up_ref, up_scale_ref)
    gate_out_ref[...] = gate
    up_out_ref[...] = up


def hidden_kernel(
    x_ref,
    near_gate_ref,
    near_up_ref,
    gate_ref,
    up_ref,
    down_ref,
    gate_scale_ref,
    up_scale_ref,
    down_scale_ref,
    send_ref,
    hidden_ref,
):
    shares = shares_in_order()
    slots, half = near_gate_ref.shape[0] // 2, gate_ref.shape[1] // 2
    width = x_ref.shape[1] // 2
    gate, up = near_gate_ref[...], near_up_ref[...]
    for part, share in enumerate(shares[2:]):
        x = x_ref[:, part * width : (part + 1) * width].astype(F32)
        gate += project(x, share, gate_ref, gate_scale_ref)
        up += project(x, share, up_ref, up_scale_ref)
    parts = []
    for i in range(2):
        g = gate[i * slots : (i + 1) * slots, i * half : (i + 1) * half]
        u = up[i * slots : (i + 1) * slots, i * half : (i + 1) * half]
        parts.append((g / (1.0 + jnp.exp(-g)) * u).astype(BF16))
        lanes = slice(i * half, (i + 1) * half)
        hidden_ref[:, lanes] = parts[i]
        send_ref[:, 2 * width + i * half : 2 * width + (i + 1) * half] = parts[i]
    project_down(hidden_ref, shares[2:], down_ref, down_scale_ref, send_ref)


def project_down(hidden_ref, shares, down_ref, scale_ref, out_ref):
    slots, half, width = hidden_ref.shape[0], hidden_ref.shape[1] // 2, down_ref.shape[1] // 4
    parts = (hidden_ref[:, :half], hidden_ref[:, half:])
    none = jnp.zeros_like(parts[0])
    stacked = jnp.concatenate(
        [jnp.concatenate([parts[0], none], axis=1), jnp.concatenate([none, parts[1]], axis=1)], axis=0
    )
    for part, share in enumerate(shares):
        lanes = pl.ds(pl.multiple_of(share * width, width), width)
        both = jnp.dot(stacked, down_ref[:, lanes], preferred_element_type=F32)
        value = both[:slots] * scale_ref[:1, lanes] + both[slots:] * scale_ref[1:, lanes]
        out_ref[:, part * width : (part + 1) * width] = value.astype(BF16)


def keep_kernel(hidden_ref, send_ref, down_ref, down_scale_ref, keep_ref, cross_ref):
    project_down(hidden_ref, shares_in_order()[:2], down_ref, down_scale_ref, keep_ref)
    rows, width = cross_ref.shape[0], down_ref.shape[1] // 4
    zero = on_core(0)
    for part in range(2):
        lanes, turned = slice(part * width, (part + 1) * width), slice((1 - part) * width, (2 - part) * width)
        value = send_ref[:rows, turned].astype(F32) * zero + keep_ref[:rows, lanes].astype(F32) * (1.0 - zero)
        cross_ref[:, lanes] = value.astype(BF16)
    for k in range(4):
        into = 2 * width + k * hidden_ref.shape[1]
        cross_ref[:, into : into + hidden_ref.shape[1]] = hidden_ref[k * rows : (k + 1) * rows, :]


def chip_sum_kernel(keep_ref, sent_ref, *out_refs):
    rows, width = out_refs[0].shape
    for k, out_ref in enumerate(out_refs):
        at = slice(k * rows, (k + 1) * rows)
        out_ref[...] = (keep_ref[at, :].astype(F32) + sent_ref[at, :width].astype(F32)).astype(BF16)


def hessian_factor(count_ref):
    rows = count_ref.shape[0] // 4
    counts = [count_ref[k * rows : k * rows + 1, :].astype(F32)[:, :1] for k in range(4)]
    return 2.0 / (counts[0] + counts[1] + counts[2] + counts[3])


def hessian_kernel(count_ref, own_ref, sent_ref, crossed_ref, out_ref, far_ref, turned_ref):
    m = lax.axis_index("mp")
    width = out_ref.shape[0]
    rows = far_ref.shape[0] // 4
    start = crossed_ref.shape[1] - 4 * width
    for k in range(4):
        far_ref[k * rows : (k + 1) * rows, :] = crossed_ref[:, start + k * width : start + (k + 1) * width]
    factor = hessian_factor(count_ref)
    turned_ref[...] = own_ref[...].astype(F32).T.astype(BF16)
    others = ((m, own_ref[...]), (m ^ 1, sent_ref[:, sent_ref.shape[1] - width :]), (m ^ 2, far_ref[...]))
    for share, other in others:
        block = jnp.dot(turned_ref[...], other, preferred_element_type=F32) * factor
        out_ref[:, pl.ds(pl.multiple_of(share * width, width), width)] = block


def collect_back_kernel(summed_ref, crossed_ref, three_ref, two_ref, one_ref, far_ref, mine_ref, other_ref):
    rows, width = one_ref.shape[0], mine_ref.shape[1]
    crossed = crossed_ref[:, : 2 * width].astype(F32)
    value = (crossed + summed_ref[...].astype(F32) * on_core(0)).astype(BF16)
    for k, rows_in in enumerate((value, one_ref[...], two_ref[...], three_ref[...])):
        mine_ref[k * rows : (k + 1) * rows, :] = rows_in[:, :width]
        other_ref[k * rows : (k + 1) * rows, :width] = rows_in[:, width:]
    other_ref[:, width:] = far_ref[...]


def combine_kernel(
    coef_ref, near_ref, far_ref, count_ref, turned_ref, _, mixed_hbm, hessian_hbm, mixed_ref, block_ref, sems
):
    width, hidden_width = near_ref.shape[1], block_ref.shape[0]
    block = jnp.dot(turned_ref[...], far_ref[:, width:], preferred_element_type=F32)
    block_ref[...] = block * hessian_factor(count_ref)
    share = lax.axis_index("mp") ^ 3
    lanes = pl.ds(pl.multiple_of(share * hidden_width, hidden_width), hidden_width)
    block_copy = pltpu.make_async_copy(block_ref, hessian_hbm.at[:, lanes], sems.at[0])
    block_copy.start()
    result = (near_ref[...].astype(F32) + far_ref[:, :width].astype(F32)).astype(BF16)
    out = jnp.dot(coef_ref[...], jnp.concatenate([result] * 4, axis=0), preferred_element_type=F32)
    mixed_ref[...] = out.astype(BF16)
    mixed_copy = pltpu.make_async_copy(mixed_ref, mixed_hbm, sems.at[1])
    mixed_copy.start()
    block_copy.wait()
    mixed_copy.wait()


def on_device(
    tokens,
    route_ids,
    route_weights,
    gate_weight,
    gate_scale,
    up_weight,
    up_scale,
    down_weight,
    down_scale,
):
    rows, width = tokens.shape
    capacity = 2 * rows * TOP // ROUTED_ALL
    slots = 4 * capacity
    hidden_width = gate_weight.shape[2]
    shape = jax.ShapeDtypeStruct

    def call(kernel, name, outs, args, scalars=0, flops=0):
        single = not isinstance(outs, tuple)
        return pl.pallas_call(
            kernel,
            out_shape=outs,
            in_specs=[SMEM] * scalars + [VMEM] * (len(args) - scalars),
            out_specs=VMEM if single else (VMEM,) * len(outs),
            compiler_params=pltpu.CompilerParams(vmem_limit_bytes=8 * 1024 * 1024),
            cost_estimate=pl.CostEstimate(flops=flops, bytes_accessed=0, transcendentals=0) if flops else None,
            name=name,
        )(*args)

    earlier = call(earlier_kernel, "earlier", shape((rows, rows), BF16), (), flops=4 * 10**9)
    other_tokens = swap_cores(tokens)
    chosen, counts = call(
        functools.partial(route_kernel, capacity),
        "route",
        (shape((slots, rows), BF16), shape((4, capacity, QBLK), BF16)),
        (earlier, route_ids.T),
    )
    picked, cross = call(
        own_kernel,
        "own",
        (shape((4, capacity, width), BF16), shape((capacity, 2 * width + QBLK), BF16)),
        (chosen, tokens),
        flops=10**11,
    )
    crossed = across(cross)
    other, *messages = call(
        line_up_kernel,
        "line_up",
        (shape((capacity, width), BF16), *[shape((capacity, 2 * width), BF16)] * 3),
        (chosen, other_tokens, picked),
    )
    *scales, coef = call(
        prepare_kernel,
        "prepare",
        (*[shape((2, 4 * width), F32)] * 3, shape((rows, 4 * slots), BF16)),
        (gate_scale[0].T, up_scale[0].T, down_scale[0], route_ids.T, route_weights.T, chosen),
        scalars=3,
    )
    gate, up, down = gate_weight[0], up_weight[0], down_weight[0]

    arrived, arrived_counts = call(
        collect_kernel,
        "collect",
        (shape((slots, 2 * width), BF16), shape((slots, QBLK), BF16)),
        (picked, other, counts, crossed, swap_cores(crossed[:, :width]), *[to_chips(messages[k - 1], k) for k in (3, 2, 1)], scales[0]),
    )
    swapped = swap_cores(arrived)
    near = call(
        near_kernel,
        "near",
        (shape((2 * slots, hidden_width), F32),) * 2,
        (arrived, gate, up, *scales[:2], down),
    )
    send, hidden = call(
        hidden_kernel,
        "hidden",
        (
            shape((slots, 2 * width + hidden_width), BF16),
            shape((slots, hidden_width), BF16),
        ),
        (swapped, *near, gate, up, down, *scales),
    )
    sent = swap_cores(send)
    keep, cross = call(
        keep_kernel,
        "keep",
        (shape((slots, 2 * width), BF16), shape((capacity, 2 * width + 4 * hidden_width), BF16)),
        (hidden, send, down, scales[2]),
    )
    crossed = across(cross)
    summed = call(chip_sum_kernel, "chip_sum", (shape((capacity, 2 * width), BF16),) * 4, (keep, sent))
    back = {k: to_chips(summed[k], k) for k in range(1, 4)}
    hessian, far, turned = call(
        hessian_kernel,
        "hessian",
        (
            shape((hidden_width, 4 * hidden_width), F32),
            shape((slots, hidden_width), BF16),
            shape((hidden_width, slots), BF16),
        ),
        (arrived_counts, hidden, sent, crossed),
    )
    mine, other = call(
        collect_back_kernel,
        "collect_back",
        (shape((slots, width), BF16), shape((slots, width + hidden_width), BF16)),
        (summed[0], crossed, *[back[k] for k in (3, 2, 1)], far),
    )
    mixed, hessian = pl.pallas_call(
        combine_kernel,
        out_shape=(shape((rows, width), BF16), shape((hidden_width, 4 * hidden_width), F32)),
        in_specs=[VMEM] * 5 + [ANY],
        out_specs=(ANY, ANY),
        scratch_shapes=[
            pltpu.VMEM((rows, width), BF16),
            pltpu.VMEM((hidden_width, hidden_width), F32),
            pltpu.SemaphoreType.DMA((2,)),
        ],
        input_output_aliases={5: 1},
        compiler_params=pltpu.CompilerParams(vmem_limit_bytes=8 * 1024 * 1024),
        name="combine",
    )(coef, mine, swap_cores(other), arrived_counts, turned, hessian)
    return mixed, hessian[None]


def solution(mesh):
    placed = (
        P(("groups", "expert"), "mp"),
        P(("groups", "expert"), None),
        P(("groups", "expert"), None),
        P("expert", None, "mp"),
        P("expert", None, "mp"),
        P("expert", None, "mp"),
        P("expert", None, "mp"),
        P("expert", "mp", None),
        P("expert", "mp", None),
    )
    two_level = mesh.shape["expert"] == 4 and mesh.shape["mp"] == 4
    return jax.shard_map(
        on_device if two_level else on_device_any_mesh,
        mesh=mesh,
        in_specs=placed,
        out_specs=(P(("groups", "expert"), "mp"), P(("groups", "expert"), "mp", None)),
        check_vma=False,
    )
```

```python
import functools

import jax
import jax.numpy as jnp
from jax import lax
from jax.experimental import pallas as pl
from jax.experimental.pallas import tpu as pltpu
from jax.sharding import PartitionSpec as P

ROUTED_ALL = 256
TOP = 8
QBLK = 128


def dequant(weight, scale):
    row_blocks, col_blocks = scale.shape
    blocks = (
        weight.astype(jnp.float32).reshape(row_blocks, QBLK, col_blocks, QBLK)
        * scale[:, None, :, None]
    )
    return blocks.astype(jnp.bfloat16).reshape(weight.shape)


def route_slots(route_ids, experts, capacity):
    flat = route_ids.reshape(-1)
    onehot = (flat[:, None] == jnp.arange(experts, dtype=jnp.int32)[None, :]).astype(jnp.int32)
    position = jnp.sum((jnp.cumsum(onehot, axis=0) - 1) * onehot, axis=1)
    kept = (flat < experts) & (position < capacity)
    counts = jnp.minimum(jnp.sum(onehot, axis=0), capacity)
    targets = jnp.where(kept, flat * capacity + position, experts * capacity)
    return (targets.reshape(route_ids.shape), counts)


def on_device_any_mesh(
    tokens,
    route_ids,
    route_weights,
    gate_weight,
    gate_scale,
    up_weight,
    up_scale,
    down_weight,
    down_scale,
):
    experts = lax.axis_size("expert")
    capacity = 2 * route_ids.shape[0] * route_ids.shape[1] // ROUTED_ALL
    slot_total = experts * capacity
    targets, counts = route_slots(route_ids, experts, capacity)
    count_column = counts[:, None]
    gate_eff = dequant(gate_weight[0], gate_scale[0])
    up_eff = dequant(up_weight[0], up_scale[0])
    down_eff = dequant(down_weight[0], down_scale[0])
    token_count = route_ids.shape[0]
    source_index = jnp.full((slot_total + 1,), token_count, jnp.int32)
    source_index = source_index.at[targets.reshape(-1)].set(
        jnp.repeat(jnp.arange(token_count, dtype=jnp.int32), TOP)
    )
    source_index = source_index[:slot_total]
    features = lax.all_gather(tokens, "mp", axis=1, tiled=True)
    padded = jnp.concatenate([features, jnp.zeros((1, features.shape[1]), jnp.bfloat16)], axis=0)
    arrived = lax.all_to_all(
        padded[source_index].reshape(experts, capacity, features.shape[1]),
        "expert",
        split_axis=0,
        concat_axis=0,
        tiled=True,
    )
    arrived_counts = lax.all_to_all(count_column, "expert", split_axis=0, concat_axis=0, tiled=True)
    inputs = arrived.reshape(slot_total, features.shape[1])
    gate_proj = jnp.dot(inputs, gate_eff, preferred_element_type=jnp.float32)
    up_proj = jnp.dot(inputs, up_eff, preferred_element_type=jnp.float32)
    hidden = (jax.nn.silu(gate_proj) * up_proj).astype(jnp.bfloat16)
    row_total = jnp.sum(arrived_counts).astype(jnp.float32)
    hessian_rows = lax.dot_general(
        hidden,
        lax.all_gather(hidden, "mp", axis=1, tiled=True),
        (((0,), (0,)), ((), ())),
        preferred_element_type=jnp.float32,
    ) * (2.0 / row_total)
    partial_value = jnp.dot(hidden, down_eff, preferred_element_type=jnp.float32)
    summed = lax.psum_scatter(
        partial_value.astype(jnp.bfloat16), "mp", scatter_dimension=1, tiled=True
    )
    returned = lax.all_to_all(
        summed.reshape(experts, capacity, summed.shape[1]),
        "expert",
        split_axis=0,
        concat_axis=0,
        tiled=True,
    )
    width = returned.shape[2]
    flat_back = jnp.concatenate(
        [returned.reshape(slot_total, width), jnp.zeros((1, width), jnp.bfloat16)], axis=0
    )
    mixed = jnp.zeros((tokens.shape[0], width), jnp.float32)
    for route in range(TOP):
        mixed = mixed + route_weights[:, route : route + 1] * flat_back[targets[:, route]].astype(
            jnp.float32
        )
    return (mixed.astype(jnp.bfloat16), hessian_rows[None])


BOTH = ("expert", "mp")
VMEM = pl.BlockSpec(memory_space=pltpu.VMEM)
SMEM = pl.BlockSpec(memory_space=pltpu.SMEM)
ANY = pl.BlockSpec(memory_space=pl.ANY)
EMPTY = 64.0
F32 = jnp.float32
BF16 = jnp.bfloat16


def swap_cores(value):
    return lax.ppermute(value, "mp", [(m, m ^ 1) for m in range(4)])


def to_chips(value, k):
    pairs = [(4 * z + m, 4 * (z ^ k) + (m ^ 2 * (m & 1))) for z in range(4) for m in range(4)]
    return lax.ppermute(value, BOTH, pairs)


def across(value):
    return lax.ppermute(value, BOTH, [(4 * z + m, 4 * z + (m ^ 2)) for z in range(4) for m in range(4)])


def earlier_kernel(out_ref):
    row, column = (lax.broadcasted_iota(jnp.int32, out_ref.shape, i) for i in range(2))
    out_ref[...] = jnp.where(row < column, 1.0, 0.0).astype(BF16)


def pick(chosen_ref, tokens_ref):
    return jnp.dot(chosen_ref[...], tokens_ref[...], preferred_element_type=F32).astype(BF16)


def route_kernel(capacity, earlier_ref, ids_ref, chosen_ref, count_ref):
    z = lax.axis_index("expert")
    ids = ids_ref[...]
    rows = ids.shape[1]
    live = [jnp.sum(jnp.where(ids == (z ^ k), 1.0, 0.0), axis=0, keepdims=True) for k in range(4)]
    position = jnp.dot(
        jnp.concatenate(live, axis=0).astype(BF16), earlier_ref[...], preferred_element_type=F32
    )
    slot = lax.broadcasted_iota(jnp.int32, (capacity, rows), 0).astype(F32)
    chosen = []
    for k in range(4):
        kept = (live[k] > 0.5) & (position[k : k + 1] == slot)
        chosen.append(jnp.where(kept, 1.0, 0.0))
        total = jnp.minimum(jnp.sum(live[k], axis=1, keepdims=True), float(capacity))
        count_ref[k] = jnp.broadcast_to(total, count_ref.shape[1:]).astype(BF16)
    chosen_ref[...] = jnp.concatenate(chosen, axis=0).astype(BF16)


def own_kernel(chosen_ref, tokens_ref, rows_ref):
    rows_ref[...] = pick(chosen_ref, tokens_ref).reshape(rows_ref.shape)


def prepare_kernel(
    gate_scale_ref, up_scale_ref, down_scale_ref, ids_ref, weights_ref, chosen_ref, gate_out, up_out, down_out, coef_ref
):
    for scale_ref, out_ref in ((gate_scale_ref, gate_out), (up_scale_ref, up_out), (down_scale_ref, down_out)):
        for at in range(scale_ref.shape[1]):
            for i in range(2):
                out_ref[i : i + 1, at * QBLK : (at + 1) * QBLK] = jnp.full((1, QBLK), scale_ref[i, at], F32)
    z = lax.axis_index("expert")
    slots = chosen_ref.shape[0]
    capacity = slots // 4
    coef = []
    for k in range(4):
        weight = jnp.sum(jnp.where(ids_ref[...] == (z ^ k), weights_ref[...], 0.0), axis=0, keepdims=True)
        coef.append(chosen_ref[k * capacity : (k + 1) * capacity, :].astype(F32) * weight)
    coef = jnp.concatenate(coef, axis=0)
    terms = []
    for _ in range(3):
        terms.append(coef.astype(BF16).astype(F32))
        coef = coef - terms[-1]
    terms.append(jnp.zeros_like(coef))
    coef_ref[...] = jnp.concatenate(terms, axis=0).T.astype(BF16)


def line_up_kernel(chosen_ref, tokens_ref, own_ref, *out_refs):
    rows, width = own_ref.shape[1:]
    other = pick(chosen_ref, tokens_ref)
    empty = 1.0 - jnp.sum(chosen_ref[...].astype(F32), axis=1, keepdims=True)
    first = lax.broadcasted_iota(jnp.int32, (rows, QBLK), 1) == 0
    for k, out_ref in enumerate(out_refs):
        at = slice(k * rows, (k + 1) * rows)
        own = own_ref[k]
        out_ref[:, :width] = own
        out_ref[:, width:] = other[at]
        if k:
            mark = jnp.where(first, empty[at] * EMPTY, 0.0)
            out_ref[:, :QBLK] = (own[:, :QBLK].astype(F32) + mark).astype(BF16)


def on_core(core):
    return (lax.axis_index("mp") % 2 == core).astype(F32)


def collect_kernel(own_ref, count_ref, two_ref, three_ref, one_ref, _, out_ref, counts_ref):
    rows, width = own_ref.shape
    out_ref[:rows, :] = (own_ref[...].astype(F32) * on_core(0)).astype(BF16)
    counts_ref[:rows, :] = count_ref[0]
    for k, ref in enumerate((one_ref, two_ref, three_ref), 1):
        at = slice(k * rows, (k + 1) * rows)
        value = ref[:, :QBLK].astype(F32)
        empty = value > 0.5 * EMPTY
        out_ref[at, :QBLK] = jnp.where(empty, 0.0, value).astype(BF16)
        out_ref[at, QBLK:] = ref[:, QBLK:]
        kept = rows - jnp.sum(jnp.where(empty[:, :1], 1.0, 0.0), axis=0, keepdims=True)
        counts_ref[at, :] = jnp.broadcast_to(kept, (rows, QBLK)).astype(BF16)


def filled(x_ref, crossed_ref, part, part_of_crossed, lacks):
    rows, width = crossed_ref.shape[0], crossed_ref.shape[1] // 2
    lanes, lanes_of_crossed = (slice(i * width, (i + 1) * width) for i in (part, part_of_crossed))
    x = x_ref[:, lanes].astype(F32)
    first = x[:rows] + crossed_ref[:, lanes_of_crossed].astype(F32) * lacks
    return jnp.concatenate([first, x[rows:]], axis=0)


def shares_in_order():
    m = lax.axis_index("mp")
    first = m ^ (2 * (m % 2))
    return (first, first ^ 1, first ^ 3, first ^ 2)


def project(x, share, weight_ref, scale_ref):
    slots, width = x.shape
    depth = pl.ds(pl.multiple_of(share * width, width), width)
    terms = []
    for i in range(2):
        scaled = x * scale_ref[i : i + 1, depth]
        terms.append(scaled.astype(BF16))
        terms.append((scaled - terms[-1].astype(F32)).astype(BF16))
    out = jnp.dot(jnp.concatenate(terms, axis=0), weight_ref[depth, :], preferred_element_type=F32)
    return jnp.concatenate([out[:slots] + out[slots : 2 * slots], out[2 * slots : 3 * slots] + out[3 * slots :]], axis=0)


def near_kernel(x_ref, crossed_ref, gate_ref, up_ref, gate_scale_ref, up_scale_ref, _, gate_out_ref, up_out_ref):
    gate, up = 0.0, 0.0
    for part, share in enumerate(shares_in_order()[:2]):
        x = filled(x_ref, crossed_ref, part, part, on_core(1))
        gate += project(x, share, gate_ref, gate_scale_ref)
        up += project(x, share, up_ref, up_scale_ref)
    gate_out_ref[...] = gate
    up_out_ref[...] = up


def hidden_kernel(
    x_ref,
    crossed_ref,
    near_gate_ref,
    near_up_ref,
    gate_ref,
    up_ref,
    down_ref,
    gate_scale_ref,
    up_scale_ref,
    down_scale_ref,
    send_ref,
    hidden_ref,
):
    shares = shares_in_order()
    slots, half = near_gate_ref.shape[0] // 2, gate_ref.shape[1] // 2
    width = x_ref.shape[1] // 2
    gate, up = near_gate_ref[...], near_up_ref[...]
    for part, share in enumerate(shares[2:]):
        x = filled(x_ref, crossed_ref, part, 1 - part, on_core(0))
        gate += project(x, share, gate_ref, gate_scale_ref)
        up += project(x, share, up_ref, up_scale_ref)
    parts = []
    for i in range(2):
        g = gate[i * slots : (i + 1) * slots, i * half : (i + 1) * half]
        u = up[i * slots : (i + 1) * slots, i * half : (i + 1) * half]
        parts.append((g / (1.0 + jnp.exp(-g)) * u).astype(BF16))
        lanes = slice(i * half, (i + 1) * half)
        hidden_ref[:, lanes] = parts[i]
        send_ref[:, 2 * width + i * half : 2 * width + (i + 1) * half] = parts[i]
    project_down(hidden_ref, shares[2:], down_ref, down_scale_ref, send_ref)


def project_down(hidden_ref, shares, down_ref, scale_ref, out_ref):
    slots, half, width = hidden_ref.shape[0], hidden_ref.shape[1] // 2, down_ref.shape[1] // 4
    parts = (hidden_ref[:, :half], hidden_ref[:, half:])
    none = jnp.zeros_like(parts[0])
    stacked = jnp.concatenate(
        [jnp.concatenate([parts[0], none], axis=1), jnp.concatenate([none, parts[1]], axis=1)], axis=0
    )
    for part, share in enumerate(shares):
        lanes = pl.ds(pl.multiple_of(share * width, width), width)
        both = jnp.dot(stacked, down_ref[:, lanes], preferred_element_type=F32)
        value = both[:slots] * scale_ref[:1, lanes] + both[slots:] * scale_ref[1:, lanes]
        out_ref[:, part * width : (part + 1) * width] = value.astype(BF16)


def keep_kernel(hidden_ref, send_ref, down_ref, down_scale_ref, keep_ref, cross_ref):
    project_down(hidden_ref, shares_in_order()[:2], down_ref, down_scale_ref, keep_ref)
    rows, width = cross_ref.shape[0], down_ref.shape[1] // 4
    zero = on_core(0)
    for part in range(2):
        lanes, turned = slice(part * width, (part + 1) * width), slice((1 - part) * width, (2 - part) * width)
        value = send_ref[:rows, turned].astype(F32) * zero + keep_ref[:rows, lanes].astype(F32) * (1.0 - zero)
        cross_ref[:, lanes] = value.astype(BF16)
    for k in range(4):
        into = 2 * width + k * hidden_ref.shape[1]
        cross_ref[:, into : into + hidden_ref.shape[1]] = hidden_ref[k * rows : (k + 1) * rows, :]


def chip_sum_kernel(keep_ref, sent_ref, *out_refs):
    rows, width = out_refs[0].shape
    for k, out_ref in enumerate(out_refs):
        at = slice(k * rows, (k + 1) * rows)
        out_ref[...] = (keep_ref[at, :].astype(F32) + sent_ref[at, :width].astype(F32)).astype(BF16)


def hessian_factor(count_ref):
    rows = count_ref.shape[0] // 4
    counts = [count_ref[k * rows : k * rows + 1, :].astype(F32)[:, :1] for k in range(4)]
    return 2.0 / (counts[0] + counts[1] + counts[2] + counts[3])


def hessian_kernel(count_ref, own_ref, sent_ref, crossed_ref, out_ref, far_ref, turned_ref):
    m = lax.axis_index("mp")
    width = out_ref.shape[0]
    rows = far_ref.shape[0] // 4
    start = crossed_ref.shape[1] - 4 * width
    for k in range(4):
        far_ref[k * rows : (k + 1) * rows, :] = crossed_ref[:, start + k * width : start + (k + 1) * width]
    factor = hessian_factor(count_ref)
    turned_ref[...] = own_ref[...].astype(F32).T.astype(BF16)
    others = ((m, own_ref[...]), (m ^ 1, sent_ref[:, sent_ref.shape[1] - width :]), (m ^ 2, far_ref[...]))
    for share, other in others:
        block = jnp.dot(turned_ref[...], other, preferred_element_type=F32) * factor
        out_ref[:, pl.ds(pl.multiple_of(share * width, width), width)] = block


def collect_back_kernel(summed_ref, crossed_ref, three_ref, one_ref, two_ref, far_ref, mine_ref, other_ref):
    rows, width = one_ref.shape[0], mine_ref.shape[1]
    crossed = crossed_ref[:, : 2 * width].astype(F32)
    value = (crossed + summed_ref[...].astype(F32) * on_core(0)).astype(BF16)
    for k, rows_in in enumerate((value, one_ref[...], two_ref[...], three_ref[...])):
        mine_ref[k * rows : (k + 1) * rows, :] = rows_in[:, :width]
        other_ref[k * rows : (k + 1) * rows, :width] = rows_in[:, width:]
    other_ref[:, width:] = far_ref[...]


def combine_kernel(
    coef_ref, near_ref, far_ref, count_ref, turned_ref, _, mixed_hbm, hessian_hbm, mixed_ref, block_ref, sems
):
    width, hidden_width = near_ref.shape[1], block_ref.shape[0]
    block = jnp.dot(turned_ref[...], far_ref[:, width:], preferred_element_type=F32)
    block_ref[...] = block * hessian_factor(count_ref)
    share = lax.axis_index("mp") ^ 3
    lanes = pl.ds(pl.multiple_of(share * hidden_width, hidden_width), hidden_width)
    block_copy = pltpu.make_async_copy(block_ref, hessian_hbm.at[:, lanes], sems.at[0])
    block_copy.start()
    result = (near_ref[...].astype(F32) + far_ref[:, :width].astype(F32)).astype(BF16)
    out = jnp.dot(coef_ref[...], jnp.concatenate([result] * 4, axis=0), preferred_element_type=F32)
    mixed_ref[...] = out.astype(BF16)
    mixed_copy = pltpu.make_async_copy(mixed_ref, mixed_hbm, sems.at[1])
    mixed_copy.start()
    block_copy.wait()
    mixed_copy.wait()


def on_device(
    tokens,
    route_ids,
    route_weights,
    gate_weight,
    gate_scale,
    up_weight,
    up_scale,
    down_weight,
    down_scale,
):
    rows, width = tokens.shape
    capacity = 2 * rows * TOP // ROUTED_ALL
    slots = 4 * capacity
    hidden_width = gate_weight.shape[2]
    shape = jax.ShapeDtypeStruct

    def call(kernel, name, outs, args, scalars=0, flops=0):
        single = not isinstance(outs, tuple)
        return pl.pallas_call(
            kernel,
            out_shape=outs,
            in_specs=[SMEM] * scalars + [VMEM] * (len(args) - scalars),
            out_specs=VMEM if single else (VMEM,) * len(outs),
            compiler_params=pltpu.CompilerParams(vmem_limit_bytes=8 * 1024 * 1024),
            cost_estimate=pl.CostEstimate(flops=flops, bytes_accessed=0, transcendentals=0) if flops else None,
            name=name,
        )(*args)

    earlier = call(earlier_kernel, "earlier", shape((rows, rows), BF16), (), flops=4 * 10**9)
    other_tokens = swap_cores(tokens)
    chosen, counts = call(
        functools.partial(route_kernel, capacity),
        "route",
        (shape((slots, rows), BF16), shape((4, capacity, QBLK), BF16)),
        (earlier, route_ids.T),
    )
    picked = call(
        own_kernel,
        "own",
        shape((4, capacity, width), BF16),
        (chosen, tokens),
        flops=10**11,
    )
    messages = call(
        line_up_kernel,
        "line_up",
        (shape((capacity, 2 * width), BF16),) * 4,
        (chosen, other_tokens, picked),
    )
    *scales, coef = call(
        prepare_kernel,
        "prepare",
        (*[shape((2, 4 * width), F32)] * 3, shape((rows, 4 * slots), BF16)),
        (gate_scale[0].T, up_scale[0].T, down_scale[0], route_ids.T, route_weights.T, chosen),
        scalars=3,
    )
    gate, up, down = gate_weight[0], up_weight[0], down_weight[0]

    arrived, arrived_counts = call(
        collect_kernel,
        "collect",
        (shape((slots, 2 * width), BF16), shape((slots, QBLK), BF16)),
        (messages[0], counts, *[to_chips(messages[k], k) for k in (2, 3, 1)], scales[0]),
    )
    swapped = swap_cores(arrived)
    crossed = across(messages[0])
    near = call(
        near_kernel,
        "near",
        (shape((2 * slots, hidden_width), F32),) * 2,
        (arrived, crossed, gate, up, *scales[:2], down),
        flops=10**10,
    )
    send, hidden = call(
        hidden_kernel,
        "hidden",
        (
            shape((slots, 2 * width + hidden_width), BF16),
            shape((slots, hidden_width), BF16),
        ),
        (swapped, crossed, *near, gate, up, down, *scales),
    )
    sent = swap_cores(send)
    keep, cross = call(
        keep_kernel,
        "keep",
        (shape((slots, 2 * width), BF16), shape((capacity, 2 * width + 4 * hidden_width), BF16)),
        (hidden, send, down, scales[2]),
    )
    crossed = across(cross)
    summed = call(chip_sum_kernel, "chip_sum", (shape((capacity, 2 * width), BF16),) * 4, (keep, sent))
    back = {k: to_chips(summed[k], k) for k in range(1, 4)}
    hessian, far, turned = call(
        hessian_kernel,
        "hessian",
        (
            shape((hidden_width, 4 * hidden_width), F32),
            shape((slots, hidden_width), BF16),
            shape((hidden_width, slots), BF16),
        ),
        (arrived_counts, hidden, sent, crossed),
    )
    mine, other = call(
        collect_back_kernel,
        "collect_back",
        (shape((slots, width), BF16), shape((slots, width + hidden_width), BF16)),
        (summed[0], crossed, *[back[k] for k in (3, 1, 2)], far),
    )
    mixed, hessian = pl.pallas_call(
        combine_kernel,
        out_shape=(shape((rows, width), BF16), shape((hidden_width, 4 * hidden_width), F32)),
        in_specs=[VMEM] * 5 + [ANY],
        out_specs=(ANY, ANY),
        scratch_shapes=[
            pltpu.VMEM((rows, width), BF16),
            pltpu.VMEM((hidden_width, hidden_width), F32),
            pltpu.SemaphoreType.DMA((2,)),
        ],
        input_output_aliases={5: 1},
        compiler_params=pltpu.CompilerParams(vmem_limit_bytes=8 * 1024 * 1024),
        name="combine",
    )(coef, mine, swap_cores(other), arrived_counts, turned, hessian)
    return mixed, hessian[None]


def solution(mesh):
    placed = (
        P(("groups", "expert"), "mp"),
        P(("groups", "expert"), None),
        P(("groups", "expert"), None),
        P("expert", None, "mp"),
        P("expert", None, "mp"),
        P("expert", None, "mp"),
        P("expert", None, "mp"),
        P("expert", "mp", None),
        P("expert", "mp", None),
    )
    two_level = mesh.shape["expert"] == 4 and mesh.shape["mp"] == 4
    return jax.shard_map(
        on_device if two_level else on_device_any_mesh,
        mesh=mesh,
        in_specs=placed,
        out_specs=(P(("groups", "expert"), "mp"), P(("groups", "expert"), "mp", None)),
        check_vma=False,
    )
```

```python
import functools

import jax
import jax.numpy as jnp
from jax import lax
from jax.experimental import pallas as pl
from jax.experimental.pallas import tpu as pltpu
from jax.sharding import PartitionSpec as P

ROUTED_ALL = 256
TOP = 8
QBLK = 128


def dequant(weight, scale):
    row_blocks, col_blocks = scale.shape
    blocks = (
        weight.astype(jnp.float32).reshape(row_blocks, QBLK, col_blocks, QBLK)
        * scale[:, None, :, None]
    )
    return blocks.astype(jnp.bfloat16).reshape(weight.shape)


def route_slots(route_ids, experts, capacity):
    flat = route_ids.reshape(-1)
    onehot = (flat[:, None] == jnp.arange(experts, dtype=jnp.int32)[None, :]).astype(jnp.int32)
    position = jnp.sum((jnp.cumsum(onehot, axis=0) - 1) * onehot, axis=1)
    kept = (flat < experts) & (position < capacity)
    counts = jnp.minimum(jnp.sum(onehot, axis=0), capacity)
    targets = jnp.where(kept, flat * capacity + position, experts * capacity)
    return (targets.reshape(route_ids.shape), counts)


def on_device_any_mesh(
    tokens,
    route_ids,
    route_weights,
    gate_weight,
    gate_scale,
    up_weight,
    up_scale,
    down_weight,
    down_scale,
):
    experts = lax.axis_size("expert")
    capacity = 2 * route_ids.shape[0] * route_ids.shape[1] // ROUTED_ALL
    slot_total = experts * capacity
    targets, counts = route_slots(route_ids, experts, capacity)
    count_column = counts[:, None]
    gate_eff = dequant(gate_weight[0], gate_scale[0])
    up_eff = dequant(up_weight[0], up_scale[0])
    down_eff = dequant(down_weight[0], down_scale[0])
    token_count = route_ids.shape[0]
    source_index = jnp.full((slot_total + 1,), token_count, jnp.int32)
    source_index = source_index.at[targets.reshape(-1)].set(
        jnp.repeat(jnp.arange(token_count, dtype=jnp.int32), TOP)
    )
    source_index = source_index[:slot_total]
    features = lax.all_gather(tokens, "mp", axis=1, tiled=True)
    padded = jnp.concatenate([features, jnp.zeros((1, features.shape[1]), jnp.bfloat16)], axis=0)
    arrived = lax.all_to_all(
        padded[source_index].reshape(experts, capacity, features.shape[1]),
        "expert",
        split_axis=0,
        concat_axis=0,
        tiled=True,
    )
    arrived_counts = lax.all_to_all(count_column, "expert", split_axis=0, concat_axis=0, tiled=True)
    inputs = arrived.reshape(slot_total, features.shape[1])
    gate_proj = jnp.dot(inputs, gate_eff, preferred_element_type=jnp.float32)
    up_proj = jnp.dot(inputs, up_eff, preferred_element_type=jnp.float32)
    hidden = (jax.nn.silu(gate_proj) * up_proj).astype(jnp.bfloat16)
    row_total = jnp.sum(arrived_counts).astype(jnp.float32)
    hessian_rows = lax.dot_general(
        hidden,
        lax.all_gather(hidden, "mp", axis=1, tiled=True),
        (((0,), (0,)), ((), ())),
        preferred_element_type=jnp.float32,
    ) * (2.0 / row_total)
    partial_value = jnp.dot(hidden, down_eff, preferred_element_type=jnp.float32)
    summed = lax.psum_scatter(
        partial_value.astype(jnp.bfloat16), "mp", scatter_dimension=1, tiled=True
    )
    returned = lax.all_to_all(
        summed.reshape(experts, capacity, summed.shape[1]),
        "expert",
        split_axis=0,
        concat_axis=0,
        tiled=True,
    )
    width = returned.shape[2]
    flat_back = jnp.concatenate(
        [returned.reshape(slot_total, width), jnp.zeros((1, width), jnp.bfloat16)], axis=0
    )
    mixed = jnp.zeros((tokens.shape[0], width), jnp.float32)
    for route in range(TOP):
        mixed = mixed + route_weights[:, route : route + 1] * flat_back[targets[:, route]].astype(
            jnp.float32
        )
    return (mixed.astype(jnp.bfloat16), hessian_rows[None])


BOTH = ("expert", "mp")
VMEM = pl.BlockSpec(memory_space=pltpu.VMEM)
SMEM = pl.BlockSpec(memory_space=pltpu.SMEM)
ANY = pl.BlockSpec(memory_space=pl.ANY)
EMPTY = 64.0
F32 = jnp.float32
BF16 = jnp.bfloat16


def swap_cores(value):
    return lax.ppermute(value, "mp", [(m, m ^ 1) for m in range(4)])


def to_chips(value, k):
    pairs = [(4 * z + m, 4 * (z ^ k) + (m ^ 2 * (m & 1))) for z in range(4) for m in range(4)]
    return lax.ppermute(value, BOTH, pairs)


def across(value):
    return lax.ppermute(value, BOTH, [(4 * z + m, 4 * z + (m ^ 2)) for z in range(4) for m in range(4)])


def earlier_kernel(out_ref):
    row, column = (lax.broadcasted_iota(jnp.int32, out_ref.shape, i) for i in range(2))
    out_ref[...] = jnp.where(row < column, 1.0, 0.0).astype(BF16)


def pick(chosen_ref, tokens_ref):
    return jnp.dot(chosen_ref[...], tokens_ref[...], preferred_element_type=F32).astype(BF16)


def route_kernel(capacity, earlier_ref, ids_ref, chosen_ref, count_ref):
    z = lax.axis_index("expert")
    ids = ids_ref[...]
    rows = ids.shape[1]
    live = [jnp.sum(jnp.where(ids == (z ^ k), 1.0, 0.0), axis=0, keepdims=True) for k in range(4)]
    position = jnp.dot(
        jnp.concatenate(live, axis=0).astype(BF16), earlier_ref[...], preferred_element_type=F32
    )
    slot = lax.broadcasted_iota(jnp.int32, (capacity, rows), 0).astype(F32)
    chosen = []
    for k in range(4):
        kept = (live[k] > 0.5) & (position[k : k + 1] == slot)
        chosen.append(jnp.where(kept, 1.0, 0.0))
        total = jnp.minimum(jnp.sum(live[k], axis=1, keepdims=True), float(capacity))
        count_ref[k] = jnp.broadcast_to(total, count_ref.shape[1:]).astype(BF16)
    chosen_ref[...] = jnp.concatenate(chosen, axis=0).astype(BF16)


def own_kernel(chosen_ref, tokens_ref, rows_ref):
    rows_ref[...] = pick(chosen_ref, tokens_ref).reshape(rows_ref.shape)


def prepare_kernel(
    gate_scale_ref, up_scale_ref, down_scale_ref, ids_ref, weights_ref, chosen_ref, gate_out, up_out, down_out, coef_ref
):
    for scale_ref, out_ref in ((gate_scale_ref, gate_out), (up_scale_ref, up_out), (down_scale_ref, down_out)):
        for at in range(scale_ref.shape[1]):
            for i in range(2):
                out_ref[i : i + 1, at * QBLK : (at + 1) * QBLK] = jnp.full((1, QBLK), scale_ref[i, at], F32)
    z = lax.axis_index("expert")
    slots = chosen_ref.shape[0]
    capacity = slots // 4
    coef = []
    for k in range(4):
        weight = jnp.sum(jnp.where(ids_ref[...] == (z ^ k), weights_ref[...], 0.0), axis=0, keepdims=True)
        coef.append(chosen_ref[k * capacity : (k + 1) * capacity, :].astype(F32) * weight)
    coef = jnp.concatenate(coef, axis=0)
    terms = []
    for _ in range(3):
        terms.append(coef.astype(BF16).astype(F32))
        coef = coef - terms[-1]
    terms.append(jnp.zeros_like(coef))
    coef_ref[...] = jnp.concatenate(terms, axis=0).T.astype(BF16)


def line_up_kernel(chosen_ref, tokens_ref, own_ref, *out_refs):
    rows, width = own_ref.shape[1:]
    other = pick(chosen_ref, tokens_ref)
    empty = 1.0 - jnp.sum(chosen_ref[...].astype(F32), axis=1, keepdims=True)
    first = lax.broadcasted_iota(jnp.int32, (rows, QBLK), 1) == 0
    for k, out_ref in enumerate(out_refs):
        at = slice(k * rows, (k + 1) * rows)
        own = own_ref[k]
        out_ref[:, :width] = own
        out_ref[:, width:] = other[at]
        if k:
            mark = jnp.where(first, empty[at] * EMPTY, 0.0)
            out_ref[:, :QBLK] = (own[:, :QBLK].astype(F32) + mark).astype(BF16)


def on_core(core):
    return (lax.axis_index("mp") % 2 == core).astype(F32)


def collect_kernel(own_ref, count_ref, two_ref, three_ref, one_ref, _, out_ref, counts_ref):
    rows, width = own_ref.shape
    out_ref[:rows, :] = (own_ref[...].astype(F32) * on_core(0)).astype(BF16)
    counts_ref[:rows, :] = count_ref[0]
    for k, ref in enumerate((one_ref, two_ref, three_ref), 1):
        at = slice(k * rows, (k + 1) * rows)
        value = ref[:, :QBLK].astype(F32)
        empty = value > 0.5 * EMPTY
        out_ref[at, :QBLK] = jnp.where(empty, 0.0, value).astype(BF16)
        out_ref[at, QBLK:] = ref[:, QBLK:]
        kept = rows - jnp.sum(jnp.where(empty[:, :1], 1.0, 0.0), axis=0, keepdims=True)
        counts_ref[at, :] = jnp.broadcast_to(kept, (rows, QBLK)).astype(BF16)


def filled(x_ref, crossed_ref, part, part_of_crossed, lacks):
    rows, width = crossed_ref.shape[0], crossed_ref.shape[1] // 2
    lanes, lanes_of_crossed = (slice(i * width, (i + 1) * width) for i in (part, part_of_crossed))
    x = x_ref[:, lanes].astype(F32)
    first = x[:rows] + crossed_ref[:, lanes_of_crossed].astype(F32) * lacks
    return jnp.concatenate([first, x[rows:]], axis=0)


def shares_in_order():
    m = lax.axis_index("mp")
    first = m ^ (2 * (m % 2))
    return (first, first ^ 1, first ^ 3, first ^ 2)


def project(x, share, weight_ref, scale_ref):
    slots, width = x.shape
    depth = pl.ds(pl.multiple_of(share * width, width), width)
    terms = []
    for i in range(2):
        scaled = x * scale_ref[i : i + 1, depth]
        terms.append(scaled.astype(BF16))
        terms.append((scaled - terms[-1].astype(F32)).astype(BF16))
    out = jnp.dot(jnp.concatenate(terms, axis=0), weight_ref[depth, :], preferred_element_type=F32)
    return jnp.concatenate([out[:slots] + out[slots : 2 * slots], out[2 * slots : 3 * slots] + out[3 * slots :]], axis=0)


def near_kernel(x_ref, crossed_ref, gate_ref, up_ref, gate_scale_ref, up_scale_ref, _, gate_out_ref, up_out_ref):
    gate, up = 0.0, 0.0
    for part, share in enumerate(shares_in_order()[:2]):
        x = filled(x_ref, crossed_ref, part, part, on_core(1))
        gate += project(x, share, gate_ref, gate_scale_ref)
        up += project(x, share, up_ref, up_scale_ref)
    gate_out_ref[...] = gate
    up_out_ref[...] = up


def hidden_kernel(
    x_ref,
    crossed_ref,
    near_gate_ref,
    near_up_ref,
    gate_ref,
    up_ref,
    down_ref,
    gate_scale_ref,
    up_scale_ref,
    down_scale_ref,
    send_ref,
    hidden_ref,
):
    shares = shares_in_order()
    slots, half = near_gate_ref.shape[0] // 2, gate_ref.shape[1] // 2
    width = x_ref.shape[1] // 2
    gate, up = near_gate_ref[...], near_up_ref[...]
    for part, share in enumerate(shares[2:]):
        x = filled(x_ref, crossed_ref, part, 1 - part, on_core(0))
        gate += project(x, share, gate_ref, gate_scale_ref)
        up += project(x, share, up_ref, up_scale_ref)
    parts = []
    for i in range(2):
        g = gate[i * slots : (i + 1) * slots, i * half : (i + 1) * half]
        u = up[i * slots : (i + 1) * slots, i * half : (i + 1) * half]
        parts.append((g / (1.0 + jnp.exp(-g)) * u).astype(BF16))
        lanes = slice(i * half, (i + 1) * half)
        hidden_ref[:, lanes] = parts[i]
        send_ref[:, 2 * width + i * half : 2 * width + (i + 1) * half] = parts[i]
    project_down(hidden_ref, shares[2:], down_ref, down_scale_ref, send_ref)


def project_down(hidden_ref, shares, down_ref, scale_ref, out_ref):
    half, width = hidden_ref.shape[1] // 2, down_ref.shape[1] // 4
    parts = (hidden_ref[:, :half], hidden_ref[:, half:])
    for part, share in enumerate(shares):
        lanes = pl.ds(pl.multiple_of(share * width, width), width)
        upper = jnp.dot(parts[0], down_ref[:half, lanes], preferred_element_type=F32)
        lower = jnp.dot(parts[1], down_ref[half:, lanes], preferred_element_type=F32)
        value = upper * scale_ref[:1, lanes] + lower * scale_ref[1:, lanes]
        out_ref[:, part * width : (part + 1) * width] = value.astype(BF16)


def keep_kernel(hidden_ref, send_ref, down_ref, down_scale_ref, keep_ref, cross_ref):
    project_down(hidden_ref, shares_in_order()[:2], down_ref, down_scale_ref, keep_ref)
    rows, width = cross_ref.shape[0], down_ref.shape[1] // 4
    zero = on_core(0)
    for part in range(2):
        lanes, turned = slice(part * width, (part + 1) * width), slice((1 - part) * width, (2 - part) * width)
        value = send_ref[:rows, turned].astype(F32) * zero + keep_ref[:rows, lanes].astype(F32) * (1.0 - zero)
        cross_ref[:, lanes] = value.astype(BF16)
    for k in range(4):
        into = 2 * width + k * hidden_ref.shape[1]
        cross_ref[:, into : into + hidden_ref.shape[1]] = hidden_ref[k * rows : (k + 1) * rows, :]


def chip_sum_kernel(keep_ref, sent_ref, *out_refs):
    rows, width = out_refs[0].shape
    for k, out_ref in enumerate(out_refs):
        at = slice(k * rows, (k + 1) * rows)
        out_ref[...] = (keep_ref[at, :].astype(F32) + sent_ref[at, :width].astype(F32)).astype(BF16)


def hessian_factor(count_ref):
    rows = count_ref.shape[0] // 4
    counts = [count_ref[k * rows : k * rows + 1, :].astype(F32)[:, :1] for k in range(4)]
    return 2.0 / (counts[0] + counts[1] + counts[2] + counts[3])


def hessian_kernel(count_ref, own_ref, sent_ref, crossed_ref, out_ref, far_ref, turned_ref):
    m = lax.axis_index("mp")
    width = out_ref.shape[0]
    rows = far_ref.shape[0] // 4
    start = crossed_ref.shape[1] - 4 * width
    for k in range(4):
        far_ref[k * rows : (k + 1) * rows, :] = crossed_ref[:, start + k * width : start + (k + 1) * width]
    factor = hessian_factor(count_ref)
    turned_ref[...] = own_ref[...].astype(F32).T.astype(BF16)
    others = ((m, own_ref[...]), (m ^ 1, sent_ref[:, sent_ref.shape[1] - width :]), (m ^ 2, far_ref[...]))
    for share, other in others:
        block = jnp.dot(turned_ref[...], other, preferred_element_type=F32) * factor
        out_ref[:, pl.ds(pl.multiple_of(share * width, width), width)] = block


def collect_back_kernel(summed_ref, crossed_ref, three_ref, one_ref, two_ref, far_ref, mine_ref, other_ref):
    rows, width = one_ref.shape[0], mine_ref.shape[1]
    crossed = crossed_ref[:, : 2 * width].astype(F32)
    value = (crossed + summed_ref[...].astype(F32) * on_core(0)).astype(BF16)
    for k, rows_in in enumerate((value, one_ref[...], two_ref[...], three_ref[...])):
        mine_ref[k * rows : (k + 1) * rows, :] = rows_in[:, :width]
        other_ref[k * rows : (k + 1) * rows, :width] = rows_in[:, width:]
    other_ref[:, width:] = far_ref[...]


def combine_kernel(
    coef_ref, near_ref, far_ref, count_ref, turned_ref, _, mixed_hbm, hessian_hbm, mixed_ref, block_ref, sems
):
    width, hidden_width = near_ref.shape[1], block_ref.shape[0]
    block = jnp.dot(turned_ref[...], far_ref[:, width:], preferred_element_type=F32)
    block_ref[...] = block * hessian_factor(count_ref)
    share = lax.axis_index("mp") ^ 3
    lanes = pl.ds(pl.multiple_of(share * hidden_width, hidden_width), hidden_width)
    block_copy = pltpu.make_async_copy(block_ref, hessian_hbm.at[:, lanes], sems.at[0])
    block_copy.start()
    result = (near_ref[...].astype(F32) + far_ref[:, :width].astype(F32)).astype(BF16)
    out = jnp.dot(coef_ref[...], jnp.concatenate([result] * 4, axis=0), preferred_element_type=F32)
    mixed_ref[...] = out.astype(BF16)
    mixed_copy = pltpu.make_async_copy(mixed_ref, mixed_hbm, sems.at[1])
    mixed_copy.start()
    block_copy.wait()
    mixed_copy.wait()


def on_device(
    tokens,
    route_ids,
    route_weights,
    gate_weight,
    gate_scale,
    up_weight,
    up_scale,
    down_weight,
    down_scale,
):
    rows, width = tokens.shape
    capacity = 2 * rows * TOP // ROUTED_ALL
    slots = 4 * capacity
    hidden_width = gate_weight.shape[2]
    shape = jax.ShapeDtypeStruct

    def call(kernel, name, outs, args, scalars=0, flops=0):
        single = not isinstance(outs, tuple)
        return pl.pallas_call(
            kernel,
            out_shape=outs,
            in_specs=[SMEM] * scalars + [VMEM] * (len(args) - scalars),
            out_specs=VMEM if single else (VMEM,) * len(outs),
            compiler_params=pltpu.CompilerParams(vmem_limit_bytes=8 * 1024 * 1024),
            cost_estimate=pl.CostEstimate(flops=flops, bytes_accessed=0, transcendentals=0) if flops else None,
            name=name,
        )(*args)

    earlier = call(earlier_kernel, "earlier", shape((rows, rows), BF16), (), flops=4 * 10**9)
    other_tokens = swap_cores(tokens)
    chosen, counts = call(
        functools.partial(route_kernel, capacity),
        "route",
        (shape((slots, rows), BF16), shape((4, capacity, QBLK), BF16)),
        (earlier, route_ids.T),
    )
    picked = call(
        own_kernel,
        "own",
        shape((4, capacity, width), BF16),
        (chosen, tokens),
        flops=10**11,
    )
    messages = call(
        line_up_kernel,
        "line_up",
        (shape((capacity, 2 * width), BF16),) * 4,
        (chosen, other_tokens, picked),
    )
    *scales, coef = call(
        prepare_kernel,
        "prepare",
        (*[shape((2, 4 * width), F32)] * 3, shape((rows, 4 * slots), BF16)),
        (gate_scale[0].T, up_scale[0].T, down_scale[0], route_ids.T, route_weights.T, chosen),
        scalars=3,
    )
    gate, up, down = gate_weight[0], up_weight[0], down_weight[0]

    arrived, arrived_counts = call(
        collect_kernel,
        "collect",
        (shape((slots, 2 * width), BF16), shape((slots, QBLK), BF16)),
        (messages[0], counts, *[to_chips(messages[k], k) for k in (2, 3, 1)], scales[0]),
    )
    swapped = swap_cores(arrived)
    crossed = across(messages[0])
    near = call(
        near_kernel,
        "near",
        (shape((2 * slots, hidden_width), F32),) * 2,
        (arrived, crossed, gate, up, *scales[:2], down),
        flops=10**10,
    )
    send, hidden = call(
        hidden_kernel,
        "hidden",
        (
            shape((slots, 2 * width + hidden_width), BF16),
            shape((slots, hidden_width), BF16),
        ),
        (swapped, crossed, *near, gate, up, down, *scales),
    )
    sent = swap_cores(send)
    keep, cross = call(
        keep_kernel,
        "keep",
        (shape((slots, 2 * width), BF16), shape((capacity, 2 * width + 4 * hidden_width), BF16)),
        (hidden, send, down, scales[2]),
    )
    crossed = across(cross)
    summed = call(chip_sum_kernel, "chip_sum", (shape((capacity, 2 * width), BF16),) * 4, (keep, sent))
    back = {k: to_chips(summed[k], k) for k in range(1, 4)}
    hessian, far, turned = call(
        hessian_kernel,
        "hessian",
        (
            shape((hidden_width, 4 * hidden_width), F32),
            shape((slots, hidden_width), BF16),
            shape((hidden_width, slots), BF16),
        ),
        (arrived_counts, hidden, sent, crossed),
    )
    mine, other = call(
        collect_back_kernel,
        "collect_back",
        (shape((slots, width), BF16), shape((slots, width + hidden_width), BF16)),
        (summed[0], crossed, *[back[k] for k in (3, 1, 2)], far),
    )
    mixed, hessian = pl.pallas_call(
        combine_kernel,
        out_shape=(shape((rows, width), BF16), shape((hidden_width, 4 * hidden_width), F32)),
        in_specs=[VMEM] * 5 + [ANY],
        out_specs=(ANY, ANY),
        scratch_shapes=[
            pltpu.VMEM((rows, width), BF16),
            pltpu.VMEM((hidden_width, hidden_width), F32),
            pltpu.SemaphoreType.DMA((2,)),
        ],
        input_output_aliases={5: 1},
        compiler_params=pltpu.CompilerParams(vmem_limit_bytes=8 * 1024 * 1024),
        name="combine",
    )(coef, mine, swap_cores(other), arrived_counts, turned, hessian)
    return mixed, hessian[None]


def solution(mesh):
    placed = (
        P(("groups", "expert"), "mp"),
        P(("groups", "expert"), None),
        P(("groups", "expert"), None),
        P("expert", None, "mp"),
        P("expert", None, "mp"),
        P("expert", None, "mp"),
        P("expert", None, "mp"),
        P("expert", "mp", None),
        P("expert", "mp", None),
    )
    two_level = mesh.shape["expert"] == 4 and mesh.shape["mp"] == 4
    return jax.shard_map(
        on_device if two_level else on_device_any_mesh,
        mesh=mesh,
        in_specs=placed,
        out_specs=(P(("groups", "expert"), "mp"), P(("groups", "expert"), "mp", None)),
        check_vma=False,
    )
```
